32 devices in a mesh: grp: 2 (over y), row: 4 (over z), col: 2 (over x), rep: 2 (over core).
Axes of the slice: x: 2, y: 2, z: 4, core: 2. Of those that a mesh axis runs over, the one named last changes fastest.
Arguments:
- h_strips: bfloat16 [64, 64, 1024], P(('grp', 'row')), parts along dimension 0, may hold values from -0.1875 to 0.1875
- h_slots: int32 [64, 16], P(('grp', 'row')), parts along dimension 0, may hold values from 0 to 23, all different within a row
- t_prev: float32 [4096, 2048], P(('grp', 'row'), ('col', 'rep')), parts along dimension 0, may hold values from -6 to 6
- t_now: float32 [4096, 2048], P(('grp', 'row'), ('col', 'rep')), parts along dimension 0, may hold values from -6 to 6
- t_mask: int32 [64, 32], P(('grp', 'row'), ('col', 'rep')), parts along dimension 0, may hold values 0 or 1
- coeffs: float32 [2], replicated, may hold values from 0.5 to 1.5
Outputs:
- t_mid: float32 [4096, 2048], P(('grp', 'row'), ('col', 'rep')), parts along dimension 0
- t_next: float32 [4096, 2048], P(('grp', 'row'), ('col', 'rep')), parts along dimension 0
- density: float32 [4096, 2048], P(('grp', 'row'), ('col', 'rep')), parts along dimension 0
The draws below stay inside these ranges and needn't reach their ends.
There are 2 independent parts, one for each index of `grp`. The reference program is written for one: setup_inputs(seed, part) draws one part's arguments, and reference() takes and returns one part's arrays. A program takes and returns all parts, laid end to end along the dimension named above; an argument that names none is the same for every part. Nothing has to cross between parts.
Inputs may be any that keep to these rules, and one draw needn't show every extreme that they name: `h_slots`: in each block row the 16 values are distinct.
All inputs are finite; a program needn't handle non-finite values. No bound on the sum of `t_mask` on one device may be relied on, other than what follows from the above.
Results may differ from the reference program's by a relative error of at most 0.0037.
Values may be sent and summed in bfloat16 or wider, within the bound.
No kernel may reach another device: no remote copies, remote signals or barrier semaphores. Data moves between devices by JAX's collectives and lax.ppermute only.
A program may use at most 64 MiB of HBM per device.

```python
import jax
import jax.numpy as jnp
from jax import lax

B = 64
RB = 8
K = 16
NB = 32
NCB = 32
N = 2048
PT = 2048
N_ROW = 4


def plant(drawn, rng, low, high):
    dims = drawn.shape
    index_at = [jax.random.randint(jax.random.fold_in(rng, axis), (), 0, dims[axis]) for axis in range(len(dims))]
    drawn = drawn.at[tuple(index_at)].set(low)
    longest = dims.index(max(dims))
    index_at[longest] = (index_at[longest] + 1) % dims[longest]
    return drawn.at[tuple(index_at)].set(high)


def shard_levels(rng, dims, cuts, low, top_value):
    factor_of, own = 1.0, jax.random.fold_in(rng, 6)
    for position, parts in cuts:
        heights = jnp.exp(jax.random.uniform(jax.random.fold_in(own, position), (parts,), jnp.float32, low / len(cuts), top_value / len(cuts)))
        factor_of = factor_of * jnp.repeat(heights, dims[position] // parts).reshape([-1 if axis == position else 1 for axis in range(len(dims))])
    return factor_of


def choose_distinct(own_key, rows, count, top, lift):
    sequence = jax.random.permutation(jax.random.fold_in(own_key, 1), count)
    boost = sequence
    for power in range(3):
        boost = boost * boost // count
    boost = boost * lift // count
    tickets = jax.random.randint(jax.random.fold_in(own_key, 2), (rows, count), 0, 4096) + boost
    fixed_rows = jax.random.permutation(jax.random.fold_in(own_key, 3), rows)[jnp.arange(count) % rows]
    tickets = jnp.where(jnp.arange(rows)[:, None] == fixed_rows[None, :], 1 << 14, tickets)
    merit = tickets * count + jnp.arange(count)
    return lax.top_k(merit.astype(jnp.int32), top)[1].astype(jnp.int32)


def gaussian(own_key, extent, width, reach, cuts=(), kind=jnp.bfloat16):
    drawn = jax.random.normal(own_key, extent, jnp.float32) * width
    if len(cuts) > 0:
        drawn = shard_levels(own_key, extent, cuts, -0.22, 0.18) * drawn
    return jnp.clip(drawn, min=-reach, max=reach).astype(kind)


def setup_inputs(seed: int = 0, part: int = 0) -> dict:
    streams_of = jax.random.split(jax.random.key(seed), 7)
    own_keys = jax.random.split(jax.random.fold_in(streams_of[6], part), 7)
    h_strips = gaussian(own_keys[0], (NB, B, K * B), (K * B) ** -0.5, 0.1875, ((0, 4),))
    h_slots = choose_distinct(own_keys[1], NB, 3 * RB, K, 0)
    t_prev = gaussian(own_keys[2], (N, PT), 1.0, 6.0, ((0, 4), (1, 4)), jnp.float32)
    t_now = gaussian(own_keys[3], (N, PT), 1.0, 6.0, ((0, 4), (1, 4)), jnp.float32)
    t_mask = plant((jax.random.randint(own_keys[4], (NB, NCB), 0, 4) < 3).astype(jnp.int32), jax.random.fold_in(own_keys[4], 1), 0, 1)
    coeffs = jnp.clip(jax.random.uniform(streams_of[5], (2,), jnp.float32, 0.5, 1.5), 0.5, 1.5)
    return dict(h_strips=h_strips, h_slots=h_slots, t_prev=t_prev, t_now=t_now, t_mask=t_mask, coeffs=coeffs)


def reference(h_strips, h_slots, t_prev, t_now, t_mask, coeffs):
    block_rows = jnp.arange(NB, dtype=jnp.int32)
    owners = block_rows // RB
    offsets = h_slots // RB - 1
    targets = (((owners[:, None] + offsets) % N_ROW) * RB + h_slots % RB).astype(jnp.int32)
    keep = jnp.repeat(jnp.repeat(t_mask.astype(jnp.float32), B, axis=0), B, axis=1)

    def apply(current):
        blocks = current.astype(jnp.bfloat16).reshape(NB, B, PT)

        def one_row(pair):
            strip, where = pair
            pieces = blocks[where].reshape(K * B, PT)
            return jnp.dot(strip, pieces, preferred_element_type=jnp.float32)

        return lax.map(one_row, (h_strips, targets)).reshape(N, PT)

    t_mid = keep * (2.0 * apply(t_now) - t_prev)
    t_next = keep * (2.0 * apply(t_mid) - t_now)
    density = coeffs[0] * t_mid + coeffs[1] * t_next
    return t_mid, t_next, density
```

```python
import functools

import jax
import jax.numpy as jnp
from jax import lax
from jax.experimental import pallas as pl
from jax.experimental.pallas import tpu as pltpu
from jax.sharding import PartitionSpec as P

PARTS = 2
LANES = 128
VMEM_LIMIT = 32 * 1024 * 1024


def from_behind(block, axis, distance):
    devices = range(lax.axis_size(axis))
    route = [((i - distance) % len(devices), i) for i in devices]
    return lax.ppermute(block, axis, route)


def params():
    return pltpu.CompilerParams(vmem_limit_bytes=VMEM_LIMIT)


def round_kernel(now_ref, out_ref):
    out_ref[...] = now_ref[...].astype(jnp.bfloat16)


def rounded_part(now, part, width):
    rows = now.shape[0]
    tile = rows // 2
    return pl.pallas_call(
        round_kernel,
        grid=(rows // tile,),
        in_specs=[pl.BlockSpec((tile, width), lambda r: (r, part))],
        out_specs=pl.BlockSpec((tile, width), lambda r: (r, 0)),
        out_shape=jax.ShapeDtypeStruct((rows, width), jnp.bfloat16),
        compiler_params=params(),
        cost_estimate=pl.CostEstimate(flops=rows * width, transcendentals=0, bytes_accessed=6 * rows * width),
        name="round_part",
    )(now)


def band_kernel(slots_ref, strips_ref, out_ref):
    row = pl.program_id(0)
    block, slot_lanes = strips_ref.shape[1], strips_ref.shape[2]
    out_ref[...] = jnp.zeros_like(out_ref)
    half = lax.broadcasted_iota(jnp.int32, (block, LANES), 1) // block
    for pair in range(slot_lanes // LANES):
        straight = strips_ref[0, :, pair * LANES:(pair + 1) * LANES].astype(jnp.float32)
        swapped = jnp.concatenate([straight[:, block:], straight[:, :block]], axis=1)
        for side in range(2):
            target = slots_ref[row, 2 * pair + side]
            odd = target % 2
            value = jnp.where(odd == side, straight, swapped)
            value = jnp.where(half == odd, value, 0.0).astype(jnp.bfloat16)
            lanes = pl.ds(pl.multiple_of((target // 2) * LANES, LANES), LANES)
            out_ref[:, lanes] += value


def banded(h_slots, h_strips):
    block_rows, block, slot_lanes = h_strips.shape
    columns = 3 * block_rows * block
    return pl.pallas_call(
        band_kernel,
        grid=(block_rows,),
        in_specs=[
            pl.BlockSpec(memory_space=pltpu.SMEM),
            pl.BlockSpec((1, block, slot_lanes), lambda r: (r, 0, 0)),
        ],
        out_specs=pl.BlockSpec((block, columns), lambda r: (r, 0)),
        out_shape=jax.ShapeDtypeStruct((block_rows * block, columns), jnp.bfloat16),
        compiler_params=params(),
        cost_estimate=pl.CostEstimate(
            flops=8 * block_rows * block * columns, transcendentals=0,
            bytes_accessed=2 * block_rows * block * (columns + slot_lanes)),
        name="band",
    )(h_slots, h_strips)


def product(band_ref, below_ref, here_ref, above_ref):
    depth = here_ref.shape[0]
    total = jnp.dot(band_ref[:, depth:2 * depth], here_ref[...], preferred_element_type=jnp.float32)
    total += jnp.dot(band_ref[:, :depth], below_ref[...], preferred_element_type=jnp.float32)
    total += jnp.dot(band_ref[:, 2 * depth:], above_ref[...], preferred_element_type=jnp.float32)
    return total


def kept(mask_ref, block_row, first, block, width):
    column = lax.broadcasted_iota(jnp.int32, (block, width), 1) // block
    row = jnp.zeros((block, width), jnp.int32)
    for c in range(width // block):
        row = jnp.where(column == c, mask_ref[block_row, first + c], row)
    return row != 0


def mid_kernel(part, mask_ref, band_ref, below_ref, here_ref, above_ref, prev_ref, *rest):
    mid_ref, round_ref = rest[-2:]
    rows, width = here_ref.shape
    block = rows // mask_ref.shape[0]
    total = product(band_ref, below_ref, here_ref, above_ref)
    for i in range(rows // block):
        at = slice(i * block, (i + 1) * block)
        keep = kept(mask_ref, i, part * (width // block), block, width)
        value = jnp.where(keep, 2.0 * total[at] - prev_ref[at, :], 0.0)
        mid_ref[at, :] = value
        round_ref[at, :] = value.astype(jnp.bfloat16)


def mid_part(part, mask, band, below, here, above, prev, mid):
    rows, width = here.shape
    whole = lambda shape: pl.BlockSpec(shape, lambda r: (0, 0))
    panel = pl.BlockSpec((rows, width), lambda r: (0, part))
    operands = [mask, band, below, here, above, prev]
    specs = [pl.BlockSpec(memory_space=pltpu.SMEM), whole(band.shape)] + [whole((rows, width))] * 3 + [panel]
    aliases = {}
    if mid is not None:
        aliases = {len(operands): 0}
        operands.append(mid)
        specs.append(pl.BlockSpec(memory_space=pl.ANY))
    return pl.pallas_call(
        functools.partial(mid_kernel, part),
        grid=(1,),
        in_specs=specs,
        out_specs=[panel, whole((rows, width))],
        out_shape=[jax.ShapeDtypeStruct(prev.shape, jnp.float32), jax.ShapeDtypeStruct((rows, width), jnp.bfloat16)],
        input_output_aliases=aliases,
        compiler_params=params(),
        cost_estimate=pl.CostEstimate(
            flops=6 * rows * rows * width, transcendentals=0,
            bytes_accessed=6 * rows * rows + 16 * rows * width),
        name="mid_part",
    )(*operands)


def next_kernel(part, mask_ref, coeffs_ref, band_ref, below_ref, here_ref, above_ref, now_ref, mid_ref, *rest):
    next_ref, density_ref = rest[-2:]
    rows, width = here_ref.shape
    block = rows // mask_ref.shape[0]
    total = product(band_ref, below_ref, here_ref, above_ref)
    for i in range(rows // block):
        at = slice(i * block, (i + 1) * block)
        keep = kept(mask_ref, i, part * (width // block), block, width)
        value = jnp.where(keep, 2.0 * total[at] - now_ref[at, :], 0.0)
        next_ref[at, :] = value
        density_ref[at, :] = coeffs_ref[0] * mid_ref[at, :] + coeffs_ref[1] * value


def next_part(part, mask, coeffs, band, below, here, above, now, mid, outs):
    rows, width = here.shape
    whole = lambda shape: pl.BlockSpec(shape, lambda r: (0, 0))
    panel = pl.BlockSpec((rows, width), lambda r: (0, part))
    smem = pl.BlockSpec(memory_space=pltpu.SMEM)
    operands = [mask, coeffs, band, below, here, above, now, mid]
    specs = [smem, smem, whole(band.shape)] + [whole((rows, width))] * 3 + [panel] * 2
    aliases = {}
    if outs is not None:
        aliases = {len(operands): 0, len(operands) + 1: 1}
        operands += list(outs)
        specs += [pl.BlockSpec(memory_space=pl.ANY)] * 2
    return pl.pallas_call(
        functools.partial(next_kernel, part),
        grid=(1,),
        in_specs=specs,
        out_specs=[panel] * 2,
        out_shape=[jax.ShapeDtypeStruct(now.shape, jnp.float32)] * 2,
        input_output_aliases=aliases,
        compiler_params=params(),
        cost_estimate=pl.CostEstimate(
            flops=6 * rows * rows * width, transcendentals=0,
            bytes_accessed=6 * rows * rows + 22 * rows * width),
        name="next_part",
    )(*operands)


def local(h_strips, h_slots, t_prev, t_now, t_mask, coeffs):
    width = t_now.shape[1] // PARTS
    here, sides = [], []
    for part in range(PARTS):
        here.append(rounded_part(t_now, part, width))
        sides.append((from_behind(here[part], "row", 1), from_behind(here[part], "row", -1)))
    band = banded(h_slots, h_strips)
    mid, here_mid, sides_mid = None, [], []
    for part in range(PARTS):
        below, above = sides[part]
        mid, rounded = mid_part(part, t_mask, band, below, here[part], above, t_prev, mid)
        here_mid.append(rounded)
        sides_mid.append((from_behind(rounded, "row", 1), from_behind(rounded, "row", -1)))
    outs = None
    for part in range(PARTS):
        below, above = sides_mid[part]
        outs = next_part(part, t_mask, coeffs, band, below, here_mid[part], above, t_now, mid, outs)
    return (mid, outs[0], outs[1])


def solution(mesh):
    panel = P(("grp", "row"), ("col", "rep"))
    return jax.shard_map(
        local,
        mesh=mesh,
        in_specs=(P(("grp", "row"), None, None), P(("grp", "row"), None), panel, panel, panel, P()),
        out_specs=(panel, panel, panel),
        check_vma=False,
    )
```

```python
import functools

import jax
import jax.numpy as jnp
from jax import lax
from jax.experimental import pallas as pl
from jax.experimental.pallas import tpu as pltpu
from jax.sharding import PartitionSpec as P

LANES = 128
WIDTH = 128
CHUNKS = 4
MIB = 1024 * 1024

SMEM = pl.BlockSpec(memory_space=pltpu.SMEM)
VMEM = pl.BlockSpec(memory_space=pltpu.VMEM)
HBM = pl.BlockSpec(memory_space=pltpu.HBM)


def from_behind(block, axis, distance):
    devices = range(lax.axis_size(axis))
    route = [((i - distance) % len(devices), i) for i in devices]
    return lax.ppermute(block, axis, route)


def both_sides(block):
    return from_behind(block, "row", 1), from_behind(block, "row", -1)


def params(limit=32 * MIB):
    return pltpu.CompilerParams(vmem_limit_bytes=limit)


def cost(flops, moved):
    return pl.CostEstimate(flops=flops, transcendentals=0, bytes_accessed=moved)


def round_kernel(part, now_ref, out_ref, held, sems):
    rows, width = out_ref.shape
    step = rows // CHUNKS
    copies = []
    for c in range(CHUNKS):
        at = pl.ds(c * step, step)
        copies.append(pltpu.make_async_copy(now_ref.at[at, pl.ds(part * width, width)], held.at[at, :], sems.at[c]))
        copies[-1].start()
    for c in range(CHUNKS):
        copies[c].wait()
        at = pl.ds(c * step, step)
        out_ref[at, :] = held[at, :].astype(jnp.bfloat16)


def rounded_part(part, now, width):
    rows = now.shape[0]
    return pl.pallas_call(
        functools.partial(round_kernel, part),
        in_specs=[HBM],
        out_specs=VMEM,
        out_shape=jax.ShapeDtypeStruct((rows, width), jnp.bfloat16),
        scratch_shapes=[pltpu.VMEM((rows, width), jnp.float32), pltpu.SemaphoreType.DMA((CHUNKS,))],
        compiler_params=params(60 * MIB),
        cost_estimate=cost(rows * width, 6 * rows * width),
        name="round_part",
    )(now)


def band_kernel(slots_ref, strips_ref, now_ref, out_ref, *round_refs):
    block_rows, block, slot_lanes = strips_ref.shape
    first = now_ref.shape[1] // round_refs[0].shape[1] - len(round_refs)
    for part, round_ref in enumerate(round_refs, first):
        width = round_ref.shape[1]
        round_ref[...] = now_ref[:, part * width:(part + 1) * width].astype(jnp.bfloat16)
    out_ref[...] = jnp.zeros_like(out_ref)
    half = lax.broadcasted_iota(jnp.int32, (block, LANES), 1) // block

    @pl.loop(0, block_rows)
    def _(row):
        at = pl.ds(pl.multiple_of(row * block, block), block)
        for pair in range(slot_lanes // LANES):
            straight = strips_ref[row, :, pair * LANES:(pair + 1) * LANES].astype(jnp.float32)
            swapped = jnp.concatenate([straight[:, block:], straight[:, :block]], axis=1)
            for side in range(2):
                target = slots_ref[row, 2 * pair + side]
                odd = target % 2
                value = jnp.where(odd == side, straight, swapped)
                value = jnp.where(half == odd, value, 0.0).astype(jnp.bfloat16)
                lanes = pl.ds(pl.multiple_of((target // 2) * LANES, LANES), LANES)
                out_ref[at, lanes] += value


def banded(h_slots, h_strips, now, width, count):
    block_rows, block, slot_lanes = h_strips.shape
    columns = 3 * block_rows * block
    rows = block_rows * block
    return pl.pallas_call(
        band_kernel,
        in_specs=[SMEM, VMEM, VMEM],
        out_specs=[VMEM] * (1 + count),
        out_shape=[jax.ShapeDtypeStruct((rows, columns), jnp.bfloat16)]
        + [jax.ShapeDtypeStruct((rows, width), jnp.bfloat16)] * count,
        compiler_params=params(),
        cost_estimate=cost(8 * rows * columns, 2 * rows * (columns + slot_lanes) + 6 * rows * width * count),
        name="band",
    )(h_slots, h_strips, now)


def product(band_ref, below_ref, here_ref, above_ref):
    depth = here_ref.shape[0]
    total = jnp.dot(band_ref[:, depth:2 * depth], here_ref[...], preferred_element_type=jnp.float32)
    total += jnp.dot(band_ref[:, :depth], below_ref[...], preferred_element_type=jnp.float32)
    total += jnp.dot(band_ref[:, 2 * depth:], above_ref[...], preferred_element_type=jnp.float32)
    return total


def kept(mask_ref, block_row, first, block, width):
    column = lax.broadcasted_iota(jnp.int32, (block, width), 1) // block
    row = jnp.zeros((block, width), jnp.int32)
    for c in range(width // block):
        row = jnp.where(column == c, mask_ref[block_row, first + c], row)
    return row != 0


def mid_kernel(part, mask_ref, coeffs_ref, band_ref, below_ref, here_ref, above_ref, prev_ref, *rest):
    mid_ref, round_ref, share_ref, held, sems = rest[-5:]
    rows, width = here_ref.shape
    block = rows // mask_ref.shape[0]
    columns = slice(part * width, (part + 1) * width)
    total = product(band_ref, below_ref, here_ref, above_ref)
    step = rows // CHUNKS
    copies = []
    for i in range(rows // block):
        at = slice(i * block, (i + 1) * block)
        keep = kept(mask_ref, i, part * (width // block), block, width)
        value = jnp.where(keep, 2.0 * total[at] - prev_ref[at, columns], 0.0)
        held[at, :] = value
        round_ref[at, :] = value.astype(jnp.bfloat16)
        share_ref[at, :] = coeffs_ref[0] * value
        if (i + 1) * block % step == 0:
            c = len(copies)
            done = pl.ds(c * step, step)
            copies.append(pltpu.make_async_copy(
                held.at[done, :], mid_ref.at[done, pl.ds(part * width, width)], sems.at[c]))
            copies[-1].start()
    for copy in copies:
        copy.wait()


def mid_part(part, mask, coeffs, band, below, here, above, prev, mid):
    rows, width = here.shape
    operands = [mask, coeffs, band, below, here, above, prev]
    specs = [SMEM] * 2 + [VMEM] * 5
    aliases = {}
    if mid is not None:
        aliases = {len(operands): 0}
        operands.append(mid)
        specs.append(HBM)
    return pl.pallas_call(
        functools.partial(mid_kernel, part),
        in_specs=specs,
        out_specs=[HBM, VMEM, VMEM],
        out_shape=[
            jax.ShapeDtypeStruct(prev.shape, jnp.float32),
            jax.ShapeDtypeStruct((rows, width), jnp.bfloat16),
            jax.ShapeDtypeStruct((rows, width), jnp.float32),
        ],
        scratch_shapes=[pltpu.VMEM((rows, width), jnp.float32), pltpu.SemaphoreType.DMA((CHUNKS,))],
        input_output_aliases=aliases,
        compiler_params=params(),
        cost_estimate=cost(6 * rows * rows * width, 6 * rows * rows + 20 * rows * width),
        name="mid_part",
    )(*operands)


def next_kernel(part, mask_ref, coeffs_ref, band_ref, below_ref, here_ref, above_ref, now_ref, share_ref, *rest):
    next_ref, density_ref, held_next, held_density, sems = rest[-5:]
    rows, width = here_ref.shape
    block = rows // mask_ref.shape[0]
    columns = slice(part * width, (part + 1) * width)
    total = product(band_ref, below_ref, here_ref, above_ref)
    step = rows // CHUNKS
    copies = []
    for i in range(rows // block):
        at = slice(i * block, (i + 1) * block)
        keep = kept(mask_ref, i, part * (width // block), block, width)
        value = jnp.where(keep, 2.0 * total[at] - now_ref[at, columns], 0.0)
        held_next[at, :] = value
        held_density[at, :] = share_ref[at, :] + coeffs_ref[1] * value
        if (i + 1) * block % step == 0:
            c = len(copies) // 2
            done = pl.ds(c * step, step)
            for held, out_ref in ((held_next, next_ref), (held_density, density_ref)):
                copies.append(pltpu.make_async_copy(
                    held.at[done, :], out_ref.at[done, pl.ds(part * width, width)], sems.at[len(copies)]))
                copies[-1].start()
    for copy in copies:
        copy.wait()


def next_part(part, mask, coeffs, band, below, here, above, now, share, outs):
    rows, width = here.shape
    operands = [mask, coeffs, band, below, here, above, now, share]
    specs = [SMEM] * 2 + [VMEM] * 6
    aliases = {}
    if outs is not None:
        aliases = {len(operands): 0, len(operands) + 1: 1}
        operands += list(outs)
        specs += [HBM] * 2
    return pl.pallas_call(
        functools.partial(next_kernel, part),
        in_specs=specs,
        out_specs=[HBM] * 2,
        out_shape=[jax.ShapeDtypeStruct(now.shape, jnp.float32)] * 2,
        scratch_shapes=[pltpu.VMEM((rows, width), jnp.float32)] * 2 + [pltpu.SemaphoreType.DMA((2 * CHUNKS,))],
        input_output_aliases=aliases,
        compiler_params=params(),
        cost_estimate=cost(6 * rows * rows * width, 6 * rows * rows + 22 * rows * width),
        name="next_part",
    )(*operands)


def local(h_strips, h_slots, t_prev, t_now, t_mask, coeffs):
    parts = t_now.shape[1] // WIDTH
    first = min(2, parts)
    here = [rounded_part(part, t_now, WIDTH) for part in range(first)]
    band, *others = banded(h_slots, h_strips, t_now, WIDTH, parts - first)
    here += others
    sides = [both_sides(block) for block in here]
    mid, here_mid, shares, sides_mid = None, [], [], []
    for part in range(parts):
        below, above = sides[part]
        mid, rounded, share = mid_part(part, t_mask, coeffs, band, below, here[part], above, t_prev, mid)
        here_mid.append(rounded)
        shares.append(share)
        sides_mid.append(both_sides(rounded))
    outs = None
    for part in range(parts):
        below, above = sides_mid[part]
        outs = next_part(part, t_mask, coeffs, band, below, here_mid[part], above, t_now, shares[part], outs)
    return (mid, outs[0], outs[1])


def solution(mesh):
    panel = P(("grp", "row"), ("col", "rep"))
    return jax.shard_map(
        local,
        mesh=mesh,
        in_specs=(P(("grp", "row"), None, None), P(("grp", "row"), None), panel, panel, panel, P()),
        out_specs=(panel, panel, panel),
        check_vma=False,
    )
```

```python
import functools

import jax
import jax.numpy as jnp
from jax import lax
from jax.experimental import pallas as pl
from jax.experimental.pallas import tpu as pltpu
from jax.sharding import PartitionSpec as P

LANES = 128
CHUNKS = 4
MIB = 1024 * 1024

SMEM = pl.BlockSpec(memory_space=pltpu.SMEM)
VMEM = pl.BlockSpec(memory_space=pltpu.VMEM)
HBM = pl.BlockSpec(memory_space=pltpu.HBM)


def spans_of(columns):
    width = columns // 2 if columns % (2 * LANES) == 0 else LANES
    return [(start, width) for start in range(0, columns, width)]


def from_behind(block, axis, distance):
    devices = range(lax.axis_size(axis))
    route = [((i - distance) % len(devices), i) for i in devices]
    return lax.ppermute(block, axis, route)


def both_sides(block):
    return from_behind(block, "row", 1), from_behind(block, "row", -1)


def params(limit=32 * MIB):
    return pltpu.CompilerParams(vmem_limit_bytes=limit)


def cost(flops, moved):
    return pl.CostEstimate(flops=flops, transcendentals=0, bytes_accessed=moved)


def round_kernel(starts, now_ref, *out_refs):
    for start, out_ref in zip(starts, out_refs):
        out_ref[...] = now_ref[:, start:start + out_ref.shape[1]].astype(jnp.bfloat16)


def rounded(now, spans):
    rows = now.shape[0]
    size = rows * sum(width for _, width in spans)
    return list(pl.pallas_call(
        functools.partial(round_kernel, [start for start, _ in spans]),
        in_specs=[VMEM],
        out_specs=[VMEM] * len(spans),
        out_shape=[jax.ShapeDtypeStruct((rows, width), jnp.bfloat16) for _, width in spans],
        compiler_params=params(),
        cost_estimate=cost(size, 6 * size),
        name="round_part",
    )(now))


def band_kernel(slots_ref, strips_ref, out_ref):
    block_rows, block, slot_lanes = strips_ref.shape
    out_ref[...] = jnp.zeros_like(out_ref)
    half = lax.broadcasted_iota(jnp.int32, (block, LANES), 1) // block

    @pl.loop(0, block_rows)
    def _(row):
        at = pl.ds(pl.multiple_of(row * block, block), block)
        for pair in range(slot_lanes // LANES):
            straight = strips_ref[row, :, pair * LANES:(pair + 1) * LANES].astype(jnp.float32)
            swapped = jnp.concatenate([straight[:, block:], straight[:, :block]], axis=1)
            for side in range(2):
                target = slots_ref[row, 2 * pair + side]
                odd = target % 2
                value = jnp.where(odd == side, straight, swapped)
                value = jnp.where(half == odd, value, 0.0).astype(jnp.bfloat16)
                lanes = pl.ds(pl.multiple_of((target // 2) * LANES, LANES), LANES)
                out_ref[at, lanes] += value


def banded(h_slots, h_strips):
    block_rows, block, slot_lanes = h_strips.shape
    rows, columns = block_rows * block, 3 * block_rows * block
    return pl.pallas_call(
        band_kernel,
        in_specs=[SMEM, VMEM],
        out_specs=VMEM,
        out_shape=jax.ShapeDtypeStruct((rows, columns), jnp.bfloat16),
        compiler_params=params(),
        cost_estimate=cost(8 * rows * columns, 2 * rows * (columns + slot_lanes)),
        name="band",
    )(h_slots, h_strips)


def product(band_ref, below_ref, here_ref, above_ref):
    depth = here_ref.shape[0]
    total = jnp.dot(band_ref[:, depth:2 * depth], here_ref[...], preferred_element_type=jnp.float32)
    total += jnp.dot(band_ref[:, :depth], below_ref[...], preferred_element_type=jnp.float32)
    total += jnp.dot(band_ref[:, 2 * depth:], above_ref[...], preferred_element_type=jnp.float32)
    return total


def kept(mask_ref, block_row, first, block, width):
    column = lax.broadcasted_iota(jnp.int32, (block, width), 1) // block
    row = jnp.zeros((block, width), jnp.int32)
    for c in range(width // block):
        row = jnp.where(column == c, mask_ref[block_row, first + c], row)
    return row != 0


def mid_kernel(start, mask_ref, coeffs_ref, band_ref, below_ref, here_ref, above_ref, prev_ref, *rest):
    mid_ref, round_ref, share_ref, held, sems = rest[-5:]
    rows, width = here_ref.shape
    block = rows // mask_ref.shape[0]
    columns = slice(start, start + width)
    total = product(band_ref, below_ref, here_ref, above_ref)
    step = rows // CHUNKS
    copies = []
    for i in range(rows // block):
        at = slice(i * block, (i + 1) * block)
        keep = kept(mask_ref, i, start // block, block, width)
        value = jnp.where(keep, 2.0 * total[at] - prev_ref[at, columns], 0.0)
        held[at, :] = value
        round_ref[at, :] = value.astype(jnp.bfloat16)
        share_ref[at, :] = coeffs_ref[0] * value
        if (i + 1) * block % step == 0:
            c = len(copies)
            done = pl.ds(c * step, step)
            copies.append(pltpu.make_async_copy(
                held.at[done, :], mid_ref.at[done, pl.ds(start, width)], sems.at[c]))
            copies[-1].start()
    for copy in copies:
        copy.wait()


def mid_part(span, mask, coeffs, band, below, here, above, prev, mid):
    rows, width = here.shape
    operands = [mask, coeffs, band, below, here, above, prev]
    specs = [SMEM] * 2 + [VMEM] * 5
    aliases = {}
    if mid is not None:
        aliases = {len(operands): 0}
        operands.append(mid)
        specs.append(HBM)
    return pl.pallas_call(
        functools.partial(mid_kernel, span[0]),
        in_specs=specs,
        out_specs=[HBM, VMEM, VMEM],
        out_shape=[
            jax.ShapeDtypeStruct(prev.shape, jnp.float32),
            jax.ShapeDtypeStruct((rows, width), jnp.bfloat16),
            jax.ShapeDtypeStruct((rows, width), jnp.float32),
        ],
        scratch_shapes=[pltpu.VMEM((rows, width), jnp.float32), pltpu.SemaphoreType.DMA((CHUNKS,))],
        input_output_aliases=aliases,
        compiler_params=params(),
        cost_estimate=cost(6 * rows * rows * width, 6 * rows * rows + 20 * rows * width),
        name="mid_part",
    )(*operands)


def begun_kernel(start, band_ref, here_ref, below_ref, now_ref, sums_ref):
    depth, width = here_ref.shape
    total = jnp.dot(band_ref[:, :depth], below_ref[...], preferred_element_type=jnp.float32)
    total += jnp.dot(band_ref[:, depth:2 * depth], here_ref[...], preferred_element_type=jnp.float32)
    sums_ref[...] = 2.0 * total - now_ref[:, start:start + width]


def begun_part(span, band, here, below, now):
    rows, width = here.shape
    return pl.pallas_call(
        functools.partial(begun_kernel, span[0]),
        in_specs=[VMEM] * 4,
        out_specs=VMEM,
        out_shape=jax.ShapeDtypeStruct((rows, width), jnp.float32),
        compiler_params=params(),
        cost_estimate=cost(4 * rows * rows * width, 4 * rows * rows + 12 * rows * width),
        name="next_begun",
    )(band, here, below, now)


def next_kernel(start, mask_ref, coeffs_ref, band_ref, above_ref, sums_ref, share_ref, *rest):
    next_ref, density_ref, held_next, held_density, sems = rest[-5:]
    rows, width = above_ref.shape
    block = rows // mask_ref.shape[0]
    step = rows // CHUNKS
    copies = []
    for c in range(CHUNKS):
        total = jnp.dot(
            band_ref[c * step:(c + 1) * step, 2 * rows:], above_ref[...], preferred_element_type=jnp.float32)
        for i in range(step // block):
            at = slice(c * step + i * block, c * step + (i + 1) * block)
            keep = kept(mask_ref, c * (step // block) + i, start // block, block, width)
            value = jnp.where(keep, 2.0 * total[i * block:(i + 1) * block] + sums_ref[at, :], 0.0)
            held_next[at, :] = value
            held_density[at, :] = share_ref[at, :] + coeffs_ref[1] * value
        done = pl.ds(c * step, step)
        for held, out_ref in ((held_next, next_ref), (held_density, density_ref)):
            copies.append(pltpu.make_async_copy(
                held.at[done, :], out_ref.at[done, pl.ds(start, width)], sems.at[len(copies)]))
            copies[-1].start()
    for copy in copies:
        copy.wait()


def next_part(span, mask, coeffs, band, above, sums, share, whole, outs):
    rows, width = above.shape
    operands = [mask, coeffs, band, above, sums, share]
    specs = [SMEM] * 2 + [VMEM] * 4
    aliases = {}
    if outs is not None:
        aliases = {len(operands): 0, len(operands) + 1: 1}
        operands += list(outs)
        specs += [HBM] * 2
    return pl.pallas_call(
        functools.partial(next_kernel, span[0]),
        in_specs=specs,
        out_specs=[HBM] * 2,
        out_shape=[jax.ShapeDtypeStruct(whole, jnp.float32)] * 2,
        scratch_shapes=[pltpu.VMEM((rows, width), jnp.float32)] * 2 + [pltpu.SemaphoreType.DMA((2 * CHUNKS,))],
        input_output_aliases=aliases,
        compiler_params=params(),
        cost_estimate=cost(2 * rows * rows * width, 2 * rows * rows + 22 * rows * width),
        name="next_part",
    )(*operands)


def local(h_strips, h_slots, t_prev, t_now, t_mask, coeffs):
    spans = spans_of(t_now.shape[1])
    parts = len(spans)
    start, width = spans[0]
    here = [t_now[:, start:start + width].astype(jnp.bfloat16)]
    here[0], t_now, t_prev, h_strips = lax.optimization_barrier((here[0], t_now, t_prev, h_strips))
    here += rounded(t_now, spans[1:])
    band = banded(h_slots, h_strips)
    sides = [both_sides(block) for block in here]
    mid, here_mid, shares, sides_mid = None, [], [], []
    for part in range(parts):
        below, above = sides[part]
        mid, low, share = mid_part(spans[part], t_mask, coeffs, band, below, here[part], above, t_prev, mid)
        here_mid.append(low)
        shares.append(share)
        sides_mid.append(both_sides(low))
    outs = None
    for part in range(parts):
        below, above = sides_mid[part]
        sums = begun_part(spans[part], band, here_mid[part], below, t_now)
        outs = next_part(spans[part], t_mask, coeffs, band, above, sums, shares[part], t_now.shape, outs)
    return (mid, outs[0], outs[1])


def solution(mesh):
    panel = P(("grp", "row"), ("col", "rep"))
    return jax.shard_map(
        local,
        mesh=mesh,
        in_specs=(P(("grp", "row"), None, None), P(("grp", "row"), None), panel, panel, panel, P()),
        out_specs=(panel, panel, panel),
        check_vma=False,
    )
```

```python
import functools

import jax
import jax.numpy as jnp
from jax import lax
from jax.experimental import pallas as pl
from jax.experimental.pallas import tpu as pltpu
from jax.sharding import PartitionSpec as P

LANES = 128
CHUNKS = 4
MIB = 1024 * 1024

SMEM = pl.BlockSpec(memory_space=pltpu.SMEM)
VMEM = pl.BlockSpec(memory_space=pltpu.VMEM)
HBM = pl.BlockSpec(memory_space=pltpu.HBM)


def spans_of(columns):
    width = columns // 2 if columns % (2 * LANES) == 0 else LANES
    return [(start, width) for start in range(0, columns, width)]


def both_sides(block):
    rows, reps = lax.axis_size("row"), lax.axis_size("rep")
    arrived = []
    for turn in (1, -1):
        route = []
        for row in range(rows):
            for rep in range(reps):
                source = (row + (turn if rep % 2 == 0 else -turn)) % rows
                route.append((source * reps + rep, row * reps + rep))
        arrived.append(lax.ppermute(block, ("row", "rep"), route))
    return tuple(arrived)


def side_columns(depth, order):
    odd = lax.axis_index("rep") % 2
    return pl.ds(pl.multiple_of(jnp.where(odd == order, 2 * depth, 0), LANES), depth)


def params(limit=32 * MIB):
    return pltpu.CompilerParams(vmem_limit_bytes=limit)


def cost(flops, moved):
    return pl.CostEstimate(flops=flops, transcendentals=0, bytes_accessed=moved)


def round_kernel(starts, now_ref, *out_refs):
    for start, out_ref in zip(starts, out_refs):
        out_ref[...] = now_ref[:, start:start + out_ref.shape[1]].astype(jnp.bfloat16)


def rounded(now, spans):
    rows = now.shape[0]
    size = rows * sum(width for _, width in spans)
    return list(pl.pallas_call(
        functools.partial(round_kernel, [start for start, _ in spans]),
        in_specs=[VMEM],
        out_specs=[VMEM] * len(spans),
        out_shape=[jax.ShapeDtypeStruct((rows, width), jnp.bfloat16) for _, width in spans],
        compiler_params=params(),
        cost_estimate=cost(size, 6 * size),
        name="round_part",
    )(now))


def band_kernel(slots_ref, strips_ref, out_ref):
    block_rows, block, slot_lanes = strips_ref.shape
    out_ref[...] = jnp.zeros_like(out_ref)
    half = lax.broadcasted_iota(jnp.int32, (block, LANES), 1) // block

    @pl.loop(0, block_rows)
    def _(row):
        at = pl.ds(pl.multiple_of(row * block, block), block)
        for pair in range(slot_lanes // LANES):
            straight = strips_ref[row, :, pair * LANES:(pair + 1) * LANES].astype(jnp.float32)
            swapped = jnp.concatenate([straight[:, block:], straight[:, :block]], axis=1)
            for side in range(2):
                target = slots_ref[row, 2 * pair + side]
                odd = target % 2
                value = jnp.where(odd == side, straight, swapped)
                value = jnp.where(half == odd, value, 0.0).astype(jnp.bfloat16)
                lanes = pl.ds(pl.multiple_of((target // 2) * LANES, LANES), LANES)
                out_ref[at, lanes] += value


def banded(h_slots, h_strips):
    block_rows, block, slot_lanes = h_strips.shape
    rows, columns = block_rows * block, 3 * block_rows * block
    return pl.pallas_call(
        band_kernel,
        in_specs=[SMEM, VMEM],
        out_specs=VMEM,
        out_shape=jax.ShapeDtypeStruct((rows, columns), jnp.bfloat16),
        compiler_params=params(),
        cost_estimate=cost(8 * rows * columns, 2 * rows * (columns + slot_lanes)),
        name="band",
    )(h_slots, h_strips)


def begun_product(band_ref, here_ref, first_ref):
    depth = here_ref.shape[0]
    total = jnp.dot(band_ref[:, depth:2 * depth], here_ref[...], preferred_element_type=jnp.float32)
    total += jnp.dot(band_ref[:, side_columns(depth, 0)], first_ref[...], preferred_element_type=jnp.float32)
    return total


def kept(mask_ref, block_row, first, block, width):
    column = lax.broadcasted_iota(jnp.int32, (block, width), 1) // block
    row = jnp.zeros((block, width), jnp.int32)
    for c in range(width // block):
        row = jnp.where(column == c, mask_ref[block_row, first + c], row)
    return row != 0


def mid_kernel(start, mask_ref, coeffs_ref, band_ref, here_ref, first_ref, second_ref, prev_ref, *rest):
    mid_ref, round_ref, share_ref, held, sems = rest[-5:]
    rows, width = here_ref.shape
    block = rows // mask_ref.shape[0]
    columns = slice(start, start + width)
    total = begun_product(band_ref, here_ref, first_ref)
    total += jnp.dot(band_ref[:, side_columns(rows, 1)], second_ref[...], preferred_element_type=jnp.float32)
    step = rows // CHUNKS
    copies = []
    for i in range(rows // block):
        at = slice(i * block, (i + 1) * block)
        keep = kept(mask_ref, i, start // block, block, width)
        value = jnp.where(keep, 2.0 * total[at] - prev_ref[at, columns], 0.0)
        held[at, :] = value
        round_ref[at, :] = value.astype(jnp.bfloat16)
        share_ref[at, :] = coeffs_ref[0] * value
        if (i + 1) * block % step == 0:
            c = len(copies)
            done = pl.ds(c * step, step)
            copies.append(pltpu.make_async_copy(
                held.at[done, :], mid_ref.at[done, pl.ds(start, width)], sems.at[c]))
            copies[-1].start()
    for copy in copies:
        copy.wait()


def mid_part(span, mask, coeffs, band, here, first, second, prev, mid):
    rows, width = here.shape
    operands = [mask, coeffs, band, here, first, second, prev]
    specs = [SMEM] * 2 + [VMEM] * 5
    aliases = {}
    if mid is not None:
        aliases = {len(operands): 0}
        operands.append(mid)
        specs.append(HBM)
    return pl.pallas_call(
        functools.partial(mid_kernel, span[0]),
        in_specs=specs,
        out_specs=[HBM, VMEM, VMEM],
        out_shape=[
            jax.ShapeDtypeStruct(prev.shape, jnp.float32),
            jax.ShapeDtypeStruct((rows, width), jnp.bfloat16),
            jax.ShapeDtypeStruct((rows, width), jnp.float32),
        ],
        scratch_shapes=[pltpu.VMEM((rows, width), jnp.float32), pltpu.SemaphoreType.DMA((CHUNKS,))],
        input_output_aliases=aliases,
        compiler_params=params(),
        cost_estimate=cost(6 * rows * rows * width, 6 * rows * rows + 20 * rows * width),
        name="mid_part",
    )(*operands)


def begun_kernel(start, band_ref, here_ref, first_ref, now_ref, sums_ref):
    width = here_ref.shape[1]
    total = begun_product(band_ref, here_ref, first_ref)
    sums_ref[...] = 2.0 * total - now_ref[:, start:start + width]


def begun_part(span, band, here, first, now):
    rows, width = here.shape
    return pl.pallas_call(
        functools.partial(begun_kernel, span[0]),
        in_specs=[VMEM] * 4,
        out_specs=VMEM,
        out_shape=jax.ShapeDtypeStruct((rows, width), jnp.float32),
        compiler_params=params(),
        cost_estimate=cost(4 * rows * rows * width, 4 * rows * rows + 12 * rows * width),
        name="next_begun",
    )(band, here, first, now)


def next_kernel(start, mask_ref, coeffs_ref, band_ref, second_ref, sums_ref, share_ref, *rest):
    next_ref, density_ref, held_next, held_density, sems = rest[-5:]
    rows, width = second_ref.shape
    block = rows // mask_ref.shape[0]
    step = rows // CHUNKS
    copies = []
    for c in range(CHUNKS):
        total = jnp.dot(
            band_ref[c * step:(c + 1) * step, side_columns(rows, 1)], second_ref[...], preferred_element_type=jnp.float32)
        for i in range(step // block):
            at = slice(c * step + i * block, c * step + (i + 1) * block)
            keep = kept(mask_ref, c * (step // block) + i, start // block, block, width)
            value = jnp.where(keep, 2.0 * total[i * block:(i + 1) * block] + sums_ref[at, :], 0.0)
            held_next[at, :] = value
            held_density[at, :] = share_ref[at, :] + coeffs_ref[1] * value
        done = pl.ds(c * step, step)
        for held, out_ref in ((held_next, next_ref), (held_density, density_ref)):
            copies.append(pltpu.make_async_copy(
                held.at[done, :], out_ref.at[done, pl.ds(start, width)], sems.at[len(copies)]))
            copies[-1].start()
    for copy in copies:
        copy.wait()


def next_part(span, mask, coeffs, band, second, sums, share, whole, outs):
    rows, width = second.shape
    operands = [mask, coeffs, band, second, sums, share]
    specs = [SMEM] * 2 + [VMEM] * 4
    aliases = {}
    if outs is not None:
        aliases = {len(operands): 0, len(operands) + 1: 1}
        operands += list(outs)
        specs += [HBM] * 2
    return pl.pallas_call(
        functools.partial(next_kernel, span[0]),
        in_specs=specs,
        out_specs=[HBM] * 2,
        out_shape=[jax.ShapeDtypeStruct(whole, jnp.float32)] * 2,
        scratch_shapes=[pltpu.VMEM((rows, width), jnp.float32)] * 2 + [pltpu.SemaphoreType.DMA((2 * CHUNKS,))],
        input_output_aliases=aliases,
        compiler_params=params(),
        cost_estimate=cost(2 * rows * rows * width, 2 * rows * rows + 22 * rows * width),
        name="next_part",
    )(*operands)


def local(h_strips, h_slots, t_prev, t_now, t_mask, coeffs):
    spans = spans_of(t_now.shape[1])
    parts = len(spans)
    start, width = spans[0]
    here = [t_now[:, start:start + width].astype(jnp.bfloat16)]
    here[0], t_now, t_prev, h_strips = lax.optimization_barrier((here[0], t_now, t_prev, h_strips))
    here += rounded(t_now, spans[1:])
    band = banded(h_slots, h_strips)
    sides = [both_sides(block) for block in here]
    mid, here_mid, shares, sides_mid = None, [], [], []
    for part in range(parts):
        mid, low, share = mid_part(spans[part], t_mask, coeffs, band, here[part], *sides[part], t_prev, mid)
        here_mid.append(low)
        shares.append(share)
        sides_mid.append(both_sides(low))
    outs = None
    for part in range(parts):
        first, second = sides_mid[part]
        sums = begun_part(spans[part], band, here_mid[part], first, t_now)
        outs = next_part(spans[part], t_mask, coeffs, band, second, sums, shares[part], t_now.shape, outs)
    return (mid, outs[0], outs[1])


def solution(mesh):
    panel = P(("grp", "row"), ("col", "rep"))
    return jax.shard_map(
        local,
        mesh=mesh,
        in_specs=(P(("grp", "row"), None, None), P(("grp", "row"), None), panel, panel, panel, P()),
        out_specs=(panel, panel, panel),
        check_vma=False,
    )
```

```python
import functools

import jax
import jax.numpy as jnp
from jax import lax
from jax.experimental import pallas as pl
from jax.experimental.pallas import tpu as pltpu
from jax.sharding import PartitionSpec as P

LANES = 128
CHUNKS = 2
MIB = 1024 * 1024

SMEM = pl.BlockSpec(memory_space=pltpu.SMEM)
VMEM = pl.BlockSpec(memory_space=pltpu.VMEM)
HBM = pl.BlockSpec(memory_space=pltpu.HBM)


def spans_of(columns):
    width = columns // 2 if columns % (2 * LANES) == 0 else LANES
    return [(start, width) for start in range(0, columns, width)]


def both_sides(block):
    rows, reps = lax.axis_size("row"), lax.axis_size("rep")
    arrived = []
    for turn in (1, -1):
        route = []
        for row in range(rows):
            for rep in range(reps):
                source = (row + (turn if rep % 2 == 0 else -turn)) % rows
                route.append((source * reps + rep, row * reps + rep))
        arrived.append(lax.ppermute(block, ("row", "rep"), route))
    return tuple(arrived)


def side_columns(depth, order):
    odd = lax.axis_index("rep") % 2
    return pl.ds(pl.multiple_of(jnp.where(odd == order, 2 * depth, 0), LANES), depth)


def params(limit=32 * MIB):
    return pltpu.CompilerParams(vmem_limit_bytes=limit)


def cost(flops, moved):
    return pl.CostEstimate(flops=flops, transcendentals=0, bytes_accessed=moved)


def round_kernel(starts, now_ref, *out_refs):
    for start, out_ref in zip(starts, out_refs):
        out_ref[...] = now_ref[:, start:start + out_ref.shape[1]].astype(jnp.bfloat16)


def rounded(now, spans):
    rows = now.shape[0]
    size = rows * sum(width for _, width in spans)
    return list(pl.pallas_call(
        functools.partial(round_kernel, [start for start, _ in spans]),
        in_specs=[VMEM],
        out_specs=[VMEM] * len(spans),
        out_shape=[jax.ShapeDtypeStruct((rows, width), jnp.bfloat16) for _, width in spans],
        compiler_params=params(),
        cost_estimate=cost(size, 6 * size),
        name="round_part",
    )(now))


def band_kernel(slots_ref, strips_ref, out_ref):
    block_rows, block, slot_lanes = strips_ref.shape
    out_ref[...] = jnp.zeros_like(out_ref)
    half = lax.broadcasted_iota(jnp.int32, (block, LANES), 1) // block

    @pl.loop(0, block_rows)
    def _(row):
        at = pl.ds(pl.multiple_of(row * block, block), block)
        for pair in range(slot_lanes // LANES):
            straight = strips_ref[row, :, pair * LANES:(pair + 1) * LANES].astype(jnp.float32)
            swapped = jnp.concatenate([straight[:, block:], straight[:, :block]], axis=1)
            for side in range(2):
                target = slots_ref[row, 2 * pair + side]
                odd = target % 2
                value = jnp.where(odd == side, straight, swapped)
                value = jnp.where(half == odd, value, 0.0).astype(jnp.bfloat16)
                lanes = pl.ds(pl.multiple_of((target // 2) * LANES, LANES), LANES)
                out_ref[at, lanes] += value


def banded(h_slots, h_strips):
    block_rows, block, slot_lanes = h_strips.shape
    rows, columns = block_rows * block, 3 * block_rows * block
    return pl.pallas_call(
        band_kernel,
        in_specs=[SMEM, VMEM],
        out_specs=VMEM,
        out_shape=jax.ShapeDtypeStruct((rows, columns), jnp.bfloat16),
        compiler_params=params(),
        cost_estimate=cost(8 * rows * columns, 2 * rows * (columns + slot_lanes)),
        name="band",
    )(h_slots, h_strips)


def begun_product(band_ref, here_ref, first_ref):
    depth = here_ref.shape[0]
    total = jnp.dot(band_ref[:, depth:2 * depth], here_ref[...], preferred_element_type=jnp.float32)
    total += jnp.dot(band_ref[:, side_columns(depth, 0)], first_ref[...], preferred_element_type=jnp.float32)
    return total


def kept(mask_ref, block_row, first, block, width):
    column = lax.broadcasted_iota(jnp.int32, (block, width), 1) // block
    row = jnp.zeros((block, width), jnp.int32)
    for c in range(width // block):
        row = jnp.where(column == c, mask_ref[block_row, first + c], row)
    return row != 0


def begun_kernel(start, band_ref, here_ref, first_ref, before_ref, sums_ref):
    width = here_ref.shape[1]
    sums_ref[...] = 2.0 * begun_product(band_ref, here_ref, first_ref) - before_ref[:, start:start + width]


def begun_part(span, band, here, first, before):
    rows, width = here.shape
    return pl.pallas_call(
        functools.partial(begun_kernel, span[0]),
        in_specs=[VMEM] * 4,
        out_specs=VMEM,
        out_shape=jax.ShapeDtypeStruct((rows, width), jnp.float32),
        compiler_params=params(),
        cost_estimate=cost(4 * rows * rows * width, 4 * rows * rows + 12 * rows * width),
        name="begun_part",
    )(band, here, first, before)


def finished(start, chunk, mask_ref, band_ref, second_ref, sums_ref):
    rows, width = second_ref.shape
    block = rows // mask_ref.shape[0]
    step = rows // CHUNKS
    total = jnp.dot(
        band_ref[chunk * step:(chunk + 1) * step, side_columns(rows, 1)], second_ref[...],
        preferred_element_type=jnp.float32)
    for i in range(step // block):
        at = slice(chunk * step + i * block, chunk * step + (i + 1) * block)
        keep = kept(mask_ref, chunk * (step // block) + i, start // block, block, width)
        yield at, jnp.where(keep, 2.0 * total[i * block:(i + 1) * block] + sums_ref[at, :], 0.0)


def send_out(start, chunk, held, out_ref, sem):
    step = held.shape[0] // CHUNKS
    done = pl.ds(chunk * step, step)
    copy = pltpu.make_async_copy(held.at[done, :], out_ref.at[done, pl.ds(start, held.shape[1])], sem)
    copy.start()
    return copy


def mid_kernel(start, mask_ref, coeffs_ref, band_ref, second_ref, sums_ref, *rest):
    mid_ref, round_ref, share_ref, held, sems = rest[-5:]
    copies = []
    for c in range(CHUNKS):
        for at, value in finished(start, c, mask_ref, band_ref, second_ref, sums_ref):
            held[at, :] = value
            round_ref[at, :] = value.astype(jnp.bfloat16)
            share_ref[at, :] = coeffs_ref[0] * value
        copies.append(send_out(start, c, held, mid_ref, sems.at[c]))
    for copy in copies:
        copy.wait()


def mid_part(span, mask, coeffs, band, second, sums, whole, mid):
    rows, width = second.shape
    operands = [mask, coeffs, band, second, sums]
    specs = [SMEM] * 2 + [VMEM] * 3
    aliases = {}
    if mid is not None:
        aliases = {len(operands): 0}
        operands.append(mid)
        specs.append(HBM)
    return pl.pallas_call(
        functools.partial(mid_kernel, span[0]),
        in_specs=specs,
        out_specs=[HBM, VMEM, VMEM],
        out_shape=[
            jax.ShapeDtypeStruct(whole, jnp.float32),
            jax.ShapeDtypeStruct((rows, width), jnp.bfloat16),
            jax.ShapeDtypeStruct((rows, width), jnp.float32),
        ],
        scratch_shapes=[pltpu.VMEM((rows, width), jnp.float32), pltpu.SemaphoreType.DMA((CHUNKS,))],
        input_output_aliases=aliases,
        compiler_params=params(),
        cost_estimate=cost(2 * rows * rows * width, 2 * rows * rows + 18 * rows * width),
        name="mid_part",
    )(*operands)


def next_kernel(start, mask_ref, coeffs_ref, band_ref, second_ref, sums_ref, share_ref, *rest):
    next_ref, density_ref, held_next, held_density, sems = rest[-5:]
    copies = []
    for c in range(CHUNKS):
        for at, value in finished(start, c, mask_ref, band_ref, second_ref, sums_ref):
            held_next[at, :] = value
            held_density[at, :] = share_ref[at, :] + coeffs_ref[1] * value
        for held, out_ref in ((held_next, next_ref), (held_density, density_ref)):
            copies.append(send_out(start, c, held, out_ref, sems.at[len(copies)]))
    for copy in copies:
        copy.wait()


def next_part(span, mask, coeffs, band, second, sums, share, whole, outs):
    rows, width = second.shape
    operands = [mask, coeffs, band, second, sums, share]
    specs = [SMEM] * 2 + [VMEM] * 4
    aliases = {}
    if outs is not None:
        aliases = {len(operands): 0, len(operands) + 1: 1}
        operands += list(outs)
        specs += [HBM] * 2
    return pl.pallas_call(
        functools.partial(next_kernel, span[0]),
        in_specs=specs,
        out_specs=[HBM] * 2,
        out_shape=[jax.ShapeDtypeStruct(whole, jnp.float32)] * 2,
        scratch_shapes=[pltpu.VMEM((rows, width), jnp.float32)] * 2 + [pltpu.SemaphoreType.DMA((2 * CHUNKS,))],
        input_output_aliases=aliases,
        compiler_params=params(),
        cost_estimate=cost(2 * rows * rows * width, 2 * rows * rows + 22 * rows * width),
        name="next_part",
    )(*operands)


def local(h_strips, h_slots, t_prev, t_now, t_mask, coeffs):
    spans = spans_of(t_now.shape[1])
    parts = len(spans)
    start, width = spans[0]
    here = [t_now[:, start:start + width].astype(jnp.bfloat16)]
    here[0], t_now, t_prev, h_strips = lax.optimization_barrier((here[0], t_now, t_prev, h_strips))
    here += rounded(t_now, spans[1:])
    band = banded(h_slots, h_strips)
    sides = [both_sides(block) for block in here]
    mid, here_mid, shares, sides_mid = None, [], [], []
    for part in range(parts):
        first, second = sides[part]
        sums = begun_part(spans[part], band, here[part], first, t_prev)
        mid, low, share = mid_part(spans[part], t_mask, coeffs, band, second, sums, t_now.shape, mid)
        here_mid.append(low)
        shares.append(share)
        sides_mid.append(both_sides(low))
    outs = None
    for part in range(parts):
        first, second = sides_mid[part]
        sums = begun_part(spans[part], band, here_mid[part], first, t_now)
        outs = next_part(spans[part], t_mask, coeffs, band, second, sums, shares[part], t_now.shape, outs)
    return (mid, outs[0], outs[1])


def solution(mesh):
    panel = P(("grp", "row"), ("col", "rep"))
    return jax.shard_map(
        local,
        mesh=mesh,
        in_specs=(P(("grp", "row"), None, None), P(("grp", "row"), None), panel, panel, panel, P()),
        out_specs=(panel, panel, panel),
        check_vma=False,
    )
```

```python
import functools

import jax
import jax.numpy as jnp
from jax import lax
from jax.experimental import pallas as pl
from jax.experimental.pallas import tpu as pltpu
from jax.sharding import PartitionSpec as P

LANES = 128
CHUNKS = 2
MIB = 1024 * 1024

SMEM = pl.BlockSpec(memory_space=pltpu.SMEM)
VMEM = pl.BlockSpec(memory_space=pltpu.VMEM)
HBM = pl.BlockSpec(memory_space=pltpu.HBM)


def spans_of(columns):
    width = columns // 4 if columns % (4 * LANES) == 0 else LANES
    return [(start, width) for start in range(0, columns, width)]


def both_sides(block):
    rows = lax.axis_size("row")
    return tuple(
        lax.ppermute(block, "row", [((row - turn) % rows, row) for row in range(rows)]) for turn in (1, -1))


def side_columns(depth, order):
    return pl.ds(2 * depth * order, depth)


def params(limit=32 * MIB):
    return pltpu.CompilerParams(vmem_limit_bytes=limit)


def cost(flops, moved):
    return pl.CostEstimate(flops=flops, transcendentals=0, bytes_accessed=moved)


def round_kernel(starts, now_ref, *out_refs):
    for start, out_ref in zip(starts, out_refs):
        out_ref[...] = now_ref[:, start:start + out_ref.shape[1]].astype(jnp.bfloat16)


def rounded(now, spans):
    rows = now.shape[0]
    size = rows * sum(width for _, width in spans)
    return list(pl.pallas_call(
        functools.partial(round_kernel, [start for start, _ in spans]),
        in_specs=[VMEM],
        out_specs=[VMEM] * len(spans),
        out_shape=[jax.ShapeDtypeStruct((rows, width), jnp.bfloat16) for _, width in spans],
        compiler_params=params(),
        cost_estimate=cost(size, 6 * size),
        name="round_part",
    )(now))


def band_kernel(slots_ref, strips_ref, out_ref):
    block_rows, block, slot_lanes = strips_ref.shape
    out_ref[...] = jnp.zeros_like(out_ref)
    half = lax.broadcasted_iota(jnp.int32, (block, LANES), 1) // block

    @pl.loop(0, block_rows)
    def _(row):
        at = pl.ds(pl.multiple_of(row * block, block), block)
        for pair in range(slot_lanes // LANES):
            straight = strips_ref[row, :, pair * LANES:(pair + 1) * LANES].astype(jnp.float32)
            swapped = jnp.concatenate([straight[:, block:], straight[:, :block]], axis=1)
            for side in range(2):
                target = slots_ref[row, 2 * pair + side]
                odd = target % 2
                value = jnp.where(odd == side, straight, swapped)
                value = jnp.where(half == odd, value, 0.0).astype(jnp.bfloat16)
                lanes = pl.ds(pl.multiple_of((target // 2) * LANES, LANES), LANES)
                out_ref[at, lanes] += value


def banded(h_slots, h_strips):
    block_rows, block, slot_lanes = h_strips.shape
    rows, columns = block_rows * block, 3 * block_rows * block
    return pl.pallas_call(
        band_kernel,
        in_specs=[SMEM, VMEM],
        out_specs=VMEM,
        out_shape=jax.ShapeDtypeStruct((rows, columns), jnp.bfloat16),
        compiler_params=params(),
        cost_estimate=cost(8 * rows * columns, 2 * rows * (columns + slot_lanes)),
        name="band",
    )(h_slots, h_strips)


def begun_product(band_ref, here_ref, first_ref):
    depth = here_ref.shape[0]
    total = jnp.dot(band_ref[:, depth:2 * depth], here_ref[...], preferred_element_type=jnp.float32)
    total += jnp.dot(band_ref[:, side_columns(depth, 0)], first_ref[...], preferred_element_type=jnp.float32)
    return total


def kept(mask_ref, block_row, first, block, width):
    column = lax.broadcasted_iota(jnp.int32, (block, width), 1) // block
    row = jnp.zeros((block, width), jnp.int32)
    for c in range(width // block):
        row = jnp.where(column == c, mask_ref[block_row, first + c], row)
    return row != 0


def begun_kernel(start, band_ref, here_ref, first_ref, before_ref, sums_ref):
    width = here_ref.shape[1]
    sums_ref[...] = 2.0 * begun_product(band_ref, here_ref, first_ref) - before_ref[:, start:start + width]


def begun_part(span, band, here, first, before):
    rows, width = here.shape
    return pl.pallas_call(
        functools.partial(begun_kernel, span[0]),
        in_specs=[VMEM] * 4,
        out_specs=VMEM,
        out_shape=jax.ShapeDtypeStruct((rows, width), jnp.float32),
        compiler_params=params(),
        cost_estimate=cost(4 * rows * rows * width, 4 * rows * rows + 12 * rows * width),
        name="begun_part",
    )(band, here, first, before)


def finished(start, chunk, mask_ref, band_ref, second_ref, sums_ref):
    rows, width = second_ref.shape
    block = rows // mask_ref.shape[0]
    step = rows // CHUNKS
    total = jnp.dot(
        band_ref[chunk * step:(chunk + 1) * step, side_columns(rows, 1)], second_ref[...],
        preferred_element_type=jnp.float32)
    for i in range(step // block):
        at = slice(chunk * step + i * block, chunk * step + (i + 1) * block)
        keep = kept(mask_ref, chunk * (step // block) + i, start // block, block, width)
        yield at, jnp.where(keep, 2.0 * total[i * block:(i + 1) * block] + sums_ref[at, :], 0.0)


def send_out(start, chunk, held, out_ref, sem):
    step = held.shape[0] // CHUNKS
    done = pl.ds(chunk * step, step)
    copy = pltpu.make_async_copy(held.at[done, :], out_ref.at[done, pl.ds(start, held.shape[1])], sem)
    copy.start()
    return copy


def mid_kernel(start, mask_ref, coeffs_ref, band_ref, second_ref, sums_ref, *rest):
    mid_ref, round_ref, share_ref, held, sems = rest[-5:]
    copies = []
    for c in range(CHUNKS):
        for at, value in finished(start, c, mask_ref, band_ref, second_ref, sums_ref):
            held[at, :] = value
            round_ref[at, :] = value.astype(jnp.bfloat16)
            share_ref[at, :] = coeffs_ref[0] * value
        copies.append(send_out(start, c, held, mid_ref, sems.at[c]))
    for copy in copies:
        copy.wait()


def mid_part(span, mask, coeffs, band, second, sums, whole, mid):
    rows, width = second.shape
    operands = [mask, coeffs, band, second, sums]
    specs = [SMEM] * 2 + [VMEM] * 3
    aliases = {}
    if mid is not None:
        aliases = {len(operands): 0}
        operands.append(mid)
        specs.append(HBM)
    return pl.pallas_call(
        functools.partial(mid_kernel, span[0]),
        in_specs=specs,
        out_specs=[HBM, VMEM, VMEM],
        out_shape=[
            jax.ShapeDtypeStruct(whole, jnp.float32),
            jax.ShapeDtypeStruct((rows, width), jnp.bfloat16),
            jax.ShapeDtypeStruct((rows, width), jnp.float32),
        ],
        scratch_shapes=[pltpu.VMEM((rows, width), jnp.float32), pltpu.SemaphoreType.DMA((CHUNKS,))],
        input_output_aliases=aliases,
        compiler_params=params(),
        cost_estimate=cost(2 * rows * rows * width, 2 * rows * rows + 18 * rows * width),
        name="mid_part",
    )(*operands)


def next_kernel(start, mask_ref, coeffs_ref, band_ref, second_ref, sums_ref, share_ref, *rest):
    next_ref, density_ref, held_next, held_density, sems = rest[-5:]
    copies = []
    for c in range(CHUNKS):
        for at, value in finished(start, c, mask_ref, band_ref, second_ref, sums_ref):
            held_next[at, :] = value
            held_density[at, :] = share_ref[at, :] + coeffs_ref[1] * value
        for held, out_ref in ((held_next, next_ref), (held_density, density_ref)):
            copies.append(send_out(start, c, held, out_ref, sems.at[len(copies)]))
    for copy in copies:
        copy.wait()


def next_part(span, mask, coeffs, band, second, sums, share, whole, outs):
    rows, width = second.shape
    operands = [mask, coeffs, band, second, sums, share]
    specs = [SMEM] * 2 + [VMEM] * 4
    aliases = {}
    if outs is not None:
        aliases = {len(operands): 0, len(operands) + 1: 1}
        operands += list(outs)
        specs += [HBM] * 2
    return pl.pallas_call(
        functools.partial(next_kernel, span[0]),
        in_specs=specs,
        out_specs=[HBM] * 2,
        out_shape=[jax.ShapeDtypeStruct(whole, jnp.float32)] * 2,
        scratch_shapes=[pltpu.VMEM((rows, width), jnp.float32)] * 2 + [pltpu.SemaphoreType.DMA((2 * CHUNKS,))],
        input_output_aliases=aliases,
        compiler_params=params(),
        cost_estimate=cost(2 * rows * rows * width, 2 * rows * rows + 22 * rows * width),
        name="next_part",
    )(*operands)


def local(h_strips, h_slots, t_prev, t_now, t_mask, coeffs):
    spans = spans_of(t_now.shape[1])
    parts = len(spans)
    start, width = spans[0]
    here = [t_now[:, start:start + width].astype(jnp.bfloat16)]
    here[0], t_now, t_prev, h_strips = lax.optimization_barrier((here[0], t_now, t_prev, h_strips))
    here += rounded(t_now, spans[1:])
    band = banded(h_slots, h_strips)
    sides = [both_sides(block) for block in here]
    mid, here_mid, shares, sides_mid = None, [], [], []
    for part in range(parts):
        first, second = sides[part]
        sums = begun_part(spans[part], band, here[part], first, t_prev)
        mid, low, share = mid_part(spans[part], t_mask, coeffs, band, second, sums, t_now.shape, mid)
        here_mid.append(low)
        shares.append(share)
        sides_mid.append(both_sides(low))
    outs = None
    for part in range(parts):
        first, second = sides_mid[part]
        sums = begun_part(spans[part], band, here_mid[part], first, t_now)
        outs = next_part(spans[part], t_mask, coeffs, band, second, sums, shares[part], t_now.shape, outs)
    return (mid, outs[0], outs[1])


def solution(mesh):
    panel = P(("grp", "row"), ("col", "rep"))
    return jax.shard_map(
        local,
        mesh=mesh,
        in_specs=(P(("grp", "row"), None, None), P(("grp", "row"), None), panel, panel, panel, P()),
        out_specs=(panel, panel, panel),
        check_vma=False,
    )
```

```python
import functools

import jax
import jax.numpy as jnp
from jax import lax
from jax.experimental import pallas as pl
from jax.experimental.pallas import tpu as pltpu
from jax.sharding import PartitionSpec as P

LANES = 128
CHUNKS = 2
MIB = 1024 * 1024

SMEM = pl.BlockSpec(memory_space=pltpu.SMEM)
VMEM = pl.BlockSpec(memory_space=pltpu.VMEM)
ANY = pl.BlockSpec(memory_space=pl.ANY)
HBM = pl.BlockSpec(memory_space=pltpu.HBM)


def spans_of(columns):
    width = columns // 4 if columns % (4 * LANES) == 0 else LANES
    return [(start, width) for start in range(0, columns, width)]


def both_sides(block):
    rows = lax.axis_size("row")
    return tuple(
        lax.ppermute(block, "row", [((row - turn) % rows, row) for row in range(rows)]) for turn in (1, -1))


def side_columns(depth, order):
    return pl.ds(2 * depth * order, depth)


def params(limit=32 * MIB):
    return pltpu.CompilerParams(vmem_limit_bytes=limit)


def cost(flops, moved):
    return pl.CostEstimate(flops=flops, transcendentals=0, bytes_accessed=moved)


def round_kernel(starts, now_ref, *out_refs):
    for start, out_ref in zip(starts, out_refs):
        out_ref[...] = now_ref[:, start:start + out_ref.shape[1]].astype(jnp.bfloat16)


def rounded(now, spans):
    rows = now.shape[0]
    size = rows * sum(width for _, width in spans)
    return list(pl.pallas_call(
        functools.partial(round_kernel, [start for start, _ in spans]),
        in_specs=[VMEM],
        out_specs=[VMEM] * len(spans),
        out_shape=[jax.ShapeDtypeStruct((rows, width), jnp.bfloat16) for _, width in spans],
        compiler_params=params(),
        cost_estimate=cost(size, 6 * size),
        name="round_part",
    )(now))


def band_kernel(slots_ref, strips_ref, out_ref):
    block_rows, block, slot_lanes = strips_ref.shape
    out_ref[...] = jnp.zeros_like(out_ref)
    half = lax.broadcasted_iota(jnp.int32, (block, LANES), 1) // block

    @pl.loop(0, block_rows)
    def _(row):
        at = pl.ds(pl.multiple_of(row * block, block), block)
        for pair in range(slot_lanes // LANES):
            straight = strips_ref[row, :, pair * LANES:(pair + 1) * LANES].astype(jnp.float32)
            swapped = jnp.concatenate([straight[:, block:], straight[:, :block]], axis=1)
            for side in range(2):
                target = slots_ref[row, 2 * pair + side]
                odd = target % 2
                value = jnp.where(odd == side, straight, swapped)
                value = jnp.where(half == odd, value, 0.0).astype(jnp.bfloat16)
                lanes = pl.ds(pl.multiple_of((target // 2) * LANES, LANES), LANES)
                out_ref[at, lanes] += value


def banded(h_slots, h_strips):
    block_rows, block, slot_lanes = h_strips.shape
    rows, columns = block_rows * block, 3 * block_rows * block
    return pl.pallas_call(
        band_kernel,
        in_specs=[SMEM, VMEM],
        out_specs=VMEM,
        out_shape=jax.ShapeDtypeStruct((rows, columns), jnp.bfloat16),
        compiler_params=params(),
        cost_estimate=cost(8 * rows * columns, 2 * rows * (columns + slot_lanes)),
        name="band",
    )(h_slots, h_strips)


def product(band_ref, here_ref, first_ref, second_ref=None):
    depth = here_ref.shape[0]
    total = jnp.dot(band_ref[:, depth:2 * depth], here_ref[...], preferred_element_type=jnp.float32)
    total += jnp.dot(band_ref[:, side_columns(depth, 0)], first_ref[...], preferred_element_type=jnp.float32)
    if second_ref is not None:
        total += jnp.dot(band_ref[:, side_columns(depth, 1)], second_ref[...], preferred_element_type=jnp.float32)
    return total


def kept(mask_ref, block_row, first, block, width):
    column = lax.broadcasted_iota(jnp.int32, (block, width), 1) // block
    row = jnp.zeros((block, width), jnp.int32)
    for c in range(width // block):
        row = jnp.where(column == c, mask_ref[block_row, first + c], row)
    return row != 0


def masked(start, mask_ref, term):
    rows, width = term.shape
    block = rows // mask_ref.shape[0]
    for i in range(rows // block):
        at = slice(i * block, (i + 1) * block)
        yield at, jnp.where(kept(mask_ref, i, start // block, block, width), term[at], 0.0)


def writes(jobs, sems):
    copies = []
    for held, out_ref, start in jobs:
        columns = pl.ds(start, held.shape[1])
        copies.append(pltpu.make_async_copy(held, out_ref.at[:, columns], sems.at[len(copies)]))
        copies[-1].start()
    return copies


def mid_kernel(start, mask_ref, band_ref, here_ref, first_ref, second_ref, prev_ref, *rest):
    mid_ref, round_ref = rest[-2:]
    total = product(band_ref, here_ref, first_ref, second_ref)
    term = 2.0 * total - prev_ref[:, start:start + here_ref.shape[1]]
    for at, value in masked(start, mask_ref, term):
        mid_ref[at, :] = value
        round_ref[at, :] = value.astype(jnp.bfloat16)


def mid_part(span, mask, band, here, first, second, prev, after):
    rows, width = here.shape
    return pl.pallas_call(
        functools.partial(mid_kernel, span[0]),
        in_specs=[SMEM] + [VMEM] * 5 + [ANY] * len(after),
        out_specs=[VMEM] * 2,
        out_shape=[jax.ShapeDtypeStruct(here.shape, jnp.float32), jax.ShapeDtypeStruct(here.shape, jnp.bfloat16)],
        compiler_params=params(),
        cost_estimate=cost(6 * rows * rows * width, 6 * rows * rows + 16 * rows * width),
        name="mid_part",
    )(mask, band, here, first, second, prev, *after)


def next_kernel(start, places, panels, unread, mask_ref, coeffs_ref, band_ref, here_ref, first_ref, second_ref, now_ref,
                mid_ref, *rest):
    rest = rest[unread:]
    held_refs, rest = rest[:len(places)], rest[len(places):]
    next_ref, density_ref, sems = rest[-panels - 3], rest[-panels - 2], rest[-1]
    out_refs = rest[-panels - 1:-1]
    copies = writes([(held, out_refs[o], at) for held, (o, at) in zip(held_refs, places)], sems)
    total = product(band_ref, here_ref, first_ref, second_ref)
    term = 2.0 * total - now_ref[:, start:start + here_ref.shape[1]]
    for at, value in masked(start, mask_ref, term):
        next_ref[at, :] = value
        density_ref[at, :] = coeffs_ref[0] * mid_ref[at, :] + coeffs_ref[1] * value
    for copy in copies:
        copy.wait()


def begun_kernel(start, places, panels, band_ref, here_ref, first_ref, now_ref, *rest):
    held_refs, rest = rest[:len(places)], rest[len(places):]
    sums_ref, sems = rest[-panels - 2], rest[-1]
    out_refs = rest[-panels - 1:-1]
    copies = writes([(held, out_refs[o], at) for held, (o, at) in zip(held_refs, places)], sems)
    sums_ref[...] = 2.0 * product(band_ref, here_ref, first_ref) - now_ref[:, start:start + here_ref.shape[1]]
    for copy in copies:
        copy.wait()


def with_writes(kernel, specs, operands, out_shapes, moves, panels, whole, outs, flops, name):
    held = [part for part, _ in moves]
    places = [place for _, place in moves]
    moved = sum(part.size for part in held)
    aliases = {}
    operands, specs = operands + held, specs + [VMEM] * len(held)
    if outs is not None:
        aliases = {len(operands) + o: len(out_shapes) + o for o in range(panels)}
        operands, specs = operands + list(outs), specs + [HBM] * panels
    results = pl.pallas_call(
        functools.partial(kernel, places),
        in_specs=specs,
        out_specs=[VMEM] * len(out_shapes) + [HBM] * panels,
        out_shape=out_shapes + [jax.ShapeDtypeStruct(whole, jnp.float32)] * panels,
        scratch_shapes=[pltpu.SemaphoreType.DMA((max(len(held), 1),))],
        input_output_aliases=aliases,
        compiler_params=params(),
        cost_estimate=cost(flops, 4 * moved + flops // 200),
        name=name,
    )(*operands)
    return results[:len(out_shapes)], tuple(results[len(out_shapes):])


def next_part(span, mask, coeffs, band, here, first, second, now, mid, after, moves, panels):
    rows, width = here.shape
    return with_writes(
        lambda places, *refs: next_kernel(span[0], places, panels, len(after), *refs),
        [SMEM] * 2 + [VMEM] * 6 + [ANY] * len(after), [mask, coeffs, band, here, first, second, now, mid, *after],
        [jax.ShapeDtypeStruct(here.shape, jnp.float32)] * 2, moves, panels, now.shape, None,
        6 * rows * rows * width, "next_part")


def begun_part(span, band, here, first, now, moves, panels, outs):
    rows, width = here.shape
    (sums,), outs = with_writes(
        lambda places, *refs: begun_kernel(span[0], places, panels, *refs),
        [VMEM] * 4, [band, here, first, now],
        [jax.ShapeDtypeStruct(here.shape, jnp.float32)], moves, panels, now.shape, outs,
        4 * rows * rows * width, "begun_part")
    return sums, outs


def last_kernel(start, mask_ref, coeffs_ref, band_ref, second_ref, sums_ref, mid_ref, *rest):
    next_ref, density_ref, held_next, held_density, sems = rest[-5:]
    rows, width = second_ref.shape
    block = rows // mask_ref.shape[0]
    step = rows // CHUNKS
    copies = []
    for c in range(CHUNKS):
        total = jnp.dot(
            band_ref[c * step:(c + 1) * step, side_columns(rows, 1)], second_ref[...],
            preferred_element_type=jnp.float32)
        for i in range(step // block):
            at = slice(c * step + i * block, c * step + (i + 1) * block)
            keep = kept(mask_ref, c * (step // block) + i, start // block, block, width)
            value = jnp.where(keep, 2.0 * total[i * block:(i + 1) * block] + sums_ref[at, :], 0.0)
            held_next[at, :] = value
            held_density[at, :] = coeffs_ref[0] * mid_ref[at, :] + coeffs_ref[1] * value
        done = pl.ds(c * step, step)
        for held, out_ref in ((held_next, next_ref), (held_density, density_ref)):
            copies.append(pltpu.make_async_copy(
                held.at[done, :], out_ref.at[done, pl.ds(start, width)], sems.at[len(copies)]))
            copies[-1].start()
    for copy in copies:
        copy.wait()


def last_part(span, mask, coeffs, band, second, sums, mid, outs):
    rows, width = second.shape
    return pl.pallas_call(
        functools.partial(last_kernel, span[0]),
        in_specs=[SMEM] * 2 + [VMEM] * 4 + [HBM] * 2,
        out_specs=[HBM] * 2,
        out_shape=[jax.ShapeDtypeStruct(out.shape, jnp.float32) for out in outs],
        scratch_shapes=[pltpu.VMEM((rows, width), jnp.float32)] * 2 + [pltpu.SemaphoreType.DMA((2 * CHUNKS,))],
        input_output_aliases={6: 0, 7: 1},
        compiler_params=params(),
        cost_estimate=cost(2 * rows * rows * width, 2 * rows * rows + 22 * rows * width),
        name="last_part",
    )(mask, coeffs, band, second, sums, mid, *outs)


def local(h_strips, h_slots, t_prev, t_now, t_mask, coeffs):
    spans = spans_of(t_now.shape[1])
    parts = len(spans)
    start, width = spans[0]
    here = [t_now[:, start:start + width].astype(jnp.bfloat16)]
    here[0], t_now, t_prev, h_strips = lax.optimization_barrier((here[0], t_now, t_prev, h_strips))
    here += rounded(t_now, spans[1:])
    band = banded(h_slots, h_strips)
    sides = [both_sides(block) for block in here]
    mids, here_mid, sides_mid = [], [], []
    for part in range(parts):
        first, second = sides[part]
        mid, low = mid_part(spans[part], t_mask, band, here[part], first, second, t_prev, mids[-1:])
        mids.append(mid)
        here_mid.append(low)
        sides_mid.append(both_sides(low))
    t_mid, outs, waiting, after = None, None, [], []
    for part in range(parts - 1):
        panels, moves = 0, []
        if part == 0:
            panels, moves = 1, [(mids[p], (0, spans[p][0])) for p in range(parts)]
        elif part == parts - 2:
            panels, moves = 2, waiting
        (term, density), written = next_part(
            spans[part], t_mask, coeffs, band, here_mid[part], *sides_mid[part], t_now, mids[part], after, moves, panels)
        after = [term]
        if part == 0:
            t_mid = written[0]
        elif part == parts - 2:
            outs, waiting = written, []
        waiting += [(term, (0, spans[part][0])), (density, (1, spans[part][0]))]
    first, second = sides_mid[-1]
    sums, outs = begun_part(spans[-1], band, here_mid[-1], first, t_now, waiting, 2, outs)
    outs = last_part(spans[-1], t_mask, coeffs, band, second, sums, mids[-1], outs)
    return (t_mid, outs[0], outs[1])


def solution(mesh):
    panel = P(("grp", "row"), ("col", "rep"))
    return jax.shard_map(
        local,
        mesh=mesh,
        in_specs=(P(("grp", "row"), None, None), P(("grp", "row"), None), panel, panel, panel, P()),
        out_specs=(panel, panel, panel),
        check_vma=False,
    )
```

```python
import functools

import jax
import jax.numpy as jnp
from jax import lax
from jax.experimental import pallas as pl
from jax.experimental.pallas import tpu as pltpu
from jax.sharding import PartitionSpec as P

LANES = 128
CHUNKS = 2
MIB = 1024 * 1024

SMEM = pl.BlockSpec(memory_space=pltpu.SMEM)
VMEM = pl.BlockSpec(memory_space=pltpu.VMEM)
ANY = pl.BlockSpec(memory_space=pl.ANY)
HBM = pl.BlockSpec(memory_space=pltpu.HBM)


def spans_of(columns):
    if columns % (4 * LANES):
        ones = [(start, LANES) for start in range(0, columns, LANES)]
        return ones, ones
    half, quarter = columns // 2, columns // 4
    return [(0, half), (half, half)], [(0, half), (half, quarter), (half + quarter, quarter)]


def both_sides(block):
    rows = lax.axis_size("row")
    second = lax.ppermute(block, "row", [((row + 1) % rows, row) for row in range(rows)])
    first = lax.ppermute(block, "row", [((row - 1) % rows, row) for row in range(rows)])
    return first, second


def side_columns(depth, order):
    return pl.ds(2 * depth * order, depth)


def params(limit=32 * MIB):
    return pltpu.CompilerParams(vmem_limit_bytes=limit)


def cost(flops, moved):
    return pl.CostEstimate(flops=flops, transcendentals=0, bytes_accessed=moved)


def round_kernel(starts, now_ref, *out_refs):
    for start, out_ref in zip(starts, out_refs):
        out_ref[...] = now_ref[:, start:start + out_ref.shape[1]].astype(jnp.bfloat16)


def rounded(now, spans):
    rows = now.shape[0]
    size = rows * sum(width for _, width in spans)
    return list(pl.pallas_call(
        functools.partial(round_kernel, [start for start, _ in spans]),
        in_specs=[VMEM],
        out_specs=[VMEM] * len(spans),
        out_shape=[jax.ShapeDtypeStruct((rows, width), jnp.bfloat16) for _, width in spans],
        compiler_params=params(),
        cost_estimate=cost(size, 6 * size),
        name="round_part",
    )(now))


def band_kernel(slots_ref, strips_ref, out_ref):
    block_rows, block, slot_lanes = strips_ref.shape
    out_ref[...] = jnp.zeros_like(out_ref)
    half = lax.broadcasted_iota(jnp.int32, (block, LANES), 1) // block

    @pl.loop(0, block_rows)
    def _(row):
        at = pl.ds(pl.multiple_of(row * block, block), block)
        for pair in range(slot_lanes // LANES):
            straight = strips_ref[row, :, pair * LANES:(pair + 1) * LANES].astype(jnp.float32)
            swapped = jnp.concatenate([straight[:, block:], straight[:, :block]], axis=1)
            for side in range(2):
                target = slots_ref[row, 2 * pair + side]
                odd = target % 2
                value = jnp.where(odd == side, straight, swapped)
                value = jnp.where(half == odd, value, 0.0).astype(jnp.bfloat16)
                lanes = pl.ds(pl.multiple_of((target // 2) * LANES, LANES), LANES)
                out_ref[at, lanes] += value


def banded(h_slots, h_strips):
    block_rows, block, slot_lanes = h_strips.shape
    rows, columns = block_rows * block, 3 * block_rows * block
    return pl.pallas_call(
        band_kernel,
        in_specs=[SMEM, VMEM],
        out_specs=VMEM,
        out_shape=jax.ShapeDtypeStruct((rows, columns), jnp.bfloat16),
        compiler_params=params(),
        cost_estimate=cost(8 * rows * columns, 2 * rows * (columns + slot_lanes)),
        name="band",
    )(h_slots, h_strips)


def product(band_ref, here_ref, first_ref, second_ref=None):
    depth = here_ref.shape[0]
    total = jnp.dot(band_ref[:, depth:2 * depth], here_ref[...], preferred_element_type=jnp.float32)
    total += jnp.dot(band_ref[:, side_columns(depth, 0)], first_ref[...], preferred_element_type=jnp.float32)
    if second_ref is not None:
        total += jnp.dot(band_ref[:, side_columns(depth, 1)], second_ref[...], preferred_element_type=jnp.float32)
    return total


def kept(mask_ref, block_row, first, block, width):
    column = lax.broadcasted_iota(jnp.int32, (block, width), 1) // block
    row = jnp.zeros((block, width), jnp.int32)
    for c in range(width // block):
        row = jnp.where(column == c, mask_ref[block_row, first + c], row)
    return row != 0


def masked(start, mask_ref, term):
    rows, width = term.shape
    block = rows // mask_ref.shape[0]
    for i in range(rows // block):
        at = slice(i * block, (i + 1) * block)
        yield at, jnp.where(kept(mask_ref, i, start // block, block, width), term[at], 0.0)


def writes(jobs, sems):
    copies = []
    for held, out_ref, start in jobs:
        columns = pl.ds(start, held.shape[1])
        copies.append(pltpu.make_async_copy(held, out_ref.at[:, columns], sems.at[len(copies)]))
        copies[-1].start()
    return copies


def mid_kernel(start, pieces, mask_ref, band_ref, here_ref, second_ref, first_ref, prev_ref, *rest):
    mid_ref, round_refs = rest[-pieces - 1], rest[-pieces:]
    total = product(band_ref, here_ref, first_ref, second_ref)
    term = 2.0 * total - prev_ref[:, start:start + here_ref.shape[1]]
    for at, value in masked(start, mask_ref, term):
        mid_ref[at, :] = value
        from_column = 0
        for round_ref in round_refs:
            to_column = from_column + round_ref.shape[1]
            round_ref[at, :] = value[:, from_column:to_column].astype(jnp.bfloat16)
            from_column = to_column


def mid_part(span, widths, mask, band, here, first, second, prev, after):
    rows, width = here.shape
    return pl.pallas_call(
        functools.partial(mid_kernel, span[0], len(widths)),
        in_specs=[SMEM] + [VMEM] * 5 + [ANY] * len(after),
        out_specs=[VMEM] * (1 + len(widths)),
        out_shape=[jax.ShapeDtypeStruct(here.shape, jnp.float32)]
        + [jax.ShapeDtypeStruct((rows, piece), jnp.bfloat16) for piece in widths],
        compiler_params=params(),
        cost_estimate=cost(6 * rows * rows * width, 6 * rows * rows + 16 * rows * width),
        name="mid_part",
    )(mask, band, here, second, first, prev, *after)


def next_kernel(start, mid_start, places, panels, unread, mask_ref, coeffs_ref, band_ref, here_ref, second_ref, first_ref, now_ref,
                mid_ref, *rest):
    rest = rest[unread:]
    held_refs, rest = rest[:len(places)], rest[len(places):]
    next_ref, density_ref, sems = rest[-panels - 3], rest[-panels - 2], rest[-1]
    out_refs = rest[-panels - 1:-1]
    copies = writes([(held, out_refs[o], at) for held, (o, at) in zip(held_refs, places)], sems)
    total = product(band_ref, here_ref, first_ref, second_ref)
    term = 2.0 * total - now_ref[:, start:start + here_ref.shape[1]]
    for at, value in masked(start, mask_ref, term):
        next_ref[at, :] = value
        mid = mid_ref[at, mid_start:mid_start + here_ref.shape[1]]
        density_ref[at, :] = coeffs_ref[0] * mid + coeffs_ref[1] * value
    for copy in copies:
        copy.wait()


def begun_kernel(start, band_ref, here_ref, first_ref, now_ref, *rest):
    sums_ref = rest[-1]
    sums_ref[...] = 2.0 * product(band_ref, here_ref, first_ref) - now_ref[:, start:start + here_ref.shape[1]]


def with_writes(kernel, specs, operands, out_shapes, moves, panels, whole, outs, flops, name):
    held = [part for part, _ in moves]
    places = [place for _, place in moves]
    moved = sum(part.size for part in held)
    aliases = {}
    operands, specs = operands + held, specs + [VMEM] * len(held)
    if outs is not None:
        aliases = {len(operands) + o: len(out_shapes) + o for o in range(panels)}
        operands, specs = operands + list(outs), specs + [HBM] * panels
    results = pl.pallas_call(
        functools.partial(kernel, places),
        in_specs=specs,
        out_specs=[VMEM] * len(out_shapes) + [HBM] * panels,
        out_shape=out_shapes + [jax.ShapeDtypeStruct(whole, jnp.float32)] * panels,
        scratch_shapes=[pltpu.SemaphoreType.DMA((max(len(held), 1),))],
        input_output_aliases=aliases,
        compiler_params=params(),
        cost_estimate=cost(flops, 4 * moved + flops // 200),
        name=name,
    )(*operands)
    return results[:len(out_shapes)], tuple(results[len(out_shapes):])


def next_part(span, mid_start, mask, coeffs, band, here, first, second, now, mid, after, moves, panels):
    rows, width = here.shape
    return with_writes(
        lambda places, *refs: next_kernel(span[0], mid_start, places, panels, len(after), *refs),
        [SMEM] * 2 + [VMEM] * 6 + [ANY] * len(after), [mask, coeffs, band, here, second, first, now, mid, *after],
        [jax.ShapeDtypeStruct(here.shape, jnp.float32)] * 2, moves, panels, now.shape, None,
        6 * rows * rows * width, "next_part")


def begun_part(span, band, here, first, now, after):
    rows, width = here.shape
    return pl.pallas_call(
        functools.partial(begun_kernel, span[0]),
        in_specs=[VMEM] * 4 + [ANY] * len(after),
        out_specs=VMEM,
        out_shape=jax.ShapeDtypeStruct(here.shape, jnp.float32),
        compiler_params=params(),
        cost_estimate=cost(4 * rows * rows * width, 4 * rows * rows + 12 * rows * width),
        name="begun_part",
    )(band, here, first, now, *after)


def last_kernel(start, mid_start, places, mask_ref, coeffs_ref, band_ref, second_ref, sums_ref, mid_ref, *rest):
    held_refs = rest[:len(places)]
    next_ref, density_ref, held_next, held_density, early_sems, sems = rest[-6:]
    copies = writes([(held, (next_ref, density_ref)[o], at) for held, (o, at) in zip(held_refs, places)], early_sems)
    early = len(copies)
    rows, width = second_ref.shape
    block = rows // mask_ref.shape[0]
    step = rows // CHUNKS
    for c in range(CHUNKS):
        total = jnp.dot(
            band_ref[c * step:(c + 1) * step, side_columns(rows, 1)], second_ref[...],
            preferred_element_type=jnp.float32)
        for i in range(step // block):
            at = slice(c * step + i * block, c * step + (i + 1) * block)
            keep = kept(mask_ref, c * (step // block) + i, start // block, block, width)
            value = jnp.where(keep, 2.0 * total[i * block:(i + 1) * block] + sums_ref[at, :], 0.0)
            held_next[at, :] = value
            density = coeffs_ref[0] * mid_ref[at, mid_start:mid_start + width] + coeffs_ref[1] * value
            held_density[at, :] = density
        done = pl.ds(c * step, step)
        for held, out_ref in ((held_next, next_ref), (held_density, density_ref)):
            copies.append(pltpu.make_async_copy(
                held.at[done, :], out_ref.at[done, pl.ds(start, width)], sems.at[len(copies) - early]))
            copies[-1].start()
    for copy in copies:
        copy.wait()


def last_part(span, mid_start, mask, coeffs, band, second, sums, mid, moves, outs):
    rows, width = second.shape
    held = [part for part, _ in moves]
    return pl.pallas_call(
        functools.partial(last_kernel, span[0], mid_start, [place for _, place in moves]),
        in_specs=[SMEM] * 2 + [VMEM] * (4 + len(held)) + [HBM] * 2,
        out_specs=[HBM] * 2,
        out_shape=[jax.ShapeDtypeStruct(out.shape, jnp.float32) for out in outs],
        scratch_shapes=[pltpu.VMEM((rows, width), jnp.float32)] * 2
        + [pltpu.SemaphoreType.DMA((max(len(held), 1),)), pltpu.SemaphoreType.DMA((2 * CHUNKS,))],
        input_output_aliases={6 + len(held): 0, 7 + len(held): 1},
        compiler_params=params(),
        cost_estimate=cost(2 * rows * rows * width, 2 * rows * rows + 22 * rows * width),
        name="last_part",
    )(mask, coeffs, band, second, sums, mid, *held, *outs)


def local(h_strips, h_slots, t_prev, t_now, t_mask, coeffs):
    spans, spans_next = spans_of(t_now.shape[1])
    start, width = spans[0]
    here = [t_now[:, start:start + width].astype(jnp.bfloat16)]
    here[0], t_now, t_prev, h_strips = lax.optimization_barrier((here[0], t_now, t_prev, h_strips))
    here += rounded(t_now, spans[1:])
    band = banded(h_slots, h_strips)
    sides = [both_sides(block) for block in here]
    mids, here_mid, sides_mid, origin = [], [], [], []
    for part, (start, width) in enumerate(spans):
        inside = [span for span in spans_next if start <= span[0] < start + width]
        mid, *lows = mid_part(
            spans[part], [piece for _, piece in inside], t_mask, band, here[part], *sides[part], t_prev, mids[-1:])
        mids.append(mid)
        here_mid += lows
        sides_mid += [both_sides(low) for low in lows]
        origin += [(part, span[0] - start) for span in inside]
    t_mid, outs, waiting, after = None, None, [], []
    last = len(spans_next) - 1
    for part, span in enumerate(spans_next[:-1]):
        panels, moves = 0, []
        if part == 0:
            panels, moves = 1, [(mid, (0, spans[p][0])) for p, mid in enumerate(mids)]
        elif part == last - 1:
            panels, moves, waiting = 2, waiting, []
        source, mid_start = origin[part]
        (term, density), written = next_part(
            span, mid_start, t_mask, coeffs, band, here_mid[part], *sides_mid[part], t_now, mids[source], after,
            moves, panels)
        after = [term]
        if part == 0:
            t_mid = written[0]
        elif part == last - 1:
            outs = written
        waiting = waiting + [(term, (0, span[0])), (density, (1, span[0]))]
    first, second = sides_mid[last]
    source, mid_start = origin[last]
    sums = begun_part(spans_next[last], band, here_mid[last], first, t_now, after)
    outs = last_part(spans_next[last], mid_start, t_mask, coeffs, band, second, sums, mids[source], waiting, outs)
    return (t_mid, outs[0], outs[1])


def solution(mesh):
    panel = P(("grp", "row"), ("col", "rep"))
    return jax.shard_map(
        local,
        mesh=mesh,
        in_specs=(P(("grp", "row"), None, None), P(("grp", "row"), None), panel, panel, panel, P()),
        out_specs=(panel, panel, panel),
        check_vma=False,
    )
```

```python
import functools

import jax
import jax.numpy as jnp
from jax import lax
from jax.experimental import pallas as pl
from jax.experimental.pallas import tpu as pltpu
from jax.sharding import PartitionSpec as P

LANES = 128
CHUNKS = 2
MIB = 1024 * 1024

SMEM = pl.BlockSpec(memory_space=pltpu.SMEM)
VMEM = pl.BlockSpec(memory_space=pltpu.VMEM)
ANY = pl.BlockSpec(memory_space=pl.ANY)
HBM = pl.BlockSpec(memory_space=pltpu.HBM)


def slots_of(blocks):
    first, later = blocks * 11 // 32, blocks * 9 // 32
    return first, later, later, blocks - first - 2 * later


def both_sides(block):
    rows = lax.axis_size("row")
    second = lax.ppermute(block, "row", [((row + 1) % rows, row) for row in range(rows)])
    first = lax.ppermute(block, "row", [((row - 1) % rows, row) for row in range(rows)])
    return first, second


def side_columns(depth, order):
    return pl.ds(2 * depth * order, depth)


def params(limit=32 * MIB):
    return pltpu.CompilerParams(vmem_limit_bytes=limit)


def cost(flops, moved):
    return pl.CostEstimate(flops=flops, transcendentals=0, bytes_accessed=moved)


def round_kernel(starts, now_ref, *out_refs):
    for start, out_ref in zip(starts, out_refs):
        out_ref[...] = now_ref[:, start:start + out_ref.shape[1]].astype(jnp.bfloat16)


def rounded(now, spans):
    rows = now.shape[0]
    size = rows * sum(width for _, width in spans)
    return list(pl.pallas_call(
        functools.partial(round_kernel, [start for start, _ in spans]),
        in_specs=[VMEM],
        out_specs=[VMEM] * len(spans),
        out_shape=[jax.ShapeDtypeStruct((rows, width), jnp.bfloat16) for _, width in spans],
        compiler_params=params(),
        cost_estimate=cost(size, 6 * size),
        name="round_part",
    )(now))


def band_kernel(slots_ref, strips_ref, out_ref):
    block_rows, block, slot_lanes = strips_ref.shape
    out_ref[...] = jnp.zeros_like(out_ref)
    half = lax.broadcasted_iota(jnp.int32, (block, LANES), 1) // block

    @pl.loop(0, block_rows)
    def _(row):
        at = pl.ds(pl.multiple_of(row * block, block), block)
        for pair in range(slot_lanes // LANES):
            straight = strips_ref[row, :, pair * LANES:(pair + 1) * LANES].astype(jnp.float32)
            swapped = jnp.concatenate([straight[:, block:], straight[:, :block]], axis=1)
            for side in range(2):
                target = slots_ref[row, 2 * pair + side]
                odd = target % 2
                value = jnp.where(odd == side, straight, swapped)
                value = jnp.where(half == odd, value, 0.0).astype(jnp.bfloat16)
                lanes = pl.ds(pl.multiple_of((target // 2) * LANES, LANES), LANES)
                out_ref[at, lanes] += value


def banded(h_slots, h_strips):
    block_rows, block, slot_lanes = h_strips.shape
    rows, columns = block_rows * block, 3 * block_rows * block
    return pl.pallas_call(
        band_kernel,
        in_specs=[SMEM, VMEM],
        out_specs=VMEM,
        out_shape=jax.ShapeDtypeStruct((rows, columns), jnp.bfloat16),
        compiler_params=params(),
        cost_estimate=cost(8 * rows * columns, 2 * rows * (columns + slot_lanes)),
        name="band",
    )(h_slots, h_strips)


def product(band_ref, here_ref, first_ref, second_ref=None):
    depth = here_ref.shape[0]
    total = jnp.dot(band_ref[:, depth:2 * depth], here_ref[...], preferred_element_type=jnp.float32)
    total += jnp.dot(band_ref[:, side_columns(depth, 0)], first_ref[...], preferred_element_type=jnp.float32)
    if second_ref is not None:
        total += jnp.dot(band_ref[:, side_columns(depth, 1)], second_ref[...], preferred_element_type=jnp.float32)
    return total


def kept(mask_ref, block_row, first, block, width):
    column = lax.broadcasted_iota(jnp.int32, (block, width), 1) // block
    row = jnp.zeros((block, width), jnp.int32)
    for c in range(width // block):
        row = jnp.where(column == c, mask_ref[block_row, first + c], row)
    return row != 0


def masked(start, mask_ref, term):
    rows, width = term.shape
    block = rows // mask_ref.shape[0]
    for i in range(rows // block):
        at = slice(i * block, (i + 1) * block)
        yield at, jnp.where(kept(mask_ref, i, start // block, block, width), term[at], 0.0)


def rows_of(slots, block):
    return slots // 2 * block


def half_mask_sum(mask_ref, columns):
    total = jnp.int32(0)
    for i in range(mask_ref.shape[0]):
        for c in columns:
            total += mask_ref[i, c]
    return total


def swapped(value, block):
    return jnp.concatenate([value[:, block:], value[:, :block]], axis=1)


def mid_kernel(half, slots, mask_ref, band_ref, here_ref, second_ref, first_ref, prev_ref, *rest):
    rows, width = here_ref.shape
    block = rows // mask_ref.shape[0]
    wide = width // block
    if half == 0:
        mid_ref, dense_ref, sent_ref, left_ref, packed = rest[-5:]
        packed[...] = jnp.zeros_like(packed)
        slot = jnp.int32(0)
    else:
        left_ref = rest[0]
        mid_ref, dense_ref, sent_ref, later_ref, spare_ref, packed = rest[-6:]
        packed[...] = jnp.zeros_like(packed)
        packed[:left_ref.shape[0], :] = left_ref[...]
        slot = jnp.maximum(half_mask_sum(mask_ref, range(wide)) - slots[0], 0)
    total = product(band_ref, here_ref, first_ref, second_ref)
    start = half * width
    term = 2.0 * total - prev_ref[:, start:start + width]
    side = lax.broadcasted_iota(jnp.int32, (block, LANES), 1) // block
    for i, (at, value) in enumerate(masked(start, mask_ref, term)):
        mid_ref[at, :] = value
        dense_ref[at, :] = value.astype(jnp.bfloat16)
        for group in range(width // LANES):
            straight = value[:, group * LANES:(group + 1) * LANES]
            turned = swapped(straight, block)
            for h in range(LANES // block):
                odd = slot % 2
                piece = jnp.where(side == odd, jnp.where(odd == h, straight, turned), 0.0)
                packed[pl.ds(pl.multiple_of(slot // 2 * block, block), block), :] += piece.astype(jnp.bfloat16)
                slot = slot + mask_ref[i, start // block + group * (LANES // block) + h]
    cut = 0
    for out_ref in ((sent_ref, left_ref) if half == 0 else (sent_ref, later_ref, spare_ref)):
        out_ref[...] = packed[cut:cut + out_ref.shape[0], :]
        cut += out_ref.shape[0]


def mid_part(half, slots, mask, band, here, first, second, prev, after):
    rows, width = here.shape
    block = rows // mask.shape[0]
    lists = [slots[0], sum(slots) // 2 - slots[0]] if half == 0 else list(slots[1:])
    packed = [jax.ShapeDtypeStruct((rows_of(count, block), LANES), jnp.bfloat16) for count in lists]
    return pl.pallas_call(
        functools.partial(mid_kernel, half, slots),
        in_specs=[SMEM] + [VMEM] * (5 + len(after)),
        out_specs=[VMEM] * (2 + len(packed)),
        out_shape=[
            jax.ShapeDtypeStruct(here.shape, jnp.float32), jax.ShapeDtypeStruct(here.shape, jnp.bfloat16)] + packed,
        scratch_shapes=[pltpu.VMEM((rows_of(sum(lists), block), LANES), jnp.bfloat16)],
        compiler_params=params(),
        cost_estimate=cost(6 * rows * rows * width, 6 * rows * rows + 20 * rows * width),
        name="mid_part",
    )(mask, band, here, second, first, prev, *after)


def unpacked(half, slots, mask_ref, list_refs, gathered, dense):
    rows, width = dense.shape
    block = rows // mask_ref.shape[0]
    wide = width // block
    cut = 0
    for list_ref in list_refs:
        size = min(list_ref.shape[0], gathered.shape[0] - cut)
        gathered[cut:cut + size, :] = list_ref[:size, :]
        cut += size
    slot = jnp.int32(0) if half == 0 else jnp.maximum(half_mask_sum(mask_ref, range(wide)) - slots[0], 0)
    side = lax.broadcasted_iota(jnp.int32, (block, LANES), 1) // block
    for i in range(rows // block):
        for group in range(width // LANES):
            value = jnp.zeros((block, LANES), jnp.float32)
            for h in range(LANES // block):
                held = gathered[pl.ds(pl.multiple_of(slot // 2 * block, block), block), :].astype(jnp.float32)
                keep = mask_ref[i, half * wide + group * (LANES // block) + h]
                piece = jnp.where(slot % 2 == h, held, swapped(held, block))
                value = jnp.where((side == h) & (keep != 0), piece, value)
                slot = slot + keep
            dense[i * block:(i + 1) * block, group * LANES:(group + 1) * LANES] = value.astype(jnp.bfloat16)


def next_kernel(slots, mask_ref, first_mask_ref, second_mask_ref, coeffs_ref, band_ref, here_ref, sent_first_ref,
                later_first_ref, sent_second_ref, later_second_ref, now_ref, mid_ref, other_mid_ref, *rest):
    next_ref, density_ref, out_ref, gathered, dense_first, dense_second, sems = rest[-7:]
    width = here_ref.shape[1]
    copies = []
    for p, held in enumerate((mid_ref, other_mid_ref)):
        copies.append(pltpu.make_async_copy(held, out_ref.at[:, pl.ds(p * width, width)], sems.at[p]))
        copies[-1].start()
    unpacked(0, slots, first_mask_ref, (sent_first_ref, later_first_ref), gathered, dense_first)
    unpacked(0, slots, second_mask_ref, (sent_second_ref, later_second_ref), gathered, dense_second)
    term = 2.0 * product(band_ref, here_ref, dense_first, dense_second) - now_ref[:, :width]
    for at, value in masked(0, mask_ref, term):
        next_ref[at, :] = value
        density_ref[at, :] = coeffs_ref[0] * mid_ref[at, :] + coeffs_ref[1] * value
    for copy in copies:
        copy.wait()


def next_part(slots, mask, masks, coeffs, band, here, lists, now, mids):
    rows, width = here.shape
    block = rows // mask.shape[0]
    half_rows = rows_of(sum(slots) // 2, block)
    return pl.pallas_call(
        functools.partial(next_kernel, slots),
        in_specs=[SMEM] * 4 + [VMEM] * (5 + len(lists)),
        out_specs=[VMEM] * 2 + [HBM],
        out_shape=[jax.ShapeDtypeStruct(here.shape, jnp.float32)] * 2 + [jax.ShapeDtypeStruct(now.shape, jnp.float32)],
        scratch_shapes=[
            pltpu.VMEM((half_rows, LANES), jnp.bfloat16), pltpu.VMEM(here.shape, jnp.bfloat16),
            pltpu.VMEM(here.shape, jnp.bfloat16), pltpu.SemaphoreType.DMA((2,))],
        compiler_params=params(),
        cost_estimate=cost(6 * rows * rows * width, 6 * rows * rows + 40 * rows * width),
        name="next_part",
    )(mask, *masks, coeffs, band, here, *lists, now, *mids)


def begun_kernel(slots, mask_ref, band_ref, here_ref, sent_ref, later_ref, spare_ref, now_ref, held_next_ref,
                 held_density_ref, *rest):
    next_ref, density_ref, sums_ref, gathered, dense, sems = rest[-6:]
    width = here_ref.shape[1]
    copies = []
    for held, out_ref in ((held_next_ref, next_ref), (held_density_ref, density_ref)):
        copies.append(pltpu.make_async_copy(held, out_ref.at[:, pl.ds(0, width)], sems.at[len(copies)]))
        copies[-1].start()
    unpacked(1, slots, mask_ref, (sent_ref, later_ref, spare_ref), gathered, dense)
    sums_ref[...] = 2.0 * product(band_ref, here_ref, dense) - now_ref[:, width:2 * width]
    for copy in copies:
        copy.wait()


def begun_part(slots, mask, band, here, lists, now, helds):
    rows, width = here.shape
    block = rows // mask.shape[0]
    return pl.pallas_call(
        functools.partial(begun_kernel, slots),
        in_specs=[SMEM] + [VMEM] * (5 + len(lists)),
        out_specs=[HBM] * 2 + [VMEM],
        out_shape=[jax.ShapeDtypeStruct(now.shape, jnp.float32)] * 2 + [jax.ShapeDtypeStruct(here.shape, jnp.float32)],
        scratch_shapes=[
            pltpu.VMEM((rows_of(sum(slots[1:]), block), LANES), jnp.bfloat16), pltpu.VMEM(here.shape, jnp.bfloat16),
            pltpu.SemaphoreType.DMA((2,))],
        compiler_params=params(),
        cost_estimate=cost(4 * rows * rows * width, 4 * rows * rows + 20 * rows * width),
        name="begun_part",
    )(mask, band, here, *lists, now, *helds)


def last_kernel(slots, mask_ref, side_mask_ref, coeffs_ref, band_ref, sent_ref, later_ref, spare_ref, sums_ref, mid_ref,
                *rest):
    next_ref, density_ref, gathered, dense, held_next, held_density, sems = rest[-7:]
    unpacked(1, slots, side_mask_ref, (sent_ref, later_ref, spare_ref), gathered, dense)
    rows, width = dense.shape
    block = rows // mask_ref.shape[0]
    step = rows // CHUNKS
    copies = []
    for c in range(CHUNKS):
        total = jnp.dot(
            band_ref[c * step:(c + 1) * step, side_columns(rows, 1)], dense[...], preferred_element_type=jnp.float32)
        for i in range(step // block):
            at = slice(c * step + i * block, c * step + (i + 1) * block)
            keep = kept(mask_ref, c * (step // block) + i, width // block, block, width)
            value = jnp.where(keep, 2.0 * total[i * block:(i + 1) * block] + sums_ref[at, :], 0.0)
            held_next[at, :] = value
            held_density[at, :] = coeffs_ref[0] * mid_ref[at, :] + coeffs_ref[1] * value
        done = pl.ds(c * step, step)
        for held, out_ref in ((held_next, next_ref), (held_density, density_ref)):
            copies.append(pltpu.make_async_copy(
                held.at[done, :], out_ref.at[done, pl.ds(width, width)], sems.at[len(copies)]))
            copies[-1].start()
    for copy in copies:
        copy.wait()


def last_part(slots, mask, side_mask, coeffs, band, lists, sums, mid, outs):
    rows, width = sums.shape
    block = rows // mask.shape[0]
    operands = [mask, side_mask, coeffs, band, *lists, sums, mid, *outs]
    return pl.pallas_call(
        functools.partial(last_kernel, slots),
        in_specs=[SMEM] * 3 + [VMEM] * (3 + len(lists)) + [HBM] * 2,
        out_specs=[HBM] * 2,
        out_shape=[jax.ShapeDtypeStruct(out.shape, jnp.float32) for out in outs],
        scratch_shapes=[
            pltpu.VMEM((rows_of(sum(slots[1:]), block), LANES), jnp.bfloat16),
            pltpu.VMEM((rows, width), jnp.bfloat16), pltpu.VMEM((rows, width), jnp.float32),
            pltpu.VMEM((rows, width), jnp.float32), pltpu.SemaphoreType.DMA((2 * CHUNKS,))],
        input_output_aliases={len(operands) - 2: 0, len(operands) - 1: 1},
        compiler_params=params(),
        cost_estimate=cost(2 * rows * rows * width, 2 * rows * rows + 24 * rows * width),
        name="last_part",
    )(*operands)


def neighbour_masks(t_mask, slots):
    axes = ("grp", "row", "col", "rep")
    masks = lax.all_gather(t_mask, axes)
    wide = t_mask.shape[1] // 2
    early = jnp.sum(masks[:, :, :wide], axis=(1, 2))
    late = jnp.sum(masks[:, :, wide:], axis=(1, 2))
    crowded = jnp.max(jnp.maximum(early, slots[0]) + late) > sum(slots[:3])
    rows = lax.axis_size("row")
    inner = lax.axis_size("col") * lax.axis_size("rep")
    row, rest = lax.axis_index("row"), lax.axis_index("col") * lax.axis_size("rep") + lax.axis_index("rep")
    found = []
    for turn in (-1, 1):
        at = (lax.axis_index("grp") * rows + (row + turn) % rows) * inner + rest
        found.append(lax.dynamic_index_in_dim(masks, at, keepdims=False))
    return found, crowded


def local(h_strips, h_slots, t_prev, t_now, t_mask, coeffs):
    slots = slots_of(t_mask.size)
    width = t_now.shape[1] // 2
    low = t_now[:, :width].astype(jnp.bfloat16)
    low, t_now, t_prev, h_strips = lax.optimization_barrier((low, t_now, t_prev, h_strips))
    (high,) = rounded(t_now, [(width, width)])
    masks, crowded = neighbour_masks(t_mask, slots)
    band = banded(h_slots, h_strips)
    low_sides, high_sides = both_sides(low), both_sides(high)
    mid_low, dense_low, sent_low, left = mid_part(0, slots, t_mask, band, low, *low_sides, t_prev, [])
    first_low, second_low = both_sides(sent_low)
    mid_high, dense_high, sent, later, spare = mid_part(1, slots, t_mask, band, high, *high_sides, t_prev, [left])
    first_sent, second_sent = both_sides(sent)
    first_later, second_later = both_sides(later)
    first_spare, second_spare = lax.cond(
        crowded, both_sides, lambda block: (jnp.zeros_like(block), jnp.zeros_like(block)), spare)
    next_low, density_low, t_mid = next_part(
        slots, t_mask, masks, coeffs, band, dense_low, [first_low, first_sent, second_low, second_sent], t_now,
        [mid_low, mid_high])
    *outs, sums = begun_part(
        slots, masks[0], band, dense_high, [first_sent, first_later, first_spare], t_now, [next_low, density_low])
    outs = last_part(
        slots, t_mask, masks[1], coeffs, band, [second_sent, second_later, second_spare], sums, mid_high, outs)
    return (t_mid, outs[0], outs[1])


def solution(mesh):
    panel = P(("grp", "row"), ("col", "rep"))
    return jax.shard_map(
        local,
        mesh=mesh,
        in_specs=(P(("grp", "row"), None, None), P(("grp", "row"), None), panel, panel, panel, P()),
        out_specs=(panel, panel, panel),
        check_vma=False,
    )
```

```python
import functools

import jax
import jax.numpy as jnp
from jax import lax
from jax.experimental import pallas as pl
from jax.experimental.pallas import tpu as pltpu
from jax.sharding import PartitionSpec as P

LANES = 128
CHUNKS = 2
MIB = 1024 * 1024

SMEM = pl.BlockSpec(memory_space=pltpu.SMEM)
VMEM = pl.BlockSpec(memory_space=pltpu.VMEM)
ANY = pl.BlockSpec(memory_space=pl.ANY)
HBM = pl.BlockSpec(memory_space=pltpu.HBM)


def spans_of(columns):
    if columns % (4 * LANES):
        ones = [(start, LANES) for start in range(0, columns, LANES)]
        return ones, ones
    half, quarter = columns // 2, columns // 4
    return [(0, half), (half, half)], [(0, half), (half, quarter), (half + quarter, quarter)]


def both_sides(block):
    rows, reps = lax.axis_size("row"), lax.axis_size("rep")
    arrived = []
    for turn in (-1, 1):
        route = []
        for row in range(rows):
            for rep in range(reps):
                source = (row + (turn if rep % 2 == 0 else -turn)) % rows
                route.append((source * reps + rep, row * reps + rep))
        arrived.append(lax.ppermute(block, ("row", "rep"), route))
    return tuple(arrived)


def side_columns(depth, order):
    odd = lax.axis_index("rep") % 2
    return pl.ds(pl.multiple_of(jnp.where(odd == order, 0, 2 * depth), LANES), depth)


def params(limit=32 * MIB):
    return pltpu.CompilerParams(vmem_limit_bytes=limit)


def cost(flops, moved):
    return pl.CostEstimate(flops=flops, transcendentals=0, bytes_accessed=moved)


def round_kernel(starts, now_ref, *out_refs):
    for start, out_ref in zip(starts, out_refs):
        out_ref[...] = now_ref[:, start:start + out_ref.shape[1]].astype(jnp.bfloat16)


def rounded(now, spans):
    rows = now.shape[0]
    size = rows * sum(width for _, width in spans)
    return list(pl.pallas_call(
        functools.partial(round_kernel, [start for start, _ in spans]),
        in_specs=[VMEM],
        out_specs=[VMEM] * len(spans),
        out_shape=[jax.ShapeDtypeStruct((rows, width), jnp.bfloat16) for _, width in spans],
        compiler_params=params(),
        cost_estimate=cost(size, 6 * size),
        name="round_part",
    )(now))


def band_kernel(slots_ref, strips_ref, out_ref):
    block_rows, block, slot_lanes = strips_ref.shape
    out_ref[...] = jnp.zeros_like(out_ref)
    half = lax.broadcasted_iota(jnp.int32, (block, LANES), 1) // block

    @pl.loop(0, block_rows)
    def _(row):
        at = pl.ds(pl.multiple_of(row * block, block), block)
        for pair in range(slot_lanes // LANES):
            straight = strips_ref[row, :, pair * LANES:(pair + 1) * LANES].astype(jnp.float32)
            swapped = jnp.concatenate([straight[:, block:], straight[:, :block]], axis=1)
            for side in range(2):
                target = slots_ref[row, 2 * pair + side]
                odd = target % 2
                value = jnp.where(odd == side, straight, swapped)
                value = jnp.where(half == odd, value, 0.0).astype(jnp.bfloat16)
                lanes = pl.ds(pl.multiple_of((target // 2) * LANES, LANES), LANES)
                out_ref[at, lanes] += value


def banded(h_slots, h_strips):
    block_rows, block, slot_lanes = h_strips.shape
    rows, columns = block_rows * block, 3 * block_rows * block
    return pl.pallas_call(
        band_kernel,
        in_specs=[SMEM, VMEM],
        out_specs=VMEM,
        out_shape=jax.ShapeDtypeStruct((rows, columns), jnp.bfloat16),
        compiler_params=params(),
        cost_estimate=cost(8 * rows * columns, 2 * rows * (columns + slot_lanes)),
        name="band",
    )(h_slots, h_strips)


def product(band_ref, here_ref, first_ref, second_ref=None):
    depth = here_ref.shape[0]
    total = jnp.dot(band_ref[:, depth:2 * depth], here_ref[...], preferred_element_type=jnp.float32)
    total += jnp.dot(band_ref[:, side_columns(depth, 0)], first_ref[...], preferred_element_type=jnp.float32)
    if second_ref is not None:
        total += jnp.dot(band_ref[:, side_columns(depth, 1)], second_ref[...], preferred_element_type=jnp.float32)
    return total


def kept(mask_ref, block_row, first, block, width):
    column = lax.broadcasted_iota(jnp.int32, (block, width), 1) // block
    row = jnp.zeros((block, width), jnp.int32)
    for c in range(width // block):
        row = jnp.where(column == c, mask_ref[block_row, first + c], row)
    return row != 0


def masked(start, mask_ref, term):
    rows, width = term.shape
    block = rows // mask_ref.shape[0]
    for i in range(rows // block):
        at = slice(i * block, (i + 1) * block)
        yield at, jnp.where(kept(mask_ref, i, start // block, block, width), term[at], 0.0)


def writes(jobs, sems):
    copies = []
    for held, out_ref, start in jobs:
        columns = pl.ds(start, held.shape[1])
        copies.append(pltpu.make_async_copy(held, out_ref.at[:, columns], sems.at[len(copies)]))
        copies[-1].start()
    return copies


def mid_kernel(start, pieces, mask_ref, band_ref, here_ref, second_ref, first_ref, prev_ref, *rest):
    mid_ref, round_refs = rest[-pieces - 1], rest[-pieces:]
    total = product(band_ref, here_ref, first_ref, second_ref)
    term = 2.0 * total - prev_ref[:, start:start + here_ref.shape[1]]
    for at, value in masked(start, mask_ref, term):
        mid_ref[at, :] = value
        from_column = 0
        for round_ref in round_refs:
            to_column = from_column + round_ref.shape[1]
            round_ref[at, :] = value[:, from_column:to_column].astype(jnp.bfloat16)
            from_column = to_column


def mid_part(span, widths, mask, band, here, first, second, prev, after):
    rows, width = here.shape
    return pl.pallas_call(
        functools.partial(mid_kernel, span[0], len(widths)),
        in_specs=[SMEM] + [VMEM] * 5 + [ANY] * len(after),
        out_specs=[VMEM] * (1 + len(widths)),
        out_shape=[jax.ShapeDtypeStruct(here.shape, jnp.float32)]
        + [jax.ShapeDtypeStruct((rows, piece), jnp.bfloat16) for piece in widths],
        compiler_params=params(),
        cost_estimate=cost(6 * rows * rows * width, 6 * rows * rows + 16 * rows * width),
        name="mid_part",
    )(mask, band, here, second, first, prev, *after)


def next_kernel(start, mid_start, places, panels, unread, mask_ref, coeffs_ref, band_ref, here_ref, second_ref, first_ref, now_ref,
                mid_ref, *rest):
    rest = rest[unread:]
    held_refs, rest = rest[:len(places)], rest[len(places):]
    next_ref, density_ref, sems = rest[-panels - 3], rest[-panels - 2], rest[-1]
    out_refs = rest[-panels - 1:-1]
    copies = writes([(held, out_refs[o], at) for held, (o, at) in zip(held_refs, places)], sems)
    total = product(band_ref, here_ref, first_ref, second_ref)
    term = 2.0 * total - now_ref[:, start:start + here_ref.shape[1]]
    for at, value in masked(start, mask_ref, term):
        next_ref[at, :] = value
        mid = mid_ref[at, mid_start:mid_start + here_ref.shape[1]]
        density_ref[at, :] = coeffs_ref[0] * mid + coeffs_ref[1] * value
    for copy in copies:
        copy.wait()


def begun_kernel(start, band_ref, here_ref, first_ref, now_ref, *rest):
    sums_ref = rest[-1]
    sums_ref[...] = 2.0 * product(band_ref, here_ref, first_ref) - now_ref[:, start:start + here_ref.shape[1]]


def with_writes(kernel, specs, operands, out_shapes, moves, panels, whole, outs, flops, name):
    held = [part for part, _ in moves]
    places = [place for _, place in moves]
    moved = sum(part.size for part in held)
    aliases = {}
    operands, specs = operands + held, specs + [VMEM] * len(held)
    if outs is not None:
        aliases = {len(operands) + o: len(out_shapes) + o for o in range(panels)}
        operands, specs = operands + list(outs), specs + [HBM] * panels
    results = pl.pallas_call(
        functools.partial(kernel, places),
        in_specs=specs,
        out_specs=[VMEM] * len(out_shapes) + [HBM] * panels,
        out_shape=out_shapes + [jax.ShapeDtypeStruct(whole, jnp.float32)] * panels,
        scratch_shapes=[pltpu.SemaphoreType.DMA((max(len(held), 1),))],
        input_output_aliases=aliases,
        compiler_params=params(),
        cost_estimate=cost(flops, 4 * moved + flops // 200),
        name=name,
    )(*operands)
    return results[:len(out_shapes)], tuple(results[len(out_shapes):])


def next_part(span, mid_start, mask, coeffs, band, here, first, second, now, mid, after, moves, panels):
    rows, width = here.shape
    return with_writes(
        lambda places, *refs: next_kernel(span[0], mid_start, places, panels, len(after), *refs),
        [SMEM] * 2 + [VMEM] * 6 + [ANY] * len(after), [mask, coeffs, band, here, second, first, now, mid, *after],
        [jax.ShapeDtypeStruct(here.shape, jnp.float32)] * 2, moves, panels, now.shape, None,
        6 * rows * rows * width, "next_part")


def begun_part(span, band, here, first, now, after):
    rows, width = here.shape
    return pl.pallas_call(
        functools.partial(begun_kernel, span[0]),
        in_specs=[VMEM] * 4 + [ANY] * len(after),
        out_specs=VMEM,
        out_shape=jax.ShapeDtypeStruct(here.shape, jnp.float32),
        compiler_params=params(),
        cost_estimate=cost(4 * rows * rows * width, 4 * rows * rows + 12 * rows * width),
        name="begun_part",
    )(band, here, first, now, *after)


def last_kernel(start, mid_start, places, mask_ref, coeffs_ref, band_ref, second_ref, sums_ref, mid_ref, *rest):
    held_refs = rest[:len(places)]
    next_ref, density_ref, held_next, held_density, early_sems, sems = rest[-6:]
    copies = writes([(held, (next_ref, density_ref)[o], at) for held, (o, at) in zip(held_refs, places)], early_sems)
    early = len(copies)
    rows, width = second_ref.shape
    block = rows // mask_ref.shape[0]
    step = rows // CHUNKS
    for c in range(CHUNKS):
        total = jnp.dot(
            band_ref[c * step:(c + 1) * step, side_columns(rows, 1)], second_ref[...],
            preferred_element_type=jnp.float32)
        for i in range(step // block):
            at = slice(c * step + i * block, c * step + (i + 1) * block)
            keep = kept(mask_ref, c * (step // block) + i, start // block, block, width)
            value = jnp.where(keep, 2.0 * total[i * block:(i + 1) * block] + sums_ref[at, :], 0.0)
            held_next[at, :] = value
            density = coeffs_ref[0] * mid_ref[at, mid_start:mid_start + width] + coeffs_ref[1] * value
            held_density[at, :] = density
        done = pl.ds(c * step, step)
        for held, out_ref in ((held_next, next_ref), (held_density, density_ref)):
            copies.append(pltpu.make_async_copy(
                held.at[done, :], out_ref.at[done, pl.ds(start, width)], sems.at[len(copies) - early]))
            copies[-1].start()
    for copy in copies:
        copy.wait()


def last_part(span, mid_start, mask, coeffs, band, second, sums, mid, moves, outs):
    rows, width = second.shape
    held = [part for part, _ in moves]
    return pl.pallas_call(
        functools.partial(last_kernel, span[0], mid_start, [place for _, place in moves]),
        in_specs=[SMEM] * 2 + [VMEM] * (4 + len(held)) + [HBM] * 2,
        out_specs=[HBM] * 2,
        out_shape=[jax.ShapeDtypeStruct(out.shape, jnp.float32) for out in outs],
        scratch_shapes=[pltpu.VMEM((rows, width), jnp.float32)] * 2
        + [pltpu.SemaphoreType.DMA((max(len(held), 1),)), pltpu.SemaphoreType.DMA((2 * CHUNKS,))],
        input_output_aliases={6 + len(held): 0, 7 + len(held): 1},
        compiler_params=params(),
        cost_estimate=cost(2 * rows * rows * width, 2 * rows * rows + 22 * rows * width),
        name="last_part",
    )(mask, coeffs, band, second, sums, mid, *held, *outs)


def local(h_strips, h_slots, t_prev, t_now, t_mask, coeffs):
    spans, spans_next = spans_of(t_now.shape[1])
    start, width = spans[0]
    here = [t_now[:, start:start + width].astype(jnp.bfloat16)]
    here[0], t_now, t_prev, h_strips = lax.optimization_barrier((here[0], t_now, t_prev, h_strips))
    here += rounded(t_now, spans[1:])
    band = banded(h_slots, h_strips)
    sides = [both_sides(block) for block in here]
    mids, here_mid, sides_mid, origin = [], [], [], []
    for part, (start, width) in enumerate(spans):
        inside = [span for span in spans_next if start <= span[0] < start + width]
        mid, *lows = mid_part(
            spans[part], [piece for _, piece in inside], t_mask, band, here[part], *sides[part], t_prev, mids[-1:])
        mids.append(mid)
        here_mid += lows
        sides_mid += [both_sides(low) for low in lows]
        origin += [(part, span[0] - start) for span in inside]
    t_mid, outs, waiting, after = None, None, [], []
    last = len(spans_next) - 1
    for part, span in enumerate(spans_next[:-1]):
        panels, moves = 0, []
        if part == 0:
            panels, moves = 1, [(mid, (0, spans[p][0])) for p, mid in enumerate(mids)]
        elif part == last - 1:
            panels, moves, waiting = 2, waiting, []
        source, mid_start = origin[part]
        (term, density), written = next_part(
            span, mid_start, t_mask, coeffs, band, here_mid[part], *sides_mid[part], t_now, mids[source], after,
            moves, panels)
        after = [term]
        if part == 0:
            t_mid = written[0]
        elif part == last - 1:
            outs = written
        waiting = waiting + [(term, (0, span[0])), (density, (1, span[0]))]
    first, second = sides_mid[last]
    source, mid_start = origin[last]
    sums = begun_part(spans_next[last], band, here_mid[last], first, t_now, after)
    outs = last_part(spans_next[last], mid_start, t_mask, coeffs, band, second, sums, mids[source], waiting, outs)
    return (t_mid, outs[0], outs[1])


def solution(mesh):
    panel = P(("grp", "row"), ("col", "rep"))
    return jax.shard_map(
        local,
        mesh=mesh,
        in_specs=(P(("grp", "row"), None, None), P(("grp", "row"), None), panel, panel, panel, P()),
        out_specs=(panel, panel, panel),
        check_vma=False,
    )
```

```python
import functools

import jax
import jax.numpy as jnp
from jax import lax
from jax.experimental import pallas as pl
from jax.experimental.pallas import tpu as pltpu
from jax.sharding import PartitionSpec as P

LANES = 128
CHUNKS = 2
MIB = 1024 * 1024

SMEM = pl.BlockSpec(memory_space=pltpu.SMEM)
VMEM = pl.BlockSpec(memory_space=pltpu.VMEM)
ANY = pl.BlockSpec(memory_space=pl.ANY)
HBM = pl.BlockSpec(memory_space=pltpu.HBM)


def both_sides(block):
    rows, reps = lax.axis_size("row"), lax.axis_size("rep")
    arrived = []
    for turn in (-1, 1):
        route = []
        for row in range(rows):
            for rep in range(reps):
                source = (row + (turn if rep % 2 == 0 else -turn)) % rows
                route.append((source * reps + rep, row * reps + rep))
        arrived.append(lax.ppermute(block, ("row", "rep"), route))
    return tuple(arrived)


def side_columns(depth, order):
    odd = lax.axis_index("rep") % 2
    return pl.ds(pl.multiple_of(jnp.where(odd == order, 0, 2 * depth), LANES), depth)


def params(limit=32 * MIB):
    return pltpu.CompilerParams(vmem_limit_bytes=limit)


def cost(flops, moved):
    return pl.CostEstimate(flops=flops, transcendentals=0, bytes_accessed=moved)


def round_kernel(starts, now_ref, *out_refs):
    for start, out_ref in zip(starts, out_refs):
        out_ref[...] = now_ref[:, start:start + out_ref.shape[1]].astype(jnp.bfloat16)


def rounded(now, spans):
    rows = now.shape[0]
    size = rows * sum(width for _, width in spans)
    return list(pl.pallas_call(
        functools.partial(round_kernel, [start for start, _ in spans]),
        in_specs=[VMEM],
        out_specs=[VMEM] * len(spans),
        out_shape=[jax.ShapeDtypeStruct((rows, width), jnp.bfloat16) for _, width in spans],
        compiler_params=params(),
        cost_estimate=cost(size, 6 * size),
        name="round_part",
    )(now))


def band_kernel(slots_ref, strips_ref, out_ref):
    block_rows, block, slot_lanes = strips_ref.shape
    out_ref[...] = jnp.zeros_like(out_ref)
    half = lax.broadcasted_iota(jnp.int32, (block, LANES), 1) // block

    @pl.loop(0, block_rows)
    def _(row):
        at = pl.ds(pl.multiple_of(row * block, block), block)
        for pair in range(slot_lanes // LANES):
            straight = strips_ref[row, :, pair * LANES:(pair + 1) * LANES].astype(jnp.float32)
            swapped = jnp.concatenate([straight[:, block:], straight[:, :block]], axis=1)
            for side in range(2):
                target = slots_ref[row, 2 * pair + side]
                odd = target % 2
                value = jnp.where(odd == side, straight, swapped)
                value = jnp.where(half == odd, value, 0.0).astype(jnp.bfloat16)
                lanes = pl.ds(pl.multiple_of((target // 2) * LANES, LANES), LANES)
                out_ref[at, lanes] += value


def banded(h_slots, h_strips):
    block_rows, block, slot_lanes = h_strips.shape
    rows, columns = block_rows * block, 3 * block_rows * block
    return pl.pallas_call(
        band_kernel,
        in_specs=[SMEM, VMEM],
        out_specs=VMEM,
        out_shape=jax.ShapeDtypeStruct((rows, columns), jnp.bfloat16),
        compiler_params=params(),
        cost_estimate=cost(8 * rows * columns, 2 * rows * (columns + slot_lanes)),
        name="band",
    )(h_slots, h_strips)


def product(band_ref, here_ref, first_ref, second_ref=None):
    depth = here_ref.shape[0]
    total = jnp.dot(band_ref[:, depth:2 * depth], here_ref[...], preferred_element_type=jnp.float32)
    total += jnp.dot(band_ref[:, side_columns(depth, 0)], first_ref[...], preferred_element_type=jnp.float32)
    if second_ref is not None:
        total += jnp.dot(band_ref[:, side_columns(depth, 1)], second_ref[...], preferred_element_type=jnp.float32)
    return total


def kept(mask_ref, block_row, first, block, width):
    column = lax.broadcasted_iota(jnp.int32, (block, width), 1) // block
    row = jnp.zeros((block, width), jnp.int32)
    for c in range(width // block):
        row = jnp.where(column == c, mask_ref[block_row, first + c], row)
    return row != 0


def masked(start, mask_ref, term):
    rows, width = term.shape
    block = rows // mask_ref.shape[0]
    for i in range(rows // block):
        at = slice(i * block, (i + 1) * block)
        yield at, jnp.where(kept(mask_ref, i, start // block, block, width), term[at], 0.0)


def start_writes(jobs, sems, first):
    copies = []
    for held, out_ref, at, column in jobs:
        copies.append(pltpu.make_async_copy(
            held.at[at, :], out_ref.at[at, pl.ds(column, held.shape[1])], sems.at[first + len(copies)]))
        copies[-1].start()
    return copies


def mid_kernel(start, mask_ref, band_ref, here_ref, second_ref, first_ref, prev_ref, *rest):
    mid_ref, round_ref = rest[-2:]
    total = product(band_ref, here_ref, first_ref, second_ref)
    term = 2.0 * total - prev_ref[:, start:start + here_ref.shape[1]]
    for at, value in masked(start, mask_ref, term):
        mid_ref[at, :] = value
        round_ref[at, :] = value.astype(jnp.bfloat16)


def mid_part(span, mask, band, here, first, second, prev, after):
    rows, width = here.shape
    return pl.pallas_call(
        functools.partial(mid_kernel, span[0]),
        in_specs=[SMEM] + [VMEM] * 5 + [ANY] * len(after),
        out_specs=[VMEM] * 2,
        out_shape=[jax.ShapeDtypeStruct(here.shape, jnp.float32), jax.ShapeDtypeStruct(here.shape, jnp.bfloat16)],
        compiler_params=params(),
        cost_estimate=cost(6 * rows * rows * width, 6 * rows * rows + 16 * rows * width),
        name="mid_part",
    )(mask, band, here, second, first, prev, *after)


def next_kernel(mask_ref, coeffs_ref, band_ref, here_ref, second_ref, first_ref, now_ref, mid_ref, other_mid_ref,
                t_mid_ref, next_ref, density_ref, token_ref, held_next, held_density, sems):
    rows, width = here_ref.shape
    block = rows // mask_ref.shape[0]
    everything = pl.ds(0, rows)
    token_ref[...] = jnp.zeros_like(token_ref)
    copies = start_writes(
        [(mid_ref, t_mid_ref, everything, 0), (other_mid_ref, t_mid_ref, everything, width)], sems, 0)
    term = 2.0 * product(band_ref, here_ref, first_ref, second_ref) - now_ref[:, :width]
    for at, value in masked(0, mask_ref, term):
        held_next[at, :] = value
        held_density[at, :] = coeffs_ref[0] * mid_ref[at, :] + coeffs_ref[1] * value
    copies += start_writes(
        [(held_next, next_ref, everything, 0), (held_density, density_ref, everything, 0)], sems, len(copies))
    for copy in copies:
        copy.wait()


def next_part(mask, coeffs, band, here, first, second, now, mids):
    rows, width = here.shape
    return pl.pallas_call(
        next_kernel,
        in_specs=[SMEM] * 2 + [VMEM] * 7,
        out_specs=[HBM] * 3 + [VMEM],
        out_shape=[jax.ShapeDtypeStruct(now.shape, jnp.float32)] * 3 + [jax.ShapeDtypeStruct((8, LANES), jnp.float32)],
        scratch_shapes=[pltpu.VMEM(here.shape, jnp.float32)] * 2 + [pltpu.SemaphoreType.DMA((4,))],
        compiler_params=params(),
        cost_estimate=cost(6 * rows * rows * width, 6 * rows * rows + 30 * rows * width),
        name="next_part",
    )(mask, coeffs, band, here, second, first, now, *mids)


def begun_kernel(start, band_ref, here_ref, first_ref, now_ref, *rest):
    sums_ref = rest[-1]
    sums_ref[...] = 2.0 * product(band_ref, here_ref, first_ref) - now_ref[:, start:start + here_ref.shape[1]]


def begun_part(span, band, here, first, now, after):
    rows, width = here.shape
    return pl.pallas_call(
        functools.partial(begun_kernel, span[0]),
        in_specs=[VMEM] * 4 + [ANY] * len(after),
        out_specs=VMEM,
        out_shape=jax.ShapeDtypeStruct(here.shape, jnp.float32),
        compiler_params=params(),
        cost_estimate=cost(4 * rows * rows * width, 4 * rows * rows + 12 * rows * width),
        name="begun_part",
    )(band, here, first, now, *after)


def last_kernel(mask_ref, coeffs_ref, band_ref, second_ref, sums_ref, mid_ref, *rest):
    next_ref, density_ref, held_next, held_density, sems = rest[-5:]
    rows, width = second_ref.shape
    block = rows // mask_ref.shape[0]
    step = rows // CHUNKS
    copies = []
    for c in range(CHUNKS):
        total = jnp.dot(
            band_ref[c * step:(c + 1) * step, side_columns(rows, 1)], second_ref[...],
            preferred_element_type=jnp.float32)
        for i in range(step // block):
            at = slice(c * step + i * block, c * step + (i + 1) * block)
            keep = kept(mask_ref, c * (step // block) + i, width // block, block, width)
            value = jnp.where(keep, 2.0 * total[i * block:(i + 1) * block] + sums_ref[at, :], 0.0)
            held_next[at, :] = value
            held_density[at, :] = coeffs_ref[0] * mid_ref[at, :] + coeffs_ref[1] * value
        done = pl.ds(c * step, step)
        copies += start_writes(
            [(held_next, next_ref, done, width), (held_density, density_ref, done, width)], sems, len(copies))
    for copy in copies:
        copy.wait()


def last_part(mask, coeffs, band, second, sums, mid, outs):
    rows, width = second.shape
    return pl.pallas_call(
        last_kernel,
        in_specs=[SMEM] * 2 + [VMEM] * 4 + [HBM] * 2,
        out_specs=[HBM] * 2,
        out_shape=[jax.ShapeDtypeStruct(out.shape, jnp.float32) for out in outs],
        scratch_shapes=[pltpu.VMEM((rows, width), jnp.float32)] * 2 + [pltpu.SemaphoreType.DMA((2 * CHUNKS,))],
        input_output_aliases={6: 0, 7: 1},
        compiler_params=params(),
        cost_estimate=cost(2 * rows * rows * width, 2 * rows * rows + 22 * rows * width),
        name="last_part",
    )(mask, coeffs, band, second, sums, mid, *outs)


def local(h_strips, h_slots, t_prev, t_now, t_mask, coeffs):
    width = t_now.shape[1] // 2
    low = t_now[:, :width].astype(jnp.bfloat16)
    low, t_now, t_prev, h_strips = lax.optimization_barrier((low, t_now, t_prev, h_strips))
    (high,) = rounded(t_now, [(width, width)])
    band = banded(h_slots, h_strips)
    low_sides, high_sides = both_sides(low), both_sides(high)
    mid_low, low_again = mid_part((0, width), t_mask, band, low, *low_sides, t_prev, [])
    low_sides = both_sides(low_again)
    mid_high, high_again = mid_part((width, width), t_mask, band, high, *high_sides, t_prev, [mid_low])
    first, second = both_sides(high_again)
    t_mid, *outs, token = next_part(t_mask, coeffs, band, low_again, *low_sides, t_now, [mid_low, mid_high])
    sums = begun_part((width, width), band, high_again, first, t_now, [token])
    outs = last_part(t_mask, coeffs, band, second, sums, mid_high, outs)
    return (t_mid, outs[0], outs[1])


def solution(mesh):
    panel = P(("grp", "row"), ("col", "rep"))
    return jax.shard_map(
        local,
        mesh=mesh,
        in_specs=(P(("grp", "row"), None, None), P(("grp", "row"), None), panel, panel, panel, P()),
        out_specs=(panel, panel, panel),
        check_vma=False,
    )
```

```python
import functools

import jax
import jax.numpy as jnp
from jax import lax
from jax.experimental import pallas as pl
from jax.experimental.pallas import tpu as pltpu
from jax.sharding import PartitionSpec as P

LANES = 128
CHUNKS = 2
MIB = 1024 * 1024

SMEM = pl.BlockSpec(memory_space=pltpu.SMEM)
VMEM = pl.BlockSpec(memory_space=pltpu.VMEM)
ANY = pl.BlockSpec(memory_space=pl.ANY)
HBM = pl.BlockSpec(memory_space=pltpu.HBM)


def from_side(block, order, mixed):
    rows, reps = lax.axis_size("row"), lax.axis_size("rep")
    route = []
    for row in range(rows):
        for rep in range(reps):
            turn = 1 if order == (mixed and rep % 2) else -1
            source = (row - turn) % rows
            route.append((source * reps + rep, row * reps + rep))
    return lax.ppermute(block, ("row", "rep"), route)


def both_sides(block):
    return tuple(from_side(block, order, True) for order in (0, 1))


def side_columns(depth, order, mixed):
    if not mixed:
        return pl.ds(2 * depth * order, depth)
    odd = lax.axis_index("rep") % 2
    return pl.ds(pl.multiple_of(jnp.where(odd == order, 0, 2 * depth), LANES), depth)


def params(limit=32 * MIB):
    return pltpu.CompilerParams(vmem_limit_bytes=limit)


def cost(flops, moved):
    return pl.CostEstimate(flops=flops, transcendentals=0, bytes_accessed=moved)


def round_kernel(starts, now_ref, *out_refs):
    for start, out_ref in zip(starts, out_refs):
        out_ref[...] = now_ref[:, start:start + out_ref.shape[1]].astype(jnp.bfloat16)


def rounded(now, spans):
    rows = now.shape[0]
    size = rows * sum(width for _, width in spans)
    return list(pl.pallas_call(
        functools.partial(round_kernel, [start for start, _ in spans]),
        in_specs=[VMEM],
        out_specs=[VMEM] * len(spans),
        out_shape=[jax.ShapeDtypeStruct((rows, width), jnp.bfloat16) for _, width in spans],
        compiler_params=params(),
        cost_estimate=cost(size, 6 * size),
        name="round_part",
    )(now))


def band_kernel(slots_ref, strips_ref, out_ref):
    block_rows, block, slot_lanes = strips_ref.shape
    out_ref[...] = jnp.zeros_like(out_ref)
    half = lax.broadcasted_iota(jnp.int32, (block, LANES), 1) // block

    @pl.loop(0, block_rows)
    def _(row):
        at = pl.ds(pl.multiple_of(row * block, block), block)
        for pair in range(slot_lanes // LANES):
            straight = strips_ref[row, :, pair * LANES:(pair + 1) * LANES].astype(jnp.float32)
            swapped = jnp.concatenate([straight[:, block:], straight[:, :block]], axis=1)
            for side in range(2):
                target = slots_ref[row, 2 * pair + side]
                odd = target % 2
                value = jnp.where(odd == side, straight, swapped)
                value = jnp.where(half == odd, value, 0.0).astype(jnp.bfloat16)
                lanes = pl.ds(pl.multiple_of((target // 2) * LANES, LANES), LANES)
                out_ref[at, lanes] += value


def banded(h_slots, h_strips):
    block_rows, block, slot_lanes = h_strips.shape
    rows, columns = block_rows * block, 3 * block_rows * block
    return pl.pallas_call(
        band_kernel,
        in_specs=[SMEM, VMEM],
        out_specs=VMEM,
        out_shape=jax.ShapeDtypeStruct((rows, columns), jnp.bfloat16),
        compiler_params=params(),
        cost_estimate=cost(8 * rows * columns, 2 * rows * (columns + slot_lanes)),
        name="band",
    )(h_slots, h_strips)


def product(band_ref, here_ref, first_ref, second_ref=None, mixed=True):
    depth = here_ref.shape[0]
    total = jnp.dot(band_ref[:, depth:2 * depth], here_ref[...], preferred_element_type=jnp.float32)
    total += jnp.dot(band_ref[:, side_columns(depth, 0, mixed)], first_ref[...], preferred_element_type=jnp.float32)
    if second_ref is not None:
        total += jnp.dot(band_ref[:, side_columns(depth, 1, mixed)], second_ref[...], preferred_element_type=jnp.float32)
    return total


def kept(mask_ref, block_row, first, block, width):
    column = lax.broadcasted_iota(jnp.int32, (block, width), 1) // block
    row = jnp.zeros((block, width), jnp.int32)
    for c in range(width // block):
        row = jnp.where(column == c, mask_ref[block_row, first + c], row)
    return row != 0


def masked(start, mask_ref, term):
    rows, width = term.shape
    block = rows // mask_ref.shape[0]
    for i in range(rows // block):
        at = slice(i * block, (i + 1) * block)
        yield at, jnp.where(kept(mask_ref, i, start // block, block, width), term[at], 0.0)


def start_writes(jobs, sems, first):
    copies = []
    for held, out_ref, at, column in jobs:
        copies.append(pltpu.make_async_copy(
            held.at[at, :], out_ref.at[at, pl.ds(column, held.shape[1])], sems.at[first + len(copies)]))
        copies[-1].start()
    return copies


def mid_kernel(start, pieces, mask_ref, band_ref, here_ref, second_ref, first_ref, prev_ref, *rest):
    mid_ref, round_refs = rest[-len(pieces) - 1], rest[-len(pieces):]
    total = product(band_ref, here_ref, first_ref, second_ref)
    term = 2.0 * total - prev_ref[:, start:start + here_ref.shape[1]]
    for at, value in masked(start, mask_ref, term):
        mid_ref[at, :] = value
        low = value.astype(jnp.bfloat16)
        for (column, size), round_ref in zip(pieces, round_refs):
            round_ref[at, :] = low[:, column:column + size]


def mid_part(span, pieces, mask, band, here, first, second, prev, after):
    rows, width = here.shape
    return pl.pallas_call(
        functools.partial(mid_kernel, span[0], pieces),
        in_specs=[SMEM] + [VMEM] * 5 + [ANY] * len(after),
        out_specs=[VMEM] * (1 + len(pieces)),
        out_shape=[jax.ShapeDtypeStruct(here.shape, jnp.float32)]
        + [jax.ShapeDtypeStruct((rows, size), jnp.bfloat16) for _, size in pieces],
        compiler_params=params(),
        cost_estimate=cost(6 * rows * rows * width, 6 * rows * rows + 16 * rows * width),
        name="mid_part",
    )(mask, band, here, second, first, prev, *after)


def next_kernel(mask_ref, coeffs_ref, band_ref, here_ref, second_ref, first_ref, now_ref, mid_ref, other_mid_ref,
                t_mid_ref, next_ref, density_ref, token_ref, held_next, held_density, sems):
    rows, width = here_ref.shape
    block = rows // mask_ref.shape[0]
    everything = pl.ds(0, rows)
    token_ref[...] = jnp.zeros_like(token_ref)
    copies = start_writes(
        [(mid_ref, t_mid_ref, everything, 0), (other_mid_ref, t_mid_ref, everything, width)], sems, 0)
    term = 2.0 * product(band_ref, here_ref, first_ref, second_ref) - now_ref[:, :width]
    for at, value in masked(0, mask_ref, term):
        held_next[at, :] = value
        held_density[at, :] = coeffs_ref[0] * mid_ref[at, :] + coeffs_ref[1] * value
    copies += start_writes(
        [(held_next, next_ref, everything, 0), (held_density, density_ref, everything, 0)], sems, len(copies))
    for copy in copies:
        copy.wait()


def next_part(mask, coeffs, band, here, first, second, now, mids):
    rows, width = here.shape
    return pl.pallas_call(
        next_kernel,
        in_specs=[SMEM] * 2 + [VMEM] * 7,
        out_specs=[HBM] * 3 + [VMEM],
        out_shape=[jax.ShapeDtypeStruct(now.shape, jnp.float32)] * 3 + [jax.ShapeDtypeStruct((8, LANES), jnp.float32)],
        scratch_shapes=[pltpu.VMEM(here.shape, jnp.float32)] * 2 + [pltpu.SemaphoreType.DMA((4,))],
        compiler_params=params(),
        cost_estimate=cost(6 * rows * rows * width, 6 * rows * rows + 30 * rows * width),
        name="next_part",
    )(mask, coeffs, band, here, second, first, now, *mids)


def begun_kernel(start, band_ref, here_ref, first_ref, now_ref, *rest):
    sums_ref = rest[-1]
    sums_ref[...] = 2.0 * product(band_ref, here_ref, first_ref, mixed=False) - now_ref[:, start:start + here_ref.shape[1]]


def begun_part(span, band, here, first, now, after):
    rows, width = here.shape
    return pl.pallas_call(
        functools.partial(begun_kernel, span[0]),
        in_specs=[VMEM] * 4 + [ANY] * len(after),
        out_specs=VMEM,
        out_shape=jax.ShapeDtypeStruct(here.shape, jnp.float32),
        compiler_params=params(),
        cost_estimate=cost(4 * rows * rows * width, 4 * rows * rows + 12 * rows * width),
        name="begun_part",
    )(band, here, first, now, *after)


def last_kernel(begin, column, mask_ref, coeffs_ref, band_ref, second_ref, sums_ref, mid_ref, *rest):
    next_ref, density_ref, held_next, held_density, sems = rest[-5:]
    rows, width = second_ref.shape
    block = rows // mask_ref.shape[0]
    step = rows // CHUNKS
    inside = slice(column, column + width)
    copies = []
    for c in range(CHUNKS):
        total = jnp.dot(
            band_ref[c * step:(c + 1) * step, side_columns(rows, 1, False)], second_ref[...],
            preferred_element_type=jnp.float32)
        for i in range(step // block):
            at = slice(c * step + i * block, c * step + (i + 1) * block)
            keep = kept(mask_ref, c * (step // block) + i, (begin + column) // block, block, width)
            value = jnp.where(keep, 2.0 * total[i * block:(i + 1) * block] + sums_ref[at, inside], 0.0)
            held_next[at, :] = value
            held_density[at, :] = coeffs_ref[0] * mid_ref[at, inside] + coeffs_ref[1] * value
        done = pl.ds(c * step, step)
        copies += start_writes(
            [(held_next, next_ref, done, begin + column), (held_density, density_ref, done, begin + column)],
            sems, len(copies))
    for copy in copies:
        copy.wait()


def last_part(begin, column, mask, coeffs, band, second, sums, mid, outs):
    rows, width = second.shape
    return pl.pallas_call(
        functools.partial(last_kernel, begin, column),
        in_specs=[SMEM] * 2 + [VMEM] * 4 + [HBM] * 2,
        out_specs=[HBM] * 2,
        out_shape=[jax.ShapeDtypeStruct(out.shape, jnp.float32) for out in outs],
        scratch_shapes=[pltpu.VMEM((rows, width), jnp.float32)] * 2 + [pltpu.SemaphoreType.DMA((2 * CHUNKS,))],
        input_output_aliases={6: 0, 7: 1},
        compiler_params=params(),
        cost_estimate=cost(2 * rows * rows * width, 2 * rows * rows + 22 * rows * width),
        name="last_part",
    )(mask, coeffs, band, second, sums, mid, *outs)


def local(h_strips, h_slots, t_prev, t_now, t_mask, coeffs):
    width = t_now.shape[1] // 2
    low = t_now[:, :width].astype(jnp.bfloat16)
    low, t_now, t_prev, h_strips = lax.optimization_barrier((low, t_now, t_prev, h_strips))
    (high,) = rounded(t_now, [(width, width)])
    band = banded(h_slots, h_strips)
    low_sides, high_sides = both_sides(low), both_sides(high)
    mid_low, low_again = mid_part((0, width), [(0, width)], t_mask, band, low, *low_sides, t_prev, [])
    low_sides = both_sides(low_again)
    pieces = [(column, width // 2) for column in (0, width // 2)]
    mid_high, high_again, *cuts = mid_part(
        (width, width), [(0, width)] + pieces, t_mask, band, high, *high_sides, t_prev, [mid_low])
    first = from_side(high_again, 0, False)
    seconds = [from_side(cut, 1, False) for cut in cuts]
    t_mid, *outs, token = next_part(t_mask, coeffs, band, low_again, *low_sides, t_now, [mid_low, mid_high])
    sums = begun_part((width, width), band, high_again, first, t_now, [token])
    for (column, _), second in zip(pieces, seconds):
        outs = last_part(width, column, t_mask, coeffs, band, second, sums, mid_high, outs)
    return (t_mid, outs[0], outs[1])


def solution(mesh):
    panel = P(("grp", "row"), ("col", "rep"))
    return jax.shard_map(
        local,
        mesh=mesh,
        in_specs=(P(("grp", "row"), None, None), P(("grp", "row"), None), panel, panel, panel, P()),
        out_specs=(panel, panel, panel),
        check_vma=False,
    )
```

```python
import functools

import jax
import jax.numpy as jnp
from jax import lax
from jax.experimental import pallas as pl
from jax.experimental.pallas import tpu as pltpu
from jax.sharding import PartitionSpec as P

LANES = 128
CHUNKS = 2
MIB = 1024 * 1024

SMEM = pl.BlockSpec(memory_space=pltpu.SMEM)
VMEM = pl.BlockSpec(memory_space=pltpu.VMEM)
ANY = pl.BlockSpec(memory_space=pl.ANY)
HBM = pl.BlockSpec(memory_space=pltpu.HBM)


def from_side(block, order, mixed):
    rows, reps = lax.axis_size("row"), lax.axis_size("rep")
    route = []
    for row in range(rows):
        for rep in range(reps):
            turn = 1 if order == (mixed and rep % 2) else -1
            source = (row - turn) % rows
            route.append((source * reps + rep, row * reps + rep))
    return lax.ppermute(block, ("row", "rep"), route)


def both_sides(block):
    return tuple(from_side(block, order, True) for order in (0, 1))


def side_columns(depth, order, mixed):
    if not mixed:
        return pl.ds(2 * depth * order, depth)
    odd = lax.axis_index("rep") % 2
    return pl.ds(pl.multiple_of(jnp.where(odd == order, 0, 2 * depth), LANES), depth)


def params(limit=32 * MIB):
    return pltpu.CompilerParams(vmem_limit_bytes=limit)


def cost(flops, moved):
    return pl.CostEstimate(flops=flops, transcendentals=0, bytes_accessed=moved)


def round_kernel(starts, now_ref, *out_refs):
    for start, out_ref in zip(starts, out_refs):
        out_ref[...] = now_ref[:, start:start + out_ref.shape[1]].astype(jnp.bfloat16)


def rounded(now, spans):
    rows = now.shape[0]
    size = rows * sum(width for _, width in spans)
    return list(pl.pallas_call(
        functools.partial(round_kernel, [start for start, _ in spans]),
        in_specs=[VMEM],
        out_specs=[VMEM] * len(spans),
        out_shape=[jax.ShapeDtypeStruct((rows, width), jnp.bfloat16) for _, width in spans],
        compiler_params=params(),
        cost_estimate=cost(size, 6 * size),
        name="round_part",
    )(now))


def band_kernel(slots_ref, strips_ref, out_ref):
    block_rows, block, slot_lanes = strips_ref.shape
    out_ref[...] = jnp.zeros_like(out_ref)
    half = lax.broadcasted_iota(jnp.int32, (block, LANES), 1) // block

    @pl.loop(0, block_rows)
    def _(row):
        at = pl.ds(pl.multiple_of(row * block, block), block)
        for pair in range(slot_lanes // LANES):
            straight = strips_ref[row, :, pair * LANES:(pair + 1) * LANES].astype(jnp.float32)
            swapped = jnp.concatenate([straight[:, block:], straight[:, :block]], axis=1)
            for side in range(2):
                target = slots_ref[row, 2 * pair + side]
                odd = target % 2
                value = jnp.where(odd == side, straight, swapped)
                value = jnp.where(half == odd, value, 0.0).astype(jnp.bfloat16)
                lanes = pl.ds(pl.multiple_of((target // 2) * LANES, LANES), LANES)
                out_ref[at, lanes] += value


def banded(h_slots, h_strips):
    block_rows, block, slot_lanes = h_strips.shape
    rows, columns = block_rows * block, 3 * block_rows * block
    return pl.pallas_call(
        band_kernel,
        in_specs=[SMEM, VMEM],
        out_specs=VMEM,
        out_shape=jax.ShapeDtypeStruct((rows, columns), jnp.bfloat16),
        compiler_params=params(),
        cost_estimate=cost(8 * rows * columns, 2 * rows * (columns + slot_lanes)),
        name="band",
    )(h_slots, h_strips)


def product(band_ref, here_ref, first_ref, second_ref=None, mixed=True):
    depth = here_ref.shape[0]
    total = jnp.dot(band_ref[:, depth:2 * depth], here_ref[...], preferred_element_type=jnp.float32)
    total += jnp.dot(band_ref[:, side_columns(depth, 0, mixed)], first_ref[...], preferred_element_type=jnp.float32)
    if second_ref is not None:
        total += jnp.dot(band_ref[:, side_columns(depth, 1, mixed)], second_ref[...], preferred_element_type=jnp.float32)
    return total


def kept(mask_ref, block_row, first, block, width):
    column = lax.broadcasted_iota(jnp.int32, (block, width), 1) // block
    row = jnp.zeros((block, width), jnp.int32)
    for c in range(width // block):
        row = jnp.where(column == c, mask_ref[block_row, first + c], row)
    return row != 0


def masked(start, mask_ref, term):
    rows, width = term.shape
    block = rows // mask_ref.shape[0]
    for i in range(rows // block):
        at = slice(i * block, (i + 1) * block)
        yield at, jnp.where(kept(mask_ref, i, start // block, block, width), term[at], 0.0)


def start_writes(jobs, sems, first):
    copies = []
    for held, out_ref, at, column in jobs:
        copies.append(pltpu.make_async_copy(
            held.at[at, :], out_ref.at[at, pl.ds(column, held.shape[1])], sems.at[first + len(copies)]))
        copies[-1].start()
    return copies


def mid_kernel(start, pieces, mask_ref, band_ref, here_ref, second_ref, first_ref, prev_ref, *rest):
    mid_ref, round_refs = rest[-len(pieces) - 1], rest[-len(pieces):]
    total = product(band_ref, here_ref, first_ref, second_ref)
    term = 2.0 * total - prev_ref[:, start:start + here_ref.shape[1]]
    for at, value in masked(start, mask_ref, term):
        mid_ref[at, :] = value
        low = value.astype(jnp.bfloat16)
        for (column, size), round_ref in zip(pieces, round_refs):
            round_ref[at, :] = low[:, column:column + size]


def mid_part(span, pieces, mask, band, here, first, second, prev, after):
    rows, width = here.shape
    return pl.pallas_call(
        functools.partial(mid_kernel, span[0], pieces),
        in_specs=[SMEM] + [VMEM] * 5 + [ANY] * len(after),
        out_specs=[VMEM] * (1 + len(pieces)),
        out_shape=[jax.ShapeDtypeStruct(here.shape, jnp.float32)]
        + [jax.ShapeDtypeStruct((rows, size), jnp.bfloat16) for _, size in pieces],
        compiler_params=params(),
        cost_estimate=cost(6 * rows * rows * width, 6 * rows * rows + 16 * rows * width),
        name="mid_part",
    )(mask, band, here, second, first, prev, *after)


def next_kernel(mask_ref, coeffs_ref, band_ref, here_ref, second_ref, first_ref, now_ref, mid_ref, other_mid_ref,
                t_mid_ref, next_ref, density_ref, token_ref, held_next, held_density, sems):
    rows, width = here_ref.shape
    block = rows // mask_ref.shape[0]
    everything = pl.ds(0, rows)
    token_ref[...] = jnp.zeros_like(token_ref)
    copies = start_writes(
        [(mid_ref, t_mid_ref, everything, 0), (other_mid_ref, t_mid_ref, everything, width)], sems, 0)
    term = 2.0 * product(band_ref, here_ref, first_ref, second_ref, mixed=False) - now_ref[:, :width]
    for at, value in masked(0, mask_ref, term):
        held_next[at, :] = value
        held_density[at, :] = coeffs_ref[0] * mid_ref[at, :] + coeffs_ref[1] * value
    copies += start_writes(
        [(held_next, next_ref, everything, 0), (held_density, density_ref, everything, 0)], sems, len(copies))
    for copy in copies:
        copy.wait()


def next_part(mask, coeffs, band, here, first, second, now, mids):
    rows, width = here.shape
    return pl.pallas_call(
        next_kernel,
        in_specs=[SMEM] * 2 + [VMEM] * 7,
        out_specs=[HBM] * 3 + [VMEM],
        out_shape=[jax.ShapeDtypeStruct(now.shape, jnp.float32)] * 3 + [jax.ShapeDtypeStruct((8, LANES), jnp.float32)],
        scratch_shapes=[pltpu.VMEM(here.shape, jnp.float32)] * 2 + [pltpu.SemaphoreType.DMA((4,))],
        compiler_params=params(),
        cost_estimate=cost(6 * rows * rows * width, 6 * rows * rows + 30 * rows * width),
        name="next_part",
    )(mask, coeffs, band, here, second, first, now, *mids)


def begun_kernel(start, band_ref, here_ref, first_ref, now_ref, *rest):
    sums_ref = rest[-1]
    sums_ref[...] = 2.0 * product(band_ref, here_ref, first_ref, mixed=False) - now_ref[:, start:start + here_ref.shape[1]]


def begun_part(span, band, here, first, now, after):
    rows, width = here.shape
    return pl.pallas_call(
        functools.partial(begun_kernel, span[0]),
        in_specs=[VMEM] * 4 + [ANY] * len(after),
        out_specs=VMEM,
        out_shape=jax.ShapeDtypeStruct(here.shape, jnp.float32),
        compiler_params=params(),
        cost_estimate=cost(4 * rows * rows * width, 4 * rows * rows + 12 * rows * width),
        name="begun_part",
    )(band, here, first, now, *after)


def piece_kernel(begin, column, mask_ref, coeffs_ref, band_ref, second_ref, sums_ref, mid_ref, next_ref, density_ref):
    rows, width = second_ref.shape
    inside = slice(column, column + width)
    total = jnp.dot(band_ref[:, side_columns(rows, 1, False)], second_ref[...], preferred_element_type=jnp.float32)
    for at, value in masked(begin + column, mask_ref, 2.0 * total + sums_ref[:, inside]):
        next_ref[at, :] = value
        density_ref[at, :] = coeffs_ref[0] * mid_ref[at, inside] + coeffs_ref[1] * value


def piece_part(begin, column, mask, coeffs, band, second, sums, mid):
    rows, width = second.shape
    return pl.pallas_call(
        functools.partial(piece_kernel, begin, column),
        in_specs=[SMEM] * 2 + [VMEM] * 4,
        out_specs=[VMEM] * 2,
        out_shape=[jax.ShapeDtypeStruct(second.shape, jnp.float32)] * 2,
        compiler_params=params(),
        cost_estimate=cost(2 * rows * rows * width, 2 * rows * rows + 22 * rows * width),
        name="piece_part",
    )(mask, coeffs, band, second, sums, mid)


def last_kernel(begin, column, mask_ref, coeffs_ref, band_ref, second_ref, sums_ref, mid_ref, piece_next_ref,
                piece_density_ref, *rest):
    next_ref, density_ref, held_next, held_density, sems = rest[-5:]
    rows, width = second_ref.shape
    block = rows // mask_ref.shape[0]
    step = rows // CHUNKS
    inside = slice(column, column + width)
    everything = pl.ds(0, rows)
    copies = start_writes(
        [(piece_next_ref, next_ref, everything, begin), (piece_density_ref, density_ref, everything, begin)], sems, 0)
    for c in range(CHUNKS):
        total = jnp.dot(
            band_ref[c * step:(c + 1) * step, side_columns(rows, 1, False)], second_ref[...],
            preferred_element_type=jnp.float32)
        for i in range(step // block):
            at = slice(c * step + i * block, c * step + (i + 1) * block)
            keep = kept(mask_ref, c * (step // block) + i, (begin + column) // block, block, width)
            value = jnp.where(keep, 2.0 * total[i * block:(i + 1) * block] + sums_ref[at, inside], 0.0)
            held_next[at, :] = value
            held_density[at, :] = coeffs_ref[0] * mid_ref[at, inside] + coeffs_ref[1] * value
        done = pl.ds(c * step, step)
        copies += start_writes(
            [(held_next, next_ref, done, begin + column), (held_density, density_ref, done, begin + column)],
            sems, len(copies))
    for copy in copies:
        copy.wait()


def last_part(begin, column, mask, coeffs, band, second, sums, mid, piece, outs):
    rows, width = second.shape
    return pl.pallas_call(
        functools.partial(last_kernel, begin, column),
        in_specs=[SMEM] * 2 + [VMEM] * 6 + [HBM] * 2,
        out_specs=[HBM] * 2,
        out_shape=[jax.ShapeDtypeStruct(out.shape, jnp.float32) for out in outs],
        scratch_shapes=[pltpu.VMEM((rows, width), jnp.float32)] * 2 + [pltpu.SemaphoreType.DMA((2 + 2 * CHUNKS,))],
        input_output_aliases={8: 0, 9: 1},
        compiler_params=params(),
        cost_estimate=cost(2 * rows * rows * width, 2 * rows * rows + 22 * rows * width),
        name="last_part",
    )(mask, coeffs, band, second, sums, mid, *piece, *outs)


def local(h_strips, h_slots, t_prev, t_now, t_mask, coeffs):
    width = t_now.shape[1] // 2
    low = t_now[:, :width].astype(jnp.bfloat16)
    low, t_now, t_prev, h_strips = lax.optimization_barrier((low, t_now, t_prev, h_strips))
    (high,) = rounded(t_now, [(width, width)])
    band = banded(h_slots, h_strips)
    low_sides, high_sides = both_sides(low), both_sides(high)
    mid_low, low_again = mid_part((0, width), [(0, width)], t_mask, band, low, *low_sides, t_prev, [])
    low_sides = [from_side(low_again, order, False) for order in (0, 1)]
    pieces = [(column, width // 2) for column in (0, width // 2)]
    mid_high, high_again, *cuts = mid_part(
        (width, width), [(0, width)] + pieces, t_mask, band, high, *high_sides, t_prev, [mid_low])
    first = from_side(high_again, 0, False)
    seconds = [from_side(cut, 1, False) for cut in cuts]
    t_mid, *outs, token = next_part(t_mask, coeffs, band, low_again, *low_sides, t_now, [mid_low, mid_high])
    sums = begun_part((width, width), band, high_again, first, t_now, [token])
    piece = piece_part(width, 0, t_mask, coeffs, band, seconds[0], sums, mid_high)
    outs = last_part(width, width // 2, t_mask, coeffs, band, seconds[1], sums, mid_high, piece, outs)
    return (t_mid, outs[0], outs[1])


def solution(mesh):
    panel = P(("grp", "row"), ("col", "rep"))
    return jax.shard_map(
        local,
        mesh=mesh,
        in_specs=(P(("grp", "row"), None, None), P(("grp", "row"), None), panel, panel, panel, P()),
        out_specs=(panel, panel, panel),
        check_vma=False,
    )
```

```python
import functools

import jax
import jax.numpy as jnp
from jax import lax
from jax.experimental import pallas as pl
from jax.experimental.pallas import tpu as pltpu
from jax.sharding import PartitionSpec as P

LANES = 128
CHUNKS = 2
MIB = 1024 * 1024

SMEM = pl.BlockSpec(memory_space=pltpu.SMEM)
VMEM = pl.BlockSpec(memory_space=pltpu.VMEM)
ANY = pl.BlockSpec(memory_space=pl.ANY)
HBM = pl.BlockSpec(memory_space=pltpu.HBM)


def from_side(block, order, mixed):
    rows, reps = lax.axis_size("row"), lax.axis_size("rep")
    route = []
    for row in range(rows):
        for rep in range(reps):
            turn = 1 if order == (mixed and rep % 2) else -1
            source = (row - turn) % rows
            route.append((source * reps + rep, row * reps + rep))
    return lax.ppermute(block, ("row", "rep"), route)


def both_sides(block, mixed):
    return tuple(from_side(block, order, mixed) for order in (0, 1))


def side_columns(depth, order, mixed):
    if not mixed:
        return pl.ds(2 * depth * order, depth)
    odd = lax.axis_index("rep") % 2
    return pl.ds(pl.multiple_of(jnp.where(odd == order, 0, 2 * depth), LANES), depth)


def params(limit=32 * MIB):
    return pltpu.CompilerParams(vmem_limit_bytes=limit)


def cost(flops, moved):
    return pl.CostEstimate(flops=flops, transcendentals=0, bytes_accessed=moved)


def round_kernel(starts, now_ref, *out_refs):
    for start, out_ref in zip(starts, out_refs):
        out_ref[...] = now_ref[:, start:start + out_ref.shape[1]].astype(jnp.bfloat16)


def rounded(now, spans):
    rows = now.shape[0]
    size = rows * sum(width for _, width in spans)
    return list(pl.pallas_call(
        functools.partial(round_kernel, [start for start, _ in spans]),
        in_specs=[VMEM],
        out_specs=[VMEM] * len(spans),
        out_shape=[jax.ShapeDtypeStruct((rows, width), jnp.bfloat16) for _, width in spans],
        compiler_params=params(),
        cost_estimate=cost(size, 6 * size),
        name="round_part",
    )(now))


def band_kernel(slots_ref, strips_ref, out_ref):
    block_rows, block, slot_lanes = strips_ref.shape
    out_ref[...] = jnp.zeros_like(out_ref)
    half = lax.broadcasted_iota(jnp.int32, (block, LANES), 1) // block

    @pl.loop(0, block_rows)
    def _(row):
        at = pl.ds(pl.multiple_of(row * block, block), block)
        for pair in range(slot_lanes // LANES):
            straight = strips_ref[row, :, pair * LANES:(pair + 1) * LANES].astype(jnp.float32)
            swapped = jnp.concatenate([straight[:, block:], straight[:, :block]], axis=1)
            for side in range(2):
                target = slots_ref[row, 2 * pair + side]
                odd = target % 2
                value = jnp.where(odd == side, straight, swapped)
                value = jnp.where(half == odd, value, 0.0).astype(jnp.bfloat16)
                lanes = pl.ds(pl.multiple_of((target // 2) * LANES, LANES), LANES)
                out_ref[at, lanes] += value


def banded(h_slots, h_strips):
    block_rows, block, slot_lanes = h_strips.shape
    rows, columns = block_rows * block, 3 * block_rows * block
    return pl.pallas_call(
        band_kernel,
        in_specs=[SMEM, VMEM],
        out_specs=VMEM,
        out_shape=jax.ShapeDtypeStruct((rows, columns), jnp.bfloat16),
        compiler_params=params(),
        cost_estimate=cost(8 * rows * columns, 2 * rows * (columns + slot_lanes)),
        name="band",
    )(h_slots, h_strips)


def product(band_ref, here_ref, first_ref, second_ref=None, mixed=True):
    depth = here_ref.shape[0]
    total = jnp.dot(band_ref[:, depth:2 * depth], here_ref[...], preferred_element_type=jnp.float32)
    total += jnp.dot(band_ref[:, side_columns(depth, 0, mixed)], first_ref[...], preferred_element_type=jnp.float32)
    if second_ref is not None:
        total += jnp.dot(band_ref[:, side_columns(depth, 1, mixed)], second_ref[...], preferred_element_type=jnp.float32)
    return total


def kept(mask_ref, block_row, first, block, width):
    column = lax.broadcasted_iota(jnp.int32, (block, width), 1) // block
    row = jnp.zeros((block, width), jnp.int32)
    for c in range(width // block):
        row = jnp.where(column == c, mask_ref[block_row, first + c], row)
    return row != 0


def masked(start, mask_ref, term):
    rows, width = term.shape
    block = rows // mask_ref.shape[0]
    for i in range(rows // block):
        at = slice(i * block, (i + 1) * block)
        yield at, jnp.where(kept(mask_ref, i, start // block, block, width), term[at], 0.0)


def start_writes(jobs, sems, first):
    copies = []
    for held, out_ref, at, column in jobs:
        copies.append(pltpu.make_async_copy(
            held.at[at, :], out_ref.at[at, pl.ds(column, held.shape[1])], sems.at[first + len(copies)]))
        copies[-1].start()
    return copies


def mid_kernel(start, pieces, mixed, mask_ref, band_ref, here_ref, second_ref, first_ref, prev_ref, *rest):
    mid_ref, round_refs = rest[-len(pieces) - 1], rest[-len(pieces):]
    total = product(band_ref, here_ref, first_ref, second_ref, mixed)
    term = 2.0 * total - prev_ref[:, start:start + here_ref.shape[1]]
    for at, value in masked(start, mask_ref, term):
        mid_ref[at, :] = value
        low = value.astype(jnp.bfloat16)
        for (column, size), round_ref in zip(pieces, round_refs):
            round_ref[at, :] = low[:, column:column + size]


def mid_part(span, pieces, mixed, mask, band, here, first, second, prev, after):
    rows, width = here.shape
    return pl.pallas_call(
        functools.partial(mid_kernel, span[0], pieces, mixed),
        in_specs=[SMEM] + [VMEM] * 5 + [ANY] * len(after),
        out_specs=[VMEM] * (1 + len(pieces)),
        out_shape=[jax.ShapeDtypeStruct(here.shape, jnp.float32)]
        + [jax.ShapeDtypeStruct((rows, size), jnp.bfloat16) for _, size in pieces],
        compiler_params=params(),
        cost_estimate=cost(6 * rows * rows * width, 6 * rows * rows + 16 * rows * width),
        name="mid_part",
    )(mask, band, here, second, first, prev, *after)


def next_kernel(mask_ref, coeffs_ref, band_ref, here_ref, second_ref, first_ref, now_ref, mid_ref, other_mid_ref,
                t_mid_ref, next_ref, density_ref, token_ref, held_next, held_density, sems):
    rows, width = here_ref.shape
    block = rows // mask_ref.shape[0]
    everything = pl.ds(0, rows)
    token_ref[...] = jnp.zeros_like(token_ref)
    copies = start_writes(
        [(mid_ref, t_mid_ref, everything, 0), (other_mid_ref, t_mid_ref, everything, width)], sems, 0)
    term = 2.0 * product(band_ref, here_ref, first_ref, second_ref, mixed=False) - now_ref[:, :width]
    for at, value in masked(0, mask_ref, term):
        held_next[at, :] = value
        held_density[at, :] = coeffs_ref[0] * mid_ref[at, :] + coeffs_ref[1] * value
    copies += start_writes(
        [(held_next, next_ref, everything, 0), (held_density, density_ref, everything, 0)], sems, len(copies))
    for copy in copies:
        copy.wait()


def next_part(mask, coeffs, band, here, first, second, now, mids):
    rows, width = here.shape
    return pl.pallas_call(
        next_kernel,
        in_specs=[SMEM] * 2 + [VMEM] * 7,
        out_specs=[HBM] * 3 + [VMEM],
        out_shape=[jax.ShapeDtypeStruct(now.shape, jnp.float32)] * 3 + [jax.ShapeDtypeStruct((8, LANES), jnp.float32)],
        scratch_shapes=[pltpu.VMEM(here.shape, jnp.float32)] * 2 + [pltpu.SemaphoreType.DMA((4,))],
        compiler_params=params(),
        cost_estimate=cost(6 * rows * rows * width, 6 * rows * rows + 30 * rows * width),
        name="next_part",
    )(mask, coeffs, band, here, second, first, now, *mids)


def begun_kernel(start, band_ref, here_ref, first_ref, now_ref, *rest):
    sums_ref = rest[-1]
    sums_ref[...] = 2.0 * product(band_ref, here_ref, first_ref, mixed=False) - now_ref[:, start:start + here_ref.shape[1]]


def begun_part(span, band, here, first, now, after):
    rows, width = here.shape
    return pl.pallas_call(
        functools.partial(begun_kernel, span[0]),
        in_specs=[VMEM] * 4 + [ANY] * len(after),
        out_specs=VMEM,
        out_shape=jax.ShapeDtypeStruct(here.shape, jnp.float32),
        compiler_params=params(),
        cost_estimate=cost(4 * rows * rows * width, 4 * rows * rows + 12 * rows * width),
        name="begun_part",
    )(band, here, first, now, *after)


def piece_kernel(begin, column, mask_ref, coeffs_ref, band_ref, second_ref, sums_ref, mid_ref, next_ref, density_ref):
    rows, width = second_ref.shape
    inside = slice(column, column + width)
    total = jnp.dot(band_ref[:, side_columns(rows, 1, False)], second_ref[...], preferred_element_type=jnp.float32)
    for at, value in masked(begin + column, mask_ref, 2.0 * total + sums_ref[:, inside]):
        next_ref[at, :] = value
        density_ref[at, :] = coeffs_ref[0] * mid_ref[at, inside] + coeffs_ref[1] * value


def piece_part(begin, column, mask, coeffs, band, second, sums, mid):
    rows, width = second.shape
    return pl.pallas_call(
        functools.partial(piece_kernel, begin, column),
        in_specs=[SMEM] * 2 + [VMEM] * 4,
        out_specs=[VMEM] * 2,
        out_shape=[jax.ShapeDtypeStruct(second.shape, jnp.float32)] * 2,
        compiler_params=params(),
        cost_estimate=cost(2 * rows * rows * width, 2 * rows * rows + 22 * rows * width),
        name="piece_part",
    )(mask, coeffs, band, second, sums, mid)


def last_kernel(begin, column, mask_ref, coeffs_ref, band_ref, second_ref, sums_ref, mid_ref, piece_next_ref,
                piece_density_ref, *rest):
    next_ref, density_ref, held_next, held_density, sems = rest[-5:]
    rows, width = second_ref.shape
    block = rows // mask_ref.shape[0]
    step = rows // CHUNKS
    inside = slice(column, column + width)
    everything = pl.ds(0, rows)
    copies = start_writes(
        [(piece_next_ref, next_ref, everything, begin), (piece_density_ref, density_ref, everything, begin)], sems, 0)
    for c in range(CHUNKS):
        total = jnp.dot(
            band_ref[c * step:(c + 1) * step, side_columns(rows, 1, False)], second_ref[...],
            preferred_element_type=jnp.float32)
        for i in range(step // block):
            at = slice(c * step + i * block, c * step + (i + 1) * block)
            keep = kept(mask_ref, c * (step // block) + i, (begin + column) // block, block, width)
            value = jnp.where(keep, 2.0 * total[i * block:(i + 1) * block] + sums_ref[at, inside], 0.0)
            held_next[at, :] = value
            held_density[at, :] = coeffs_ref[0] * mid_ref[at, inside] + coeffs_ref[1] * value
        done = pl.ds(c * step, step)
        copies += start_writes(
            [(held_next, next_ref, done, begin + column), (held_density, density_ref, done, begin + column)],
            sems, len(copies))
    for copy in copies:
        copy.wait()


def last_part(begin, column, mask, coeffs, band, second, sums, mid, piece, outs):
    rows, width = second.shape
    return pl.pallas_call(
        functools.partial(last_kernel, begin, column),
        in_specs=[SMEM] * 2 + [VMEM] * 6 + [HBM] * 2,
        out_specs=[HBM] * 2,
        out_shape=[jax.ShapeDtypeStruct(out.shape, jnp.float32) for out in outs],
        scratch_shapes=[pltpu.VMEM((rows, width), jnp.float32)] * 2 + [pltpu.SemaphoreType.DMA((2 + 2 * CHUNKS,))],
        input_output_aliases={8: 0, 9: 1},
        compiler_params=params(),
        cost_estimate=cost(2 * rows * rows * width, 2 * rows * rows + 22 * rows * width),
        name="last_part",
    )(mask, coeffs, band, second, sums, mid, *piece, *outs)


def local(h_strips, h_slots, t_prev, t_now, t_mask, coeffs):
    width = t_now.shape[1] // 2
    low = t_now[:, :width].astype(jnp.bfloat16)
    low, t_now, t_prev, h_strips = lax.optimization_barrier((low, t_now, t_prev, h_strips))
    (high,) = rounded(t_now, [(width, width)])
    band = banded(h_slots, h_strips)
    low_sides, high_sides = both_sides(low, False), both_sides(high, True)
    mid_low, low_again = mid_part((0, width), [(0, width)], False, t_mask, band, low, *low_sides, t_prev, [])
    low_sides = both_sides(low_again, False)
    pieces = [(column, width // 2) for column in (0, width // 2)]
    mid_high, high_again, *cuts = mid_part(
        (width, width), [(0, width)] + pieces, True, t_mask, band, high, *high_sides, t_prev, [mid_low])
    first = from_side(high_again, 0, False)
    seconds = [from_side(cut, 1, False) for cut in cuts]
    t_mid, *outs, token = next_part(t_mask, coeffs, band, low_again, *low_sides, t_now, [mid_low, mid_high])
    sums = begun_part((width, width), band, high_again, first, t_now, [token])
    piece = piece_part(width, 0, t_mask, coeffs, band, seconds[0], sums, mid_high)
    outs = last_part(width, width // 2, t_mask, coeffs, band, seconds[1], sums, mid_high, piece, outs)
    return (t_mid, outs[0], outs[1])


def solution(mesh):
    panel = P(("grp", "row"), ("col", "rep"))
    return jax.shard_map(
        local,
        mesh=mesh,
        in_specs=(P(("grp", "row"), None, None), P(("grp", "row"), None), panel, panel, panel, P()),
        out_specs=(panel, panel, panel),
        check_vma=False,
    )
```

```python
import functools

import jax
import jax.numpy as jnp
from jax import lax
from jax.experimental import pallas as pl
from jax.experimental.pallas import tpu as pltpu
from jax.sharding import PartitionSpec as P

LANES = 128
CHUNKS = 2
MIB = 1024 * 1024

SMEM = pl.BlockSpec(memory_space=pltpu.SMEM)
VMEM = pl.BlockSpec(memory_space=pltpu.VMEM)
ANY = pl.BlockSpec(memory_space=pl.ANY)
HBM = pl.BlockSpec(memory_space=pltpu.HBM)


def from_side(block, order, mixed):
    rows, reps = lax.axis_size("row"), lax.axis_size("rep")
    route = []
    for row in range(rows):
        for rep in range(reps):
            turn = 1 if order == (mixed and rep % 2) else -1
            source = (row - turn) % rows
            route.append((source * reps + rep, row * reps + rep))
    return lax.ppermute(block, ("row", "rep"), route)


def both_sides(block, mixed):
    return tuple(from_side(block, order, mixed) for order in (0, 1))


def side_columns(depth, order, mixed):
    if not mixed:
        return pl.ds(2 * depth * order, depth)
    odd = lax.axis_index("rep") % 2
    return pl.ds(pl.multiple_of(jnp.where(odd == order, 0, 2 * depth), LANES), depth)


def params(limit=32 * MIB):
    return pltpu.CompilerParams(vmem_limit_bytes=limit)


def cost(flops, moved):
    return pl.CostEstimate(flops=flops, transcendentals=0, bytes_accessed=moved)


def round_kernel(starts, now_ref, *out_refs):
    for start, out_ref in zip(starts, out_refs):
        out_ref[...] = now_ref[:, start:start + out_ref.shape[1]].astype(jnp.bfloat16)


def rounded(now, spans):
    rows = now.shape[0]
    size = rows * sum(width for _, width in spans)
    return list(pl.pallas_call(
        functools.partial(round_kernel, [start for start, _ in spans]),
        in_specs=[VMEM],
        out_specs=[VMEM] * len(spans),
        out_shape=[jax.ShapeDtypeStruct((rows, width), jnp.bfloat16) for _, width in spans],
        compiler_params=params(),
        cost_estimate=cost(size, 6 * size),
        name="round_part",
    )(now))


def band_kernel(slots_ref, strips_ref, out_ref):
    block_rows, block, slot_lanes = strips_ref.shape
    out_ref[...] = jnp.zeros_like(out_ref)
    half = lax.broadcasted_iota(jnp.int32, (block, LANES), 1) // block

    @pl.loop(0, block_rows)
    def _(row):
        at = pl.ds(pl.multiple_of(row * block, block), block)
        for pair in range(slot_lanes // LANES):
            straight = strips_ref[row, :, pair * LANES:(pair + 1) * LANES].astype(jnp.float32)
            swapped = jnp.concatenate([straight[:, block:], straight[:, :block]], axis=1)
            for side in range(2):
                target = slots_ref[row, 2 * pair + side]
                odd = target % 2
                value = jnp.where(odd == side, straight, swapped)
                value = jnp.where(half == odd, value, 0.0).astype(jnp.bfloat16)
                lanes = pl.ds(pl.multiple_of((target // 2) * LANES, LANES), LANES)
                out_ref[at, lanes] += value


def banded(h_slots, h_strips):
    block_rows, block, slot_lanes = h_strips.shape
    rows, columns = block_rows * block, 3 * block_rows * block
    return pl.pallas_call(
        band_kernel,
        in_specs=[SMEM, VMEM],
        out_specs=VMEM,
        out_shape=jax.ShapeDtypeStruct((rows, columns), jnp.bfloat16),
        compiler_params=params(),
        cost_estimate=cost(8 * rows * columns, 2 * rows * (columns + slot_lanes)),
        name="band",
    )(h_slots, h_strips)


def product(band_ref, here_ref, first_ref, second_ref=None, mixed=True):
    depth = here_ref.shape[0]
    total = jnp.dot(band_ref[:, depth:2 * depth], here_ref[...], preferred_element_type=jnp.float32)
    total += jnp.dot(band_ref[:, side_columns(depth, 0, mixed)], first_ref[...], preferred_element_type=jnp.float32)
    if second_ref is not None:
        total += jnp.dot(band_ref[:, side_columns(depth, 1, mixed)], second_ref[...], preferred_element_type=jnp.float32)
    return total


def kept(mask_ref, block_row, first, block, width):
    column = lax.broadcasted_iota(jnp.int32, (block, width), 1) // block
    row = jnp.zeros((block, width), jnp.int32)
    for c in range(width // block):
        row = jnp.where(column == c, mask_ref[block_row, first + c], row)
    return row != 0


def masked(start, mask_ref, term):
    rows, width = term.shape
    block = rows // mask_ref.shape[0]
    for i in range(rows // block):
        at = slice(i * block, (i + 1) * block)
        yield at, jnp.where(kept(mask_ref, i, start // block, block, width), term[at], 0.0)


def start_writes(jobs, sems, first):
    copies = []
    for held, out_ref, at, column in jobs:
        copies.append(pltpu.make_async_copy(
            held.at[at, :], out_ref.at[at, pl.ds(column, held.shape[1])], sems.at[first + len(copies)]))
        copies[-1].start()
    return copies


def mid_kernel(start, pieces, mixed, mask_ref, band_ref, here_ref, second_ref, first_ref, prev_ref, *rest):
    mid_ref, round_refs = rest[-len(pieces) - 1], rest[-len(pieces):]
    total = product(band_ref, here_ref, first_ref, second_ref, mixed)
    term = 2.0 * total - prev_ref[:, start:start + here_ref.shape[1]]
    for at, value in masked(start, mask_ref, term):
        mid_ref[at, :] = value
        low = value.astype(jnp.bfloat16)
        for (column, size), round_ref in zip(pieces, round_refs):
            round_ref[at, :] = low[:, column:column + size]


def mid_part(span, pieces, mixed, mask, band, here, first, second, prev, after):
    rows, width = here.shape
    return pl.pallas_call(
        functools.partial(mid_kernel, span[0], pieces, mixed),
        in_specs=[SMEM] + [VMEM] * 5 + [ANY] * len(after),
        out_specs=[VMEM] * (1 + len(pieces)),
        out_shape=[jax.ShapeDtypeStruct(here.shape, jnp.float32)]
        + [jax.ShapeDtypeStruct((rows, size), jnp.bfloat16) for _, size in pieces],
        compiler_params=params(),
        cost_estimate=cost(6 * rows * rows * width, 6 * rows * rows + 16 * rows * width),
        name="mid_part",
    )(mask, band, here, second, first, prev, *after)


def next_kernel(mask_ref, coeffs_ref, band_ref, here_ref, second_ref, first_ref, now_ref, mid_ref, other_mid_ref,
                t_mid_ref, next_ref, density_ref, token_ref, held_next, held_density, sems):
    rows, width = here_ref.shape
    block = rows // mask_ref.shape[0]
    everything = pl.ds(0, rows)
    token_ref[...] = jnp.zeros_like(token_ref)
    copies = start_writes(
        [(mid_ref, t_mid_ref, everything, 0), (other_mid_ref, t_mid_ref, everything, width)], sems, 0)
    term = 2.0 * product(band_ref, here_ref, first_ref, second_ref, mixed=False) - now_ref[:, :width]
    for at, value in masked(0, mask_ref, term):
        held_next[at, :] = value
        held_density[at, :] = coeffs_ref[0] * mid_ref[at, :] + coeffs_ref[1] * value
    copies += start_writes(
        [(held_next, next_ref, everything, 0), (held_density, density_ref, everything, 0)], sems, len(copies))
    for copy in copies:
        copy.wait()


def next_part(mask, coeffs, band, here, first, second, now, mids):
    rows, width = here.shape
    return pl.pallas_call(
        next_kernel,
        in_specs=[SMEM] * 2 + [VMEM] * 7,
        out_specs=[HBM] * 3 + [VMEM],
        out_shape=[jax.ShapeDtypeStruct(now.shape, jnp.float32)] * 3 + [jax.ShapeDtypeStruct((8, LANES), jnp.float32)],
        scratch_shapes=[pltpu.VMEM(here.shape, jnp.float32)] * 2 + [pltpu.SemaphoreType.DMA((4,))],
        compiler_params=params(),
        cost_estimate=cost(6 * rows * rows * width, 6 * rows * rows + 30 * rows * width),
        name="next_part",
    )(mask, coeffs, band, here, second, first, now, *mids)


def begun_kernel(start, band_ref, here_ref, first_ref, now_ref, *rest):
    sums_ref = rest[-1]
    sums_ref[...] = 2.0 * product(band_ref, here_ref, first_ref, mixed=False) - now_ref[:, start:start + here_ref.shape[1]]


def begun_part(span, band, here, first, now, after):
    rows, width = here.shape
    return pl.pallas_call(
        functools.partial(begun_kernel, span[0]),
        in_specs=[VMEM] * 4 + [ANY] * len(after),
        out_specs=VMEM,
        out_shape=jax.ShapeDtypeStruct(here.shape, jnp.float32),
        compiler_params=params(),
        cost_estimate=cost(4 * rows * rows * width, 4 * rows * rows + 12 * rows * width),
        name="begun_part",
    )(band, here, first, now, *after)


def piece_kernel(begin, column, mask_ref, coeffs_ref, band_ref, second_ref, sums_ref, mid_ref, next_ref, density_ref):
    rows, width = second_ref.shape
    inside = slice(column, column + width)
    total = jnp.dot(band_ref[:, side_columns(rows, 1, False)], second_ref[...], preferred_element_type=jnp.float32)
    for at, value in masked(begin + column, mask_ref, 2.0 * total + sums_ref[:, inside]):
        next_ref[at, :] = value
        density_ref[at, :] = coeffs_ref[0] * mid_ref[at, inside] + coeffs_ref[1] * value


def piece_part(begin, column, mask, coeffs, band, second, sums, mid):
    rows, width = second.shape
    return pl.pallas_call(
        functools.partial(piece_kernel, begin, column),
        in_specs=[SMEM] * 2 + [VMEM] * 4,
        out_specs=[VMEM] * 2,
        out_shape=[jax.ShapeDtypeStruct(second.shape, jnp.float32)] * 2,
        compiler_params=params(),
        cost_estimate=cost(2 * rows * rows * width, 2 * rows * rows + 22 * rows * width),
        name="piece_part",
    )(mask, coeffs, band, second, sums, mid)


def last_kernel(begin, column, mask_ref, coeffs_ref, band_ref, second_ref, sums_ref, mid_ref, piece_next_ref,
                piece_density_ref, *rest):
    next_ref, density_ref, held_next, held_density, sems = rest[-5:]
    rows, width = second_ref.shape
    block = rows // mask_ref.shape[0]
    step = rows // CHUNKS
    inside = slice(column, column + width)
    everything = pl.ds(0, rows)
    copies = start_writes(
        [(piece_next_ref, next_ref, everything, begin), (piece_density_ref, density_ref, everything, begin)], sems, 0)
    for c in range(CHUNKS):
        total = jnp.dot(
            band_ref[c * step:(c + 1) * step, side_columns(rows, 1, False)], second_ref[...],
            preferred_element_type=jnp.float32)
        for i in range(step // block):
            at = slice(c * step + i * block, c * step + (i + 1) * block)
            keep = kept(mask_ref, c * (step // block) + i, (begin + column) // block, block, width)
            value = jnp.where(keep, 2.0 * total[i * block:(i + 1) * block] + sums_ref[at, inside], 0.0)
            held_next[at, :] = value
            held_density[at, :] = coeffs_ref[0] * mid_ref[at, inside] + coeffs_ref[1] * value
        done = pl.ds(c * step, step)
        copies += start_writes(
            [(held_next, next_ref, done, begin + column), (held_density, density_ref, done, begin + column)],
            sems, len(copies))
    for copy in copies:
        copy.wait()


def last_part(begin, column, mask, coeffs, band, second, sums, mid, piece, outs):
    rows, width = second.shape
    return pl.pallas_call(
        functools.partial(last_kernel, begin, column),
        in_specs=[SMEM] * 2 + [VMEM] * 6 + [HBM] * 2,
        out_specs=[HBM] * 2,
        out_shape=[jax.ShapeDtypeStruct(out.shape, jnp.float32) for out in outs],
        scratch_shapes=[pltpu.VMEM((rows, width), jnp.float32)] * 2 + [pltpu.SemaphoreType.DMA((2 + 2 * CHUNKS,))],
        input_output_aliases={8: 0, 9: 1},
        compiler_params=params(),
        cost_estimate=cost(2 * rows * rows * width, 2 * rows * rows + 22 * rows * width),
        name="last_part",
    )(mask, coeffs, band, second, sums, mid, *piece, *outs)


def local(h_strips, h_slots, t_prev, t_now, t_mask, coeffs):
    width = t_now.shape[1] // 2
    low = t_now[:, :width].astype(jnp.bfloat16)
    low, t_now, t_prev, h_strips = lax.optimization_barrier((low, t_now, t_prev, h_strips))
    (high,) = rounded(t_now, [(width, width)])
    band = banded(h_slots, h_strips)
    low_sides, high_sides = both_sides(low, True), both_sides(high, False)
    mid_low, low_again = mid_part((0, width), [(0, width)], True, t_mask, band, low, *low_sides, t_prev, [])
    low_sides = both_sides(low_again, False)
    pieces = [(column, width // 2) for column in (0, width // 2)]
    mid_high, high_again, *cuts = mid_part(
        (width, width), [(0, width)] + pieces, False, t_mask, band, high, *high_sides, t_prev, [mid_low])
    first = from_side(high_again, 0, False)
    seconds = [from_side(cut, 1, False) for cut in cuts]
    t_mid, *outs, token = next_part(t_mask, coeffs, band, low_again, *low_sides, t_now, [mid_low, mid_high])
    sums = begun_part((width, width), band, high_again, first, t_now, [token])
    piece = piece_part(width, 0, t_mask, coeffs, band, seconds[0], sums, mid_high)
    outs = last_part(width, width // 2, t_mask, coeffs, band, seconds[1], sums, mid_high, piece, outs)
    return (t_mid, outs[0], outs[1])


def solution(mesh):
    panel = P(("grp", "row"), ("col", "rep"))
    return jax.shard_map(
        local,
        mesh=mesh,
        in_specs=(P(("grp", "row"), None, None), P(("grp", "row"), None), panel, panel, panel, P()),
        out_specs=(panel, panel, panel),
        check_vma=False,
    )
```

```python
import functools

import jax
import jax.numpy as jnp
from jax import lax
from jax.experimental import pallas as pl
from jax.experimental.pallas import tpu as pltpu
from jax.sharding import PartitionSpec as P

LANES = 128
CHUNKS = 2
MIB = 1024 * 1024

SMEM = pl.BlockSpec(memory_space=pltpu.SMEM)
VMEM = pl.BlockSpec(memory_space=pltpu.VMEM)
ANY = pl.BlockSpec(memory_space=pl.ANY)
HBM = pl.BlockSpec(memory_space=pltpu.HBM)


def from_side(block, order, mixed):
    rows, reps = lax.axis_size("row"), lax.axis_size("rep")
    route = []
    for row in range(rows):
        for rep in range(reps):
            turn = 1 if order == (mixed and rep % 2) else -1
            source = (row - turn) % rows
            route.append((source * reps + rep, row * reps + rep))
    return lax.ppermute(block, ("row", "rep"), route)


def both_sides(block):
    return tuple(from_side(block, order, True) for order in (0, 1))


def side_columns(depth, order, mixed):
    if not mixed:
        return pl.ds(2 * depth * order, depth)
    odd = lax.axis_index("rep") % 2
    return pl.ds(pl.multiple_of(jnp.where(odd == order, 0, 2 * depth), LANES), depth)


def params(limit=32 * MIB):
    return pltpu.CompilerParams(vmem_limit_bytes=limit)


def cost(flops, moved):
    return pl.CostEstimate(flops=flops, transcendentals=0, bytes_accessed=moved)


def round_kernel(starts, now_ref, *out_refs):
    for start, out_ref in zip(starts, out_refs):
        out_ref[...] = now_ref[:, start:start + out_ref.shape[1]].astype(jnp.bfloat16)


def rounded(now, spans):
    rows = now.shape[0]
    size = rows * sum(width for _, width in spans)
    return list(pl.pallas_call(
        functools.partial(round_kernel, [start for start, _ in spans]),
        in_specs=[VMEM],
        out_specs=[VMEM] * len(spans),
        out_shape=[jax.ShapeDtypeStruct((rows, width), jnp.bfloat16) for _, width in spans],
        compiler_params=params(),
        cost_estimate=cost(size, 6 * size),
        name="round_part",
    )(now))


def band_kernel(slots_ref, strips_ref, out_ref):
    block_rows, block, slot_lanes = strips_ref.shape
    out_ref[...] = jnp.zeros_like(out_ref)
    half = lax.broadcasted_iota(jnp.int32, (block, LANES), 1) // block

    @pl.loop(0, block_rows)
    def _(row):
        at = pl.ds(pl.multiple_of(row * block, block), block)
        for pair in range(slot_lanes // LANES):
            straight = strips_ref[row, :, pair * LANES:(pair + 1) * LANES].astype(jnp.float32)
            swapped = jnp.concatenate([straight[:, block:], straight[:, :block]], axis=1)
            for side in range(2):
                target = slots_ref[row, 2 * pair + side]
                odd = target % 2
                value = jnp.where(odd == side, straight, swapped)
                value = jnp.where(half == odd, value, 0.0).astype(jnp.bfloat16)
                lanes = pl.ds(pl.multiple_of((target // 2) * LANES, LANES), LANES)
                out_ref[at, lanes] += value


def banded(h_slots, h_strips):
    block_rows, block, slot_lanes = h_strips.shape
    rows, columns = block_rows * block, 3 * block_rows * block
    return pl.pallas_call(
        band_kernel,
        in_specs=[SMEM, VMEM],
        out_specs=VMEM,
        out_shape=jax.ShapeDtypeStruct((rows, columns), jnp.bfloat16),
        compiler_params=params(),
        cost_estimate=cost(8 * rows * columns, 2 * rows * (columns + slot_lanes)),
        name="band",
    )(h_slots, h_strips)


def product(band_ref, here_ref, first_ref, second_ref=None, mixed=True):
    depth = here_ref.shape[0]
    total = jnp.dot(band_ref[:, depth:2 * depth], here_ref[...], preferred_element_type=jnp.float32)
    total += jnp.dot(band_ref[:, side_columns(depth, 0, mixed)], first_ref[...], preferred_element_type=jnp.float32)
    if second_ref is not None:
        total += jnp.dot(band_ref[:, side_columns(depth, 1, mixed)], second_ref[...], preferred_element_type=jnp.float32)
    return total


def kept(mask_ref, block_row, first, block, width):
    column = lax.broadcasted_iota(jnp.int32, (block, width), 1) // block
    row = jnp.zeros((block, width), jnp.int32)
    for c in range(width // block):
        row = jnp.where(column == c, mask_ref[block_row, first + c], row)
    return row != 0


def masked(start, mask_ref, term):
    rows, width = term.shape
    block = rows // mask_ref.shape[0]
    for i in range(rows // block):
        at = slice(i * block, (i + 1) * block)
        yield at, jnp.where(kept(mask_ref, i, start // block, block, width), term[at], 0.0)


def start_writes(jobs, sems, first):
    copies = []
    for held, out_ref, at, column in jobs:
        copies.append(pltpu.make_async_copy(
            held.at[at, :], out_ref.at[at, pl.ds(column, held.shape[1])], sems.at[first + len(copies)]))
        copies[-1].start()
    return copies


def mid_kernel(start, pieces, mask_ref, band_ref, here_ref, second_ref, first_ref, prev_ref, *rest):
    mid_ref, round_refs = rest[-len(pieces) - 1], rest[-len(pieces):]
    total = product(band_ref, here_ref, first_ref, second_ref)
    term = 2.0 * total - prev_ref[:, start:start + here_ref.shape[1]]
    for at, value in masked(start, mask_ref, term):
        mid_ref[at, :] = value
        low = value.astype(jnp.bfloat16)
        for (column, size), round_ref in zip(pieces, round_refs):
            round_ref[at, :] = low[:, column:column + size]


def mid_part(span, pieces, mask, band, here, first, second, prev, after):
    rows, width = here.shape
    return pl.pallas_call(
        functools.partial(mid_kernel, span[0], pieces),
        in_specs=[SMEM] + [VMEM] * 5 + [ANY] * len(after),
        out_specs=[VMEM] * (1 + len(pieces)),
        out_shape=[jax.ShapeDtypeStruct(here.shape, jnp.float32)]
        + [jax.ShapeDtypeStruct((rows, size), jnp.bfloat16) for _, size in pieces],
        compiler_params=params(),
        cost_estimate=cost(6 * rows * rows * width, 6 * rows * rows + 16 * rows * width),
        name="mid_part",
    )(mask, band, here, second, first, prev, *after)


def next_kernel(mask_ref, coeffs_ref, band_ref, here_ref, second_ref, first_ref, now_ref, mid_ref, other_mid_ref,
                t_mid_ref, next_ref, density_ref, token_ref, held_next, held_density, sems):
    rows, width = here_ref.shape
    block = rows // mask_ref.shape[0]
    everything = pl.ds(0, rows)
    token_ref[...] = jnp.zeros_like(token_ref)
    copies = start_writes(
        [(mid_ref, t_mid_ref, everything, 0), (other_mid_ref, t_mid_ref, everything, width)], sems, 0)
    term = 2.0 * product(band_ref, here_ref, first_ref, second_ref) - now_ref[:, :width]
    for at, value in masked(0, mask_ref, term):
        held_next[at, :] = value
        held_density[at, :] = coeffs_ref[0] * mid_ref[at, :] + coeffs_ref[1] * value
    copies += start_writes(
        [(held_next, next_ref, everything, 0), (held_density, density_ref, everything, 0)], sems, len(copies))
    for copy in copies:
        copy.wait()


def next_part(mask, coeffs, band, here, first, second, now, mids):
    rows, width = here.shape
    return pl.pallas_call(
        next_kernel,
        in_specs=[SMEM] * 2 + [VMEM] * 7,
        out_specs=[HBM] * 3 + [VMEM],
        out_shape=[jax.ShapeDtypeStruct(now.shape, jnp.float32)] * 3 + [jax.ShapeDtypeStruct((8, LANES), jnp.float32)],
        scratch_shapes=[pltpu.VMEM(here.shape, jnp.float32)] * 2 + [pltpu.SemaphoreType.DMA((4,))],
        compiler_params=params(),
        cost_estimate=cost(6 * rows * rows * width, 6 * rows * rows + 30 * rows * width),
        name="next_part",
    )(mask, coeffs, band, here, second, first, now, *mids)


def begun_kernel(start, band_ref, here_ref, first_ref, now_ref, *rest):
    sums_ref = rest[-1]
    sums_ref[...] = 2.0 * product(band_ref, here_ref, first_ref, mixed=False) - now_ref[:, start:start + here_ref.shape[1]]


def begun_part(span, band, here, first, now, after):
    rows, width = here.shape
    return pl.pallas_call(
        functools.partial(begun_kernel, span[0]),
        in_specs=[VMEM] * 4 + [ANY] * len(after),
        out_specs=VMEM,
        out_shape=jax.ShapeDtypeStruct(here.shape, jnp.float32),
        compiler_params=params(),
        cost_estimate=cost(4 * rows * rows * width, 4 * rows * rows + 12 * rows * width),
        name="begun_part",
    )(band, here, first, now, *after)


def piece_kernel(begin, column, mask_ref, coeffs_ref, band_ref, second_ref, sums_ref, mid_ref, next_ref, density_ref):
    rows, width = second_ref.shape
    inside = slice(column, column + width)
    total = jnp.dot(band_ref[:, side_columns(rows, 1, False)], second_ref[...], preferred_element_type=jnp.float32)
    for at, value in masked(begin + column, mask_ref, 2.0 * total + sums_ref[:, inside]):
        next_ref[at, :] = value
        density_ref[at, :] = coeffs_ref[0] * mid_ref[at, inside] + coeffs_ref[1] * value


def piece_part(begin, column, mask, coeffs, band, second, sums, mid):
    rows, width = second.shape
    return pl.pallas_call(
        functools.partial(piece_kernel, begin, column),
        in_specs=[SMEM] * 2 + [VMEM] * 4,
        out_specs=[VMEM] * 2,
        out_shape=[jax.ShapeDtypeStruct(second.shape, jnp.float32)] * 2,
        compiler_params=params(),
        cost_estimate=cost(2 * rows * rows * width, 2 * rows * rows + 22 * rows * width),
        name="piece_part",
    )(mask, coeffs, band, second, sums, mid)


def last_kernel(begin, column, mask_ref, coeffs_ref, band_ref, second_ref, sums_ref, mid_ref, piece_next_ref,
                piece_density_ref, *rest):
    next_ref, density_ref, held_next, held_density, sems = rest[-5:]
    rows, width = second_ref.shape
    block = rows // mask_ref.shape[0]
    step = rows // CHUNKS
    inside = slice(column, column + width)
    everything = pl.ds(0, rows)
    copies = start_writes(
        [(piece_next_ref, next_ref, everything, begin), (piece_density_ref, density_ref, everything, begin)], sems, 0)
    for c in range(CHUNKS):
        total = jnp.dot(
            band_ref[c * step:(c + 1) * step, side_columns(rows, 1, False)], second_ref[...],
            preferred_element_type=jnp.float32)
        for i in range(step // block):
            at = slice(c * step + i * block, c * step + (i + 1) * block)
            keep = kept(mask_ref, c * (step // block) + i, (begin + column) // block, block, width)
            value = jnp.where(keep, 2.0 * total[i * block:(i + 1) * block] + sums_ref[at, inside], 0.0)
            held_next[at, :] = value
            held_density[at, :] = coeffs_ref[0] * mid_ref[at, inside] + coeffs_ref[1] * value
        done = pl.ds(c * step, step)
        copies += start_writes(
            [(held_next, next_ref, done, begin + column), (held_density, density_ref, done, begin + column)],
            sems, len(copies))
    for copy in copies:
        copy.wait()


def last_part(begin, column, mask, coeffs, band, second, sums, mid, piece, outs):
    rows, width = second.shape
    return pl.pallas_call(
        functools.partial(last_kernel, begin, column),
        in_specs=[SMEM] * 2 + [VMEM] * 6 + [HBM] * 2,
        out_specs=[HBM] * 2,
        out_shape=[jax.ShapeDtypeStruct(out.shape, jnp.float32) for out in outs],
        scratch_shapes=[pltpu.VMEM((rows, width), jnp.float32)] * 2 + [pltpu.SemaphoreType.DMA((2 + 2 * CHUNKS,))],
        input_output_aliases={8: 0, 9: 1},
        compiler_params=params(),
        cost_estimate=cost(2 * rows * rows * width, 2 * rows * rows + 22 * rows * width),
        name="last_part",
    )(mask, coeffs, band, second, sums, mid, *piece, *outs)


def local(h_strips, h_slots, t_prev, t_now, t_mask, coeffs):
    width = t_now.shape[1] // 2
    low = t_now[:, :width].astype(jnp.bfloat16)
    low, t_now, t_prev, h_strips = lax.optimization_barrier((low, t_now, t_prev, h_strips))
    (high,) = rounded(t_now, [(width, width)])
    band = banded(h_slots, h_strips)
    low_sides, high_sides = both_sides(low), both_sides(high)
    mid_low, low_again = mid_part((0, width), [(0, width)], t_mask, band, low, *low_sides, t_prev, [])
    low_sides = both_sides(low_again)
    pieces = [(column, width // 2) for column in (0, width // 2)]
    mid_high, high_again, *cuts = mid_part(
        (width, width), [(0, width)] + pieces, t_mask, band, high, *high_sides, t_prev, [mid_low])
    first = from_side(high_again, 0, False)
    seconds = [from_side(cut, 1, False) for cut in cuts]
    t_mid, *outs, token = next_part(t_mask, coeffs, band, low_again, *low_sides, t_now, [mid_low, mid_high])
    sums = begun_part((width, width), band, high_again, first, t_now, [token])
    piece = piece_part(width, 0, t_mask, coeffs, band, seconds[0], sums, mid_high)
    outs = last_part(width, width // 2, t_mask, coeffs, band, seconds[1], sums, mid_high, piece, outs)
    return (t_mid, outs[0], outs[1])


def solution(mesh):
    panel = P(("grp", "row"), ("col", "rep"))
    return jax.shard_map(
        local,
        mesh=mesh,
        in_specs=(P(("grp", "row"), None, None), P(("grp", "row"), None), panel, panel, panel, P()),
        out_specs=(panel, panel, panel),
        check_vma=False,
    )
```

```python
import functools

import jax
import jax.numpy as jnp
from jax import lax
from jax.experimental import pallas as pl
from jax.experimental.pallas import tpu as pltpu
from jax.sharding import PartitionSpec as P

LANES = 128
CHUNKS = 4
MIB = 1024 * 1024

SMEM = pl.BlockSpec(memory_space=pltpu.SMEM)
VMEM = pl.BlockSpec(memory_space=pltpu.VMEM)
ANY = pl.BlockSpec(memory_space=pl.ANY)
HBM = pl.BlockSpec(memory_space=pltpu.HBM)


def from_side(block, order, mixed):
    rows, reps = lax.axis_size("row"), lax.axis_size("rep")
    route = []
    for row in range(rows):
        for rep in range(reps):
            turn = 1 if order == (mixed and rep % 2) else -1
            source = (row - turn) % rows
            route.append((source * reps + rep, row * reps + rep))
    return lax.ppermute(block, ("row", "rep"), route)


def both_sides(block):
    return tuple(from_side(block, order, True) for order in (0, 1))


def side_columns(depth, order, mixed):
    if not mixed:
        return pl.ds(2 * depth * order, depth)
    odd = lax.axis_index("rep") % 2
    return pl.ds(pl.multiple_of(jnp.where(odd == order, 0, 2 * depth), LANES), depth)


def params(limit=32 * MIB):
    return pltpu.CompilerParams(vmem_limit_bytes=limit)


def cost(flops, moved):
    return pl.CostEstimate(flops=flops, transcendentals=0, bytes_accessed=moved)


def round_kernel(starts, now_ref, *out_refs):
    for start, out_ref in zip(starts, out_refs):
        out_ref[...] = now_ref[:, start:start + out_ref.shape[1]].astype(jnp.bfloat16)


def rounded(now, spans):
    rows = now.shape[0]
    size = rows * sum(width for _, width in spans)
    return list(pl.pallas_call(
        functools.partial(round_kernel, [start for start, _ in spans]),
        in_specs=[VMEM],
        out_specs=[VMEM] * len(spans),
        out_shape=[jax.ShapeDtypeStruct((rows, width), jnp.bfloat16) for _, width in spans],
        compiler_params=params(),
        cost_estimate=cost(size, 6 * size),
        name="round_part",
    )(now))


def band_kernel(slots_ref, strips_ref, out_ref):
    block_rows, block, slot_lanes = strips_ref.shape
    out_ref[...] = jnp.zeros_like(out_ref)
    half = lax.broadcasted_iota(jnp.int32, (block, LANES), 1) // block

    @pl.loop(0, block_rows)
    def _(row):
        at = pl.ds(pl.multiple_of(row * block, block), block)
        for pair in range(slot_lanes // LANES):
            straight = strips_ref[row, :, pair * LANES:(pair + 1) * LANES].astype(jnp.float32)
            swapped = jnp.concatenate([straight[:, block:], straight[:, :block]], axis=1)
            for side in range(2):
                target = slots_ref[row, 2 * pair + side]
                odd = target % 2
                value = jnp.where(odd == side, straight, swapped)
                value = jnp.where(half == odd, value, 0.0).astype(jnp.bfloat16)
                lanes = pl.ds(pl.multiple_of((target // 2) * LANES, LANES), LANES)
                out_ref[at, lanes] += value


def banded(h_slots, h_strips):
    block_rows, block, slot_lanes = h_strips.shape
    rows, columns = block_rows * block, 3 * block_rows * block
    return pl.pallas_call(
        band_kernel,
        in_specs=[SMEM, VMEM],
        out_specs=VMEM,
        out_shape=jax.ShapeDtypeStruct((rows, columns), jnp.bfloat16),
        compiler_params=params(),
        cost_estimate=cost(8 * rows * columns, 2 * rows * (columns + slot_lanes)),
        name="band",
    )(h_slots, h_strips)


def product(band_ref, here_ref, first_ref, second_ref=None, mixed=True):
    depth = here_ref.shape[0]
    total = jnp.dot(band_ref[:, depth:2 * depth], here_ref[...], preferred_element_type=jnp.float32)
    total += jnp.dot(band_ref[:, side_columns(depth, 0, mixed)], first_ref[...], preferred_element_type=jnp.float32)
    if second_ref is not None:
        total += jnp.dot(band_ref[:, side_columns(depth, 1, mixed)], second_ref[...], preferred_element_type=jnp.float32)
    return total


def kept(mask_ref, block_row, first, block, width):
    column = lax.broadcasted_iota(jnp.int32, (block, width), 1) // block
    row = jnp.zeros((block, width), jnp.int32)
    for c in range(width // block):
        row = jnp.where(column == c, mask_ref[block_row, first + c], row)
    return row != 0


def masked(start, mask_ref, term):
    rows, width = term.shape
    block = rows // mask_ref.shape[0]
    for i in range(rows // block):
        at = slice(i * block, (i + 1) * block)
        yield at, jnp.where(kept(mask_ref, i, start // block, block, width), term[at], 0.0)


def start_writes(jobs, sems, first):
    copies = []
    for held, out_ref, at, column in jobs:
        copies.append(pltpu.make_async_copy(
            held.at[at, :], out_ref.at[at, pl.ds(column, held.shape[1])], sems.at[first + len(copies)]))
        copies[-1].start()
    return copies


def mid_kernel(start, pieces, mask_ref, band_ref, here_ref, second_ref, first_ref, prev_ref, *rest):
    mid_ref, round_refs = rest[-len(pieces) - 1], rest[-len(pieces):]
    total = product(band_ref, here_ref, first_ref, second_ref)
    term = 2.0 * total - prev_ref[:, start:start + here_ref.shape[1]]
    for at, value in masked(start, mask_ref, term):
        mid_ref[at, :] = value
        low = value.astype(jnp.bfloat16)
        for (column, size), round_ref in zip(pieces, round_refs):
            round_ref[at, :] = low[:, column:column + size]


def mid_part(span, pieces, mask, band, here, first, second, prev, after):
    rows, width = here.shape
    return pl.pallas_call(
        functools.partial(mid_kernel, span[0], pieces),
        in_specs=[SMEM] + [VMEM] * 5 + [ANY] * len(after),
        out_specs=[VMEM] * (1 + len(pieces)),
        out_shape=[jax.ShapeDtypeStruct(here.shape, jnp.float32)]
        + [jax.ShapeDtypeStruct((rows, size), jnp.bfloat16) for _, size in pieces],
        compiler_params=params(),
        cost_estimate=cost(6 * rows * rows * width, 6 * rows * rows + 16 * rows * width),
        name="mid_part",
    )(mask, band, here, second, first, prev, *after)


def next_kernel(mask_ref, coeffs_ref, band_ref, here_ref, second_ref, first_ref, now_ref, mid_ref, other_mid_ref,
                t_mid_ref, next_ref, density_ref, token_ref, held_next, held_density, sems):
    rows, width = here_ref.shape
    block = rows // mask_ref.shape[0]
    everything = pl.ds(0, rows)
    token_ref[...] = jnp.zeros_like(token_ref)
    copies = start_writes(
        [(mid_ref, t_mid_ref, everything, 0), (other_mid_ref, t_mid_ref, everything, width)], sems, 0)
    term = 2.0 * product(band_ref, here_ref, first_ref, second_ref) - now_ref[:, :width]
    for at, value in masked(0, mask_ref, term):
        held_next[at, :] = value
        held_density[at, :] = coeffs_ref[0] * mid_ref[at, :] + coeffs_ref[1] * value
    copies += start_writes(
        [(held_next, next_ref, everything, 0), (held_density, density_ref, everything, 0)], sems, len(copies))
    for copy in copies:
        copy.wait()


def next_part(mask, coeffs, band, here, first, second, now, mids):
    rows, width = here.shape
    return pl.pallas_call(
        next_kernel,
        in_specs=[SMEM] * 2 + [VMEM] * 7,
        out_specs=[HBM] * 3 + [VMEM],
        out_shape=[jax.ShapeDtypeStruct(now.shape, jnp.float32)] * 3 + [jax.ShapeDtypeStruct((8, LANES), jnp.float32)],
        scratch_shapes=[pltpu.VMEM(here.shape, jnp.float32)] * 2 + [pltpu.SemaphoreType.DMA((4,))],
        compiler_params=params(),
        cost_estimate=cost(6 * rows * rows * width, 6 * rows * rows + 30 * rows * width),
        name="next_part",
    )(mask, coeffs, band, here, second, first, now, *mids)


def begun_kernel(start, band_ref, here_ref, first_ref, now_ref, *rest):
    sums_ref = rest[-1]
    sums_ref[...] = 2.0 * product(band_ref, here_ref, first_ref, mixed=False) - now_ref[:, start:start + here_ref.shape[1]]


def begun_part(span, band, here, first, now, after):
    rows, width = here.shape
    return pl.pallas_call(
        functools.partial(begun_kernel, span[0]),
        in_specs=[VMEM] * 4 + [ANY] * len(after),
        out_specs=VMEM,
        out_shape=jax.ShapeDtypeStruct(here.shape, jnp.float32),
        compiler_params=params(),
        cost_estimate=cost(4 * rows * rows * width, 4 * rows * rows + 12 * rows * width),
        name="begun_part",
    )(band, here, first, now, *after)


def last_kernel(begin, column, mask_ref, coeffs_ref, band_ref, second_ref, sums_ref, mid_ref, *rest):
    next_ref, density_ref, held_next, held_density, sems = rest[-5:]
    rows, width = second_ref.shape
    block = rows // mask_ref.shape[0]
    step = rows // CHUNKS
    inside = slice(column, column + width)
    copies = []
    for c in range(CHUNKS):
        total = jnp.dot(
            band_ref[c * step:(c + 1) * step, side_columns(rows, 1, False)], second_ref[...],
            preferred_element_type=jnp.float32)
        for i in range(step // block):
            at = slice(c * step + i * block, c * step + (i + 1) * block)
            keep = kept(mask_ref, c * (step // block) + i, (begin + column) // block, block, width)
            value = jnp.where(keep, 2.0 * total[i * block:(i + 1) * block] + sums_ref[at, inside], 0.0)
            held_next[at, :] = value
            held_density[at, :] = coeffs_ref[0] * mid_ref[at, inside] + coeffs_ref[1] * value
        done = pl.ds(c * step, step)
        copies += start_writes(
            [(held_next, next_ref, done, begin + column), (held_density, density_ref, done, begin + column)],
            sems, len(copies))
    for copy in copies:
        copy.wait()


def last_part(begin, column, mask, coeffs, band, second, sums, mid, outs):
    rows, width = second.shape
    return pl.pallas_call(
        functools.partial(last_kernel, begin, column),
        in_specs=[SMEM] * 2 + [VMEM] * 4 + [HBM] * 2,
        out_specs=[HBM] * 2,
        out_shape=[jax.ShapeDtypeStruct(out.shape, jnp.float32) for out in outs],
        scratch_shapes=[pltpu.VMEM((rows, width), jnp.float32)] * 2 + [pltpu.SemaphoreType.DMA((2 * CHUNKS,))],
        input_output_aliases={6: 0, 7: 1},
        compiler_params=params(),
        cost_estimate=cost(2 * rows * rows * width, 2 * rows * rows + 22 * rows * width),
        name="last_part",
    )(mask, coeffs, band, second, sums, mid, *outs)


def local(h_strips, h_slots, t_prev, t_now, t_mask, coeffs):
    width = t_now.shape[1] // 2
    low = t_now[:, :width].astype(jnp.bfloat16)
    low, t_now, t_prev, h_strips = lax.optimization_barrier((low, t_now, t_prev, h_strips))
    (high,) = rounded(t_now, [(width, width)])
    band = banded(h_slots, h_strips)
    low_sides, high_sides = both_sides(low), both_sides(high)
    mid_low, low_again = mid_part((0, width), [(0, width)], t_mask, band, low, *low_sides, t_prev, [])
    low_sides = both_sides(low_again)
    pieces = [(column, width // 2) for column in (0, width // 2)]
    mid_high, high_again, *cuts = mid_part(
        (width, width), [(0, width)] + pieces, t_mask, band, high, *high_sides, t_prev, [mid_low])
    first = from_side(high_again, 0, False)
    seconds = [from_side(cut, 1, False) for cut in cuts]
    t_mid, *outs, token = next_part(t_mask, coeffs, band, low_again, *low_sides, t_now, [mid_low, mid_high])
    sums = begun_part((width, width), band, high_again, first, t_now, [token])
    for (column, _), second in zip(pieces, seconds):
        outs = last_part(width, column, t_mask, coeffs, band, second, sums, mid_high, outs)
    return (t_mid, outs[0], outs[1])


def solution(mesh):
    panel = P(("grp", "row"), ("col", "rep"))
    return jax.shard_map(
        local,
        mesh=mesh,
        in_specs=(P(("grp", "row"), None, None), P(("grp", "row"), None), panel, panel, panel, P()),
        out_specs=(panel, panel, panel),
        check_vma=False,
    )
```

```python
import functools

import jax
import jax.numpy as jnp
from jax import lax
from jax.experimental import pallas as pl
from jax.experimental.pallas import tpu as pltpu
from jax.sharding import PartitionSpec as P

LANES = 128
CHUNKS = 2
MIB = 1024 * 1024

SMEM = pl.BlockSpec(memory_space=pltpu.SMEM)
VMEM = pl.BlockSpec(memory_space=pltpu.VMEM)
ANY = pl.BlockSpec(memory_space=pl.ANY)
HBM = pl.BlockSpec(memory_space=pltpu.HBM)


def from_side(block, order, mixed):
    rows, reps = lax.axis_size("row"), lax.axis_size("rep")
    route = []
    for row in range(rows):
        for rep in range(reps):
            turn = 1 if order == (mixed and rep % 2) else -1
            source = (row - turn) % rows
            route.append((source * reps + rep, row * reps + rep))
    return lax.ppermute(block, ("row", "rep"), route)


def both_sides(block):
    return tuple(from_side(block, order, True) for order in (0, 1))


def side_columns(depth, order, mixed):
    if not mixed:
        return pl.ds(2 * depth * order, depth)
    odd = lax.axis_index("rep") % 2
    return pl.ds(pl.multiple_of(jnp.where(odd == order, 0, 2 * depth), LANES), depth)


def params(limit=32 * MIB):
    return pltpu.CompilerParams(vmem_limit_bytes=limit)


def cost(flops, moved):
    return pl.CostEstimate(flops=flops, transcendentals=0, bytes_accessed=moved)


def round_kernel(starts, now_ref, *out_refs):
    for start, out_ref in zip(starts, out_refs):
        out_ref[...] = now_ref[:, start:start + out_ref.shape[1]].astype(jnp.bfloat16)


def rounded(now, spans):
    rows = now.shape[0]
    size = rows * sum(width for _, width in spans)
    return list(pl.pallas_call(
        functools.partial(round_kernel, [start for start, _ in spans]),
        in_specs=[VMEM],
        out_specs=[VMEM] * len(spans),
        out_shape=[jax.ShapeDtypeStruct((rows, width), jnp.bfloat16) for _, width in spans],
        compiler_params=params(),
        cost_estimate=cost(size, 6 * size),
        name="round_part",
    )(now))


def band_kernel(slots_ref, strips_ref, out_ref):
    block_rows, block, slot_lanes = strips_ref.shape
    out_ref[...] = jnp.zeros_like(out_ref)
    half = lax.broadcasted_iota(jnp.int32, (block, LANES), 1) // block

    @pl.loop(0, block_rows)
    def _(row):
        at = pl.ds(pl.multiple_of(row * block, block), block)
        for pair in range(slot_lanes // LANES):
            straight = strips_ref[row, :, pair * LANES:(pair + 1) * LANES].astype(jnp.float32)
            swapped = jnp.concatenate([straight[:, block:], straight[:, :block]], axis=1)
            for side in range(2):
                target = slots_ref[row, 2 * pair + side]
                odd = target % 2
                value = jnp.where(odd == side, straight, swapped)
                value = jnp.where(half == odd, value, 0.0).astype(jnp.bfloat16)
                lanes = pl.ds(pl.multiple_of((target // 2) * LANES, LANES), LANES)
                out_ref[at, lanes] += value


def banded(h_slots, h_strips):
    block_rows, block, slot_lanes = h_strips.shape
    rows, columns = block_rows * block, 3 * block_rows * block
    return pl.pallas_call(
        band_kernel,
        in_specs=[SMEM, VMEM],
        out_specs=VMEM,
        out_shape=jax.ShapeDtypeStruct((rows, columns), jnp.bfloat16),
        compiler_params=params(),
        cost_estimate=cost(8 * rows * columns, 2 * rows * (columns + slot_lanes)),
        name="band",
    )(h_slots, h_strips)


def product(band_ref, here_ref, first_ref, second_ref=None, mixed=True):
    depth = here_ref.shape[0]
    total = jnp.dot(band_ref[:, depth:2 * depth], here_ref[...], preferred_element_type=jnp.float32)
    total += jnp.dot(band_ref[:, side_columns(depth, 0, mixed)], first_ref[...], preferred_element_type=jnp.float32)
    if second_ref is not None:
        total += jnp.dot(band_ref[:, side_columns(depth, 1, mixed)], second_ref[...], preferred_element_type=jnp.float32)
    return total


def kept(mask_ref, block_row, first, block, width):
    column = lax.broadcasted_iota(jnp.int32, (block, width), 1) // block
    row = jnp.zeros((block, width), jnp.int32)
    for c in range(width // block):
        row = jnp.where(column == c, mask_ref[block_row, first + c], row)
    return row != 0


def masked(start, mask_ref, term):
    rows, width = term.shape
    block = rows // mask_ref.shape[0]
    for i in range(rows // block):
        at = slice(i * block, (i + 1) * block)
        yield at, jnp.where(kept(mask_ref, i, start // block, block, width), term[at], 0.0)


def start_writes(jobs, sems, first):
    copies = []
    for held, out_ref, at, column in jobs:
        copies.append(pltpu.make_async_copy(
            held.at[at, :], out_ref.at[at, pl.ds(column, held.shape[1])], sems.at[first + len(copies)]))
        copies[-1].start()
    return copies


def mid_kernel(start, pieces, mask_ref, band_ref, here_ref, second_ref, first_ref, prev_ref, *rest):
    mid_ref, round_refs = rest[-len(pieces) - 1], rest[-len(pieces):]
    total = product(band_ref, here_ref, first_ref, second_ref)
    term = 2.0 * total - prev_ref[:, start:start + here_ref.shape[1]]
    for at, value in masked(start, mask_ref, term):
        mid_ref[at, :] = value
        low = value.astype(jnp.bfloat16)
        for (column, size), round_ref in zip(pieces, round_refs):
            round_ref[at, :] = low[:, column:column + size]


def mid_part(span, pieces, mask, band, here, first, second, prev, after):
    rows, width = here.shape
    return pl.pallas_call(
        functools.partial(mid_kernel, span[0], pieces),
        in_specs=[SMEM] + [VMEM] * 5 + [ANY] * len(after),
        out_specs=[VMEM] * (1 + len(pieces)),
        out_shape=[jax.ShapeDtypeStruct(here.shape, jnp.float32)]
        + [jax.ShapeDtypeStruct((rows, size), jnp.bfloat16) for _, size in pieces],
        compiler_params=params(),
        cost_estimate=cost(6 * rows * rows * width, 6 * rows * rows + 16 * rows * width),
        name="mid_part",
    )(mask, band, here, second, first, prev, *after)


def next_kernel(mask_ref, coeffs_ref, band_ref, here_ref, second_ref, first_ref, now_ref, mid_ref, other_mid_ref,
                t_mid_ref, next_ref, density_ref, token_ref, held_next, held_density, sems):
    rows, width = here_ref.shape
    block = rows // mask_ref.shape[0]
    everything = pl.ds(0, rows)
    token_ref[...] = jnp.zeros_like(token_ref)
    copies = start_writes(
        [(mid_ref, t_mid_ref, everything, 0), (other_mid_ref, t_mid_ref, everything, width)], sems, 0)
    term = 2.0 * product(band_ref, here_ref, first_ref, second_ref) - now_ref[:, :width]
    for at, value in masked(0, mask_ref, term):
        held_next[at, :] = value
        held_density[at, :] = coeffs_ref[0] * mid_ref[at, :] + coeffs_ref[1] * value
    copies += start_writes(
        [(held_next, next_ref, everything, 0), (held_density, density_ref, everything, 0)], sems, len(copies))
    for copy in copies:
        copy.wait()


def next_part(mask, coeffs, band, here, first, second, now, mids):
    rows, width = here.shape
    return pl.pallas_call(
        next_kernel,
        in_specs=[SMEM] * 2 + [VMEM] * 7,
        out_specs=[HBM] * 3 + [VMEM],
        out_shape=[jax.ShapeDtypeStruct(now.shape, jnp.float32)] * 3 + [jax.ShapeDtypeStruct((8, LANES), jnp.float32)],
        scratch_shapes=[pltpu.VMEM(here.shape, jnp.float32)] * 2 + [pltpu.SemaphoreType.DMA((4,))],
        compiler_params=params(),
        cost_estimate=cost(6 * rows * rows * width, 6 * rows * rows + 30 * rows * width),
        name="next_part",
    )(mask, coeffs, band, here, second, first, now, *mids)


def begun_kernel(start, band_ref, here_ref, first_ref, now_ref, *rest):
    sums_ref = rest[-1]
    sums_ref[...] = 2.0 * product(band_ref, here_ref, first_ref, mixed=False) - now_ref[:, start:start + here_ref.shape[1]]


def begun_part(span, band, here, first, now, after):
    rows, width = here.shape
    return pl.pallas_call(
        functools.partial(begun_kernel, span[0]),
        in_specs=[VMEM] * 4 + [ANY] * len(after),
        out_specs=VMEM,
        out_shape=jax.ShapeDtypeStruct(here.shape, jnp.float32),
        compiler_params=params(),
        cost_estimate=cost(4 * rows * rows * width, 4 * rows * rows + 12 * rows * width),
        name="begun_part",
    )(band, here, first, now, *after)


def last_kernel(begin, column, mask_ref, coeffs_ref, band_ref, second_ref, sums_ref, mid_ref, *rest):
    next_ref, density_ref, held_next, held_density, sems = rest[-5:]
    rows, width = second_ref.shape
    block = rows // mask_ref.shape[0]
    step = rows // CHUNKS
    inside = slice(column, column + width)
    copies = []
    for c in range(CHUNKS):
        total = jnp.dot(
            band_ref[c * step:(c + 1) * step, side_columns(rows, 1, False)], second_ref[...],
            preferred_element_type=jnp.float32)
        for i in range(step // block):
            at = slice(c * step + i * block, c * step + (i + 1) * block)
            keep = kept(mask_ref, c * (step // block) + i, (begin + column) // block, block, width)
            value = jnp.where(keep, 2.0 * total[i * block:(i + 1) * block] + sums_ref[at, inside], 0.0)
            held_next[at, :] = value
            held_density[at, :] = coeffs_ref[0] * mid_ref[at, inside] + coeffs_ref[1] * value
        done = pl.ds(c * step, step)
        copies += start_writes(
            [(held_next, next_ref, done, begin + column), (held_density, density_ref, done, begin + column)],
            sems, len(copies))
    for copy in copies:
        copy.wait()


def last_part(begin, column, mask, coeffs, band, second, sums, mid, outs):
    rows, width = second.shape
    return pl.pallas_call(
        functools.partial(last_kernel, begin, column),
        in_specs=[SMEM] * 2 + [VMEM] * 4 + [HBM] * 2,
        out_specs=[HBM] * 2,
        out_shape=[jax.ShapeDtypeStruct(out.shape, jnp.float32) for out in outs],
        scratch_shapes=[pltpu.VMEM((rows, width), jnp.float32)] * 2 + [pltpu.SemaphoreType.DMA((2 * CHUNKS,))],
        input_output_aliases={6: 0, 7: 1},
        compiler_params=params(),
        cost_estimate=cost(2 * rows * rows * width, 2 * rows * rows + 22 * rows * width),
        name="last_part",
    )(mask, coeffs, band, second, sums, mid, *outs)


def local(h_strips, h_slots, t_prev, t_now, t_mask, coeffs):
    width = t_now.shape[1] // 2
    low = t_now[:, :width].astype(jnp.bfloat16)
    low, t_now, t_prev, h_strips = lax.optimization_barrier((low, t_now, t_prev, h_strips))
    high = t_now[:, width:].astype(jnp.bfloat16)
    band = banded(h_slots, h_strips)
    low_sides, high_sides = both_sides(low), both_sides(high)
    mid_low, low_again = mid_part((0, width), [(0, width)], t_mask, band, low, *low_sides, t_prev, [])
    low_sides = both_sides(low_again)
    pieces = [(column, width // 2) for column in (0, width // 2)]
    mid_high, high_again, *cuts = mid_part(
        (width, width), [(0, width)] + pieces, t_mask, band, high, *high_sides, t_prev, [mid_low])
    first = from_side(high_again, 0, False)
    seconds = [from_side(cut, 1, False) for cut in cuts]
    t_mid, *outs, token = next_part(t_mask, coeffs, band, low_again, *low_sides, t_now, [mid_low, mid_high])
    sums = begun_part((width, width), band, high_again, first, t_now, [token])
    for (column, _), second in zip(pieces, seconds):
        outs = last_part(width, column, t_mask, coeffs, band, second, sums, mid_high, outs)
    return (t_mid, outs[0], outs[1])


def solution(mesh):
    panel = P(("grp", "row"), ("col", "rep"))
    return jax.shard_map(
        local,
        mesh=mesh,
        in_specs=(P(("grp", "row"), None, None), P(("grp", "row"), None), panel, panel, panel, P()),
        out_specs=(panel, panel, panel),
        check_vma=False,
    )
```

```python
import functools

import jax
import jax.numpy as jnp
from jax import lax
from jax.experimental import pallas as pl
from jax.experimental.pallas import tpu as pltpu
from jax.sharding import PartitionSpec as P

LANES = 128
CHUNKS = 1
MIB = 1024 * 1024

SMEM = pl.BlockSpec(memory_space=pltpu.SMEM)
VMEM = pl.BlockSpec(memory_space=pltpu.VMEM)
ANY = pl.BlockSpec(memory_space=pl.ANY)
HBM = pl.BlockSpec(memory_space=pltpu.HBM)


def from_side(block, order, mixed):
    rows, reps = lax.axis_size("row"), lax.axis_size("rep")
    route = []
    for row in range(rows):
        for rep in range(reps):
            turn = 1 if order == (mixed and rep % 2) else -1
            source = (row - turn) % rows
            route.append((source * reps + rep, row * reps + rep))
    return lax.ppermute(block, ("row", "rep"), route)


def both_sides(block):
    return tuple(from_side(block, order, True) for order in (0, 1))


def side_columns(depth, order, mixed):
    if not mixed:
        return pl.ds(2 * depth * order, depth)
    odd = lax.axis_index("rep") % 2
    return pl.ds(pl.multiple_of(jnp.where(odd == order, 0, 2 * depth), LANES), depth)


def params(limit=32 * MIB):
    return pltpu.CompilerParams(vmem_limit_bytes=limit)


def cost(flops, moved):
    return pl.CostEstimate(flops=flops, transcendentals=0, bytes_accessed=moved)


def round_kernel(starts, now_ref, *out_refs):
    for start, out_ref in zip(starts, out_refs):
        out_ref[...] = now_ref[:, start:start + out_ref.shape[1]].astype(jnp.bfloat16)


def rounded(now, spans):
    rows = now.shape[0]
    size = rows * sum(width for _, width in spans)
    return list(pl.pallas_call(
        functools.partial(round_kernel, [start for start, _ in spans]),
        in_specs=[VMEM],
        out_specs=[VMEM] * len(spans),
        out_shape=[jax.ShapeDtypeStruct((rows, width), jnp.bfloat16) for _, width in spans],
        compiler_params=params(),
        cost_estimate=cost(size, 6 * size),
        name="round_part",
    )(now))


def band_kernel(slots_ref, strips_ref, out_ref):
    block_rows, block, slot_lanes = strips_ref.shape
    out_ref[...] = jnp.zeros_like(out_ref)
    half = lax.broadcasted_iota(jnp.int32, (block, LANES), 1) // block

    @pl.loop(0, block_rows)
    def _(row):
        at = pl.ds(pl.multiple_of(row * block, block), block)
        for pair in range(slot_lanes // LANES):
            straight = strips_ref[row, :, pair * LANES:(pair + 1) * LANES].astype(jnp.float32)
            swapped = jnp.concatenate([straight[:, block:], straight[:, :block]], axis=1)
            for side in range(2):
                target = slots_ref[row, 2 * pair + side]
                odd = target % 2
                value = jnp.where(odd == side, straight, swapped)
                value = jnp.where(half == odd, value, 0.0).astype(jnp.bfloat16)
                lanes = pl.ds(pl.multiple_of((target // 2) * LANES, LANES), LANES)
                out_ref[at, lanes] += value


def banded(h_slots, h_strips):
    block_rows, block, slot_lanes = h_strips.shape
    rows, columns = block_rows * block, 3 * block_rows * block
    return pl.pallas_call(
        band_kernel,
        in_specs=[SMEM, VMEM],
        out_specs=VMEM,
        out_shape=jax.ShapeDtypeStruct((rows, columns), jnp.bfloat16),
        compiler_params=params(),
        cost_estimate=cost(8 * rows * columns, 2 * rows * (columns + slot_lanes)),
        name="band",
    )(h_slots, h_strips)


def product(band_ref, here_ref, first_ref, second_ref=None, mixed=True):
    depth = here_ref.shape[0]
    total = jnp.dot(band_ref[:, depth:2 * depth], here_ref[...], preferred_element_type=jnp.float32)
    total += jnp.dot(band_ref[:, side_columns(depth, 0, mixed)], first_ref[...], preferred_element_type=jnp.float32)
    if second_ref is not None:
        total += jnp.dot(band_ref[:, side_columns(depth, 1, mixed)], second_ref[...], preferred_element_type=jnp.float32)
    return total


def kept(mask_ref, block_row, first, block, width):
    column = lax.broadcasted_iota(jnp.int32, (block, width), 1) // block
    row = jnp.zeros((block, width), jnp.int32)
    for c in range(width // block):
        row = jnp.where(column == c, mask_ref[block_row, first + c], row)
    return row != 0


def masked(start, mask_ref, term):
    rows, width = term.shape
    block = rows // mask_ref.shape[0]
    for i in range(rows // block):
        at = slice(i * block, (i + 1) * block)
        yield at, jnp.where(kept(mask_ref, i, start // block, block, width), term[at], 0.0)


def start_writes(jobs, sems, first):
    copies = []
    for held, out_ref, at, column in jobs:
        copies.append(pltpu.make_async_copy(
            held.at[at, :], out_ref.at[at, pl.ds(column, held.shape[1])], sems.at[first + len(copies)]))
        copies[-1].start()
    return copies


def mid_kernel(start, pieces, mask_ref, band_ref, here_ref, second_ref, first_ref, prev_ref, *rest):
    mid_ref, round_refs = rest[-len(pieces) - 1], rest[-len(pieces):]
    total = product(band_ref, here_ref, first_ref, second_ref)
    term = 2.0 * total - prev_ref[:, start:start + here_ref.shape[1]]
    for at, value in masked(start, mask_ref, term):
        mid_ref[at, :] = value
        low = value.astype(jnp.bfloat16)
        for (column, size), round_ref in zip(pieces, round_refs):
            round_ref[at, :] = low[:, column:column + size]


def mid_part(span, pieces, mask, band, here, first, second, prev, after):
    rows, width = here.shape
    return pl.pallas_call(
        functools.partial(mid_kernel, span[0], pieces),
        in_specs=[SMEM] + [VMEM] * 5 + [ANY] * len(after),
        out_specs=[VMEM] * (1 + len(pieces)),
        out_shape=[jax.ShapeDtypeStruct(here.shape, jnp.float32)]
        + [jax.ShapeDtypeStruct((rows, size), jnp.bfloat16) for _, size in pieces],
        compiler_params=params(),
        cost_estimate=cost(6 * rows * rows * width, 6 * rows * rows + 16 * rows * width),
        name="mid_part",
    )(mask, band, here, second, first, prev, *after)


def next_kernel(mask_ref, coeffs_ref, band_ref, here_ref, second_ref, first_ref, now_ref, mid_ref, other_mid_ref,
                t_mid_ref, next_ref, density_ref, token_ref, held_next, held_density, sems):
    rows, width = here_ref.shape
    block = rows // mask_ref.shape[0]
    everything = pl.ds(0, rows)
    token_ref[...] = jnp.zeros_like(token_ref)
    copies = start_writes(
        [(mid_ref, t_mid_ref, everything, 0), (other_mid_ref, t_mid_ref, everything, width)], sems, 0)
    term = 2.0 * product(band_ref, here_ref, first_ref, second_ref) - now_ref[:, :width]
    for at, value in masked(0, mask_ref, term):
        held_next[at, :] = value
        held_density[at, :] = coeffs_ref[0] * mid_ref[at, :] + coeffs_ref[1] * value
    copies += start_writes(
        [(held_next, next_ref, everything, 0), (held_density, density_ref, everything, 0)], sems, len(copies))
    for copy in copies:
        copy.wait()


def next_part(mask, coeffs, band, here, first, second, now, mids):
    rows, width = here.shape
    return pl.pallas_call(
        next_kernel,
        in_specs=[SMEM] * 2 + [VMEM] * 7,
        out_specs=[HBM] * 3 + [VMEM],
        out_shape=[jax.ShapeDtypeStruct(now.shape, jnp.float32)] * 3 + [jax.ShapeDtypeStruct((8, LANES), jnp.float32)],
        scratch_shapes=[pltpu.VMEM(here.shape, jnp.float32)] * 2 + [pltpu.SemaphoreType.DMA((4,))],
        compiler_params=params(),
        cost_estimate=cost(6 * rows * rows * width, 6 * rows * rows + 30 * rows * width),
        name="next_part",
    )(mask, coeffs, band, here, second, first, now, *mids)


def begun_kernel(start, band_ref, here_ref, first_ref, now_ref, *rest):
    sums_ref = rest[-1]
    sums_ref[...] = 2.0 * product(band_ref, here_ref, first_ref, mixed=False) - now_ref[:, start:start + here_ref.shape[1]]


def begun_part(span, band, here, first, now, after):
    rows, width = here.shape
    return pl.pallas_call(
        functools.partial(begun_kernel, span[0]),
        in_specs=[VMEM] * 4 + [ANY] * len(after),
        out_specs=VMEM,
        out_shape=jax.ShapeDtypeStruct(here.shape, jnp.float32),
        compiler_params=params(),
        cost_estimate=cost(4 * rows * rows * width, 4 * rows * rows + 12 * rows * width),
        name="begun_part",
    )(band, here, first, now, *after)


def last_kernel(begin, column, mask_ref, coeffs_ref, band_ref, second_ref, sums_ref, mid_ref, *rest):
    next_ref, density_ref, held_next, held_density, sems = rest[-5:]
    rows, width = second_ref.shape
    block = rows // mask_ref.shape[0]
    step = rows // CHUNKS
    inside = slice(column, column + width)
    copies = []
    for c in range(CHUNKS):
        total = jnp.dot(
            band_ref[c * step:(c + 1) * step, side_columns(rows, 1, False)], second_ref[...],
            preferred_element_type=jnp.float32)
        for i in range(step // block):
            at = slice(c * step + i * block, c * step + (i + 1) * block)
            keep = kept(mask_ref, c * (step // block) + i, (begin + column) // block, block, width)
            value = jnp.where(keep, 2.0 * total[i * block:(i + 1) * block] + sums_ref[at, inside], 0.0)
            held_next[at, :] = value
            held_density[at, :] = coeffs_ref[0] * mid_ref[at, inside] + coeffs_ref[1] * value
        done = pl.ds(c * step, step)
        copies += start_writes(
            [(held_next, next_ref, done, begin + column), (held_density, density_ref, done, begin + column)],
            sems, len(copies))
    for copy in copies:
        copy.wait()


def last_part(begin, column, mask, coeffs, band, second, sums, mid, outs):
    rows, width = second.shape
    return pl.pallas_call(
        functools.partial(last_kernel, begin, column),
        in_specs=[SMEM] * 2 + [VMEM] * 4 + [HBM] * 2,
        out_specs=[HBM] * 2,
        out_shape=[jax.ShapeDtypeStruct(out.shape, jnp.float32) for out in outs],
        scratch_shapes=[pltpu.VMEM((rows, width), jnp.float32)] * 2 + [pltpu.SemaphoreType.DMA((2 * CHUNKS,))],
        input_output_aliases={6: 0, 7: 1},
        compiler_params=params(),
        cost_estimate=cost(2 * rows * rows * width, 2 * rows * rows + 22 * rows * width),
        name="last_part",
    )(mask, coeffs, band, second, sums, mid, *outs)


def local(h_strips, h_slots, t_prev, t_now, t_mask, coeffs):
    width = t_now.shape[1] // 2
    low = t_now[:, :width].astype(jnp.bfloat16)
    low, t_now, t_prev, h_strips = lax.optimization_barrier((low, t_now, t_prev, h_strips))
    (high,) = rounded(t_now, [(width, width)])
    band = banded(h_slots, h_strips)
    low_sides, high_sides = both_sides(low), both_sides(high)
    mid_low, low_again = mid_part((0, width), [(0, width)], t_mask, band, low, *low_sides, t_prev, [])
    low_sides = both_sides(low_again)
    pieces = [(column, width // 2) for column in (0, width // 2)]
    mid_high, high_again, *cuts = mid_part(
        (width, width), [(0, width)] + pieces, t_mask, band, high, *high_sides, t_prev, [mid_low])
    first = from_side(high_again, 0, False)
    seconds = [from_side(cut, 1, False) for cut in cuts]
    t_mid, *outs, token = next_part(t_mask, coeffs, band, low_again, *low_sides, t_now, [mid_low, mid_high])
    sums = begun_part((width, width), band, high_again, first, t_now, [token])
    for (column, _), second in zip(pieces, seconds):
        outs = last_part(width, column, t_mask, coeffs, band, second, sums, mid_high, outs)
    return (t_mid, outs[0], outs[1])


def solution(mesh):
    panel = P(("grp", "row"), ("col", "rep"))
    return jax.shard_map(
        local,
        mesh=mesh,
        in_specs=(P(("grp", "row"), None, None), P(("grp", "row"), None), panel, panel, panel, P()),
        out_specs=(panel, panel, panel),
        check_vma=False,
    )
```
